32 devices in a mesh: dp: 4 (over y, x), blk: 8 (over z, core).
Axes of the slice: x: 2, y: 2, z: 4, core: 2. Of those that a mesh axis runs over, the one named last changes fastest.
Arguments:
- crops_seven: bfloat16 [256, 7, 7, 2048], P(('dp', 'blk')), may hold values from -12 to 12
- crops_six: bfloat16 [192, 6, 6, 2048], P(('dp', 'blk')), may hold values from -12 to 12
- crops_five: bfloat16 [256, 5, 5, 2048], P(('dp', 'blk')), may hold values from -12 to 12
- conv_in: bfloat16 [2048, 512], replicated, may hold values from -0.125 to 0.125
- gain_in: float32 [512], replicated, may hold values from 0.5 to 1.5
- bias_in: float32 [512], replicated, may hold values from -1.75 to 1.75
- conv_mid: bfloat16 [3, 3, 512, 512], replicated, may hold values from -0.09375 to 0.09375
- gain_mid: float32 [512], replicated, may hold values from 0.5 to 1.5
- bias_mid: float32 [512], replicated, may hold values from -1.75 to 1.75
- conv_out: bfloat16 [512, 2048], replicated, may hold values from -0.25 to 0.25
- gain_out: float32 [2048], replicated, may hold values from 0.5 to 1.5
- bias_out: float32 [2048], replicated, may hold values from -1.75 to 1.75
- proj_hidden: bfloat16 [2048, 1024], replicated, may hold values from -0.125 to 0.125
- gain_proj: float32 [1024], replicated, may hold values from 0.5 to 1.5
- bias_proj: float32 [1024], replicated, may hold values from -1.75 to 1.75
- proj_embed: bfloat16 [1024, 128], replicated, may hold values from -0.1875 to 0.1875
- pair_index: int32 [1024, 2], P(('dp', 'blk')), may hold values from 0 to 21
Outputs:
- grad_seven: float32 [256, 7, 7, 2048], P(('dp', 'blk'))
- grad_six: float32 [192, 6, 6, 2048], P(('dp', 'blk'))
- grad_five: float32 [256, 5, 5, 2048], P(('dp', 'blk'))
- grad_conv_in: float32 [2048, 512], P('blk')
- grad_conv_mid: float32 [3, 3, 512, 512], P(None, None, 'blk')
- grad_conv_out: float32 [512, 2048], P('blk')
- grad_proj_hidden: float32 [2048, 1024], P('blk')
- grad_proj_embed: float32 [1024, 128], P('blk')
- grad_gain_in: float32 [512], replicated
- grad_bias_in: float32 [512], replicated
- grad_gain_mid: float32 [512], replicated
- grad_bias_mid: float32 [512], replicated
- grad_gain_out: float32 [2048], replicated
- grad_bias_out: float32 [2048], replicated
- grad_gain_proj: float32 [1024], replicated
- grad_bias_proj: float32 [1024], replicated
The draws below stay inside these ranges and needn't reach their ends.
Inputs may be any that keep to these rules, and one draw needn't show every extreme that they name: `pair_index`: row r names two crops of device r // 32, as indices into that device's crops in the order 7x7, 6x6, 5x5.
All inputs are finite; a program needn't handle non-finite values.
Results may differ from the reference program's by a relative error of at most 0.014.
Values sent between devices are 32-bit elements; how exact they have to be, the bound alone decides.
No kernel may reach another device: no remote copies, remote signals or barrier semaphores. Data moves between devices by JAX's collectives and lax.ppermute only.
A program may use at most 192 MiB of HBM per device.

```python
import jax
import jax.numpy as jnp
from jax import lax

CIN = 2048
MID = 512
PH = 1024
EMB = 128
C7 = 8
C6 = 6
C5 = 8
PAIRS_DEV = 32
SLOTS = 22
PIX_DEV = 808
CROPS7 = 256
CROPS6 = 192
CROPS5 = 256
CROPS = 704
PAIRS = 1024
N_DP = 4
N_BLK = 8


def shape_field(noise, jitter, chan_unit, per_device):
    count_all = noise.shape[0]
    device_count = count_all // per_device
    place = (jnp.arange(count_all) // per_device).astype(jnp.float32) / max(device_count - 1, 1)
    crop_scale = jnp.exp(jnp.log(3.0) * (place + jitter - 1.0))
    chan_scale = jnp.exp(jnp.log(0.5) + chan_unit * (jnp.log(2.0) - jnp.log(0.5)))
    values = noise * crop_scale[:, None, None, None] * chan_scale
    return jnp.clip(values, -12.0, 12.0)


def draw_crops_seven(key, part):
    key = jax.random.fold_in(key, 7)
    key_noise, key_crop, key_chan = jax.random.split(key, 3)
    jitter = jax.random.uniform(key_crop, (CROPS7,), jnp.float32)
    chan_unit = jax.random.uniform(key_chan, (CIN,), jnp.float32)
    noise = jax.random.normal(key_noise, (CROPS7, 7, 7, CIN), jnp.float32)
    return shape_field(noise, jitter, chan_unit, C7).astype(jnp.bfloat16)


def draw_crops_six(key, part):
    key = jax.random.fold_in(key, 6)
    key_noise, key_crop, key_chan = jax.random.split(key, 3)
    jitter = jax.random.uniform(key_crop, (CROPS6,), jnp.float32)
    chan_unit = jax.random.uniform(key_chan, (CIN,), jnp.float32)
    noise = jax.random.normal(key_noise, (CROPS6, 6, 6, CIN), jnp.float32)
    return shape_field(noise, jitter, chan_unit, C6).astype(jnp.bfloat16)


def draw_crops_five(key, part):
    key = jax.random.fold_in(key, 5)
    key_noise, key_crop, key_chan = jax.random.split(key, 3)
    jitter = jax.random.uniform(key_crop, (CROPS5,), jnp.float32)
    chan_unit = jax.random.uniform(key_chan, (CIN,), jnp.float32)
    noise = jax.random.normal(key_noise, (CROPS5, 5, 5, CIN), jnp.float32)
    return shape_field(noise, jitter, chan_unit, C5).astype(jnp.bfloat16)


def touch_ends(entries, stream_key, least, largest):
    extent = entries.shape
    spot = [jax.random.randint(jax.random.fold_in(stream_key, axis), (), 0, extent[axis]) for axis in range(len(extent))]
    entries = entries.at[tuple(spot)].set(least)
    longest = extent.index(max(extent))
    spot[longest] = (spot[longest] + 1) % extent[longest]
    return entries.at[tuple(spot)].set(largest)


def bell_draw(own_key, dims, scale, reach, kind=jnp.bfloat16):
    values = jax.random.normal(own_key, dims, jnp.float32) * scale
    return jnp.minimum(jnp.maximum(values, -reach), reach).astype(kind)


def setup_inputs(seed: int = 0) -> dict:
    splits = jax.random.split(jax.random.key(seed), 18)
    crops_seven = draw_crops_seven(jax.random.fold_in(splits[17], 71), 0)
    crops_six = draw_crops_six(jax.random.fold_in(splits[17], 71), 0)
    crops_five = draw_crops_five(jax.random.fold_in(splits[17], 71), 0)
    conv_in = bell_draw(splits[3], (CIN, MID), CIN ** -0.5, 0.125)
    gain_in = jnp.clip(1.0 + 0.1 * jax.random.normal(splits[4], (MID,), jnp.float32), 0.5, 1.5)
    bias_in = bell_draw(splits[5], (MID,), 0.3, 1.75, jnp.float32)
    conv_mid = bell_draw(splits[6], (3, 3, MID, MID), (9 * MID) ** -0.5, 0.09375)
    gain_mid = jnp.clip(1.0 + 0.1 * jax.random.normal(splits[7], (MID,), jnp.float32), 0.5, 1.5)
    bias_mid = bell_draw(splits[8], (MID,), 0.3, 1.75, jnp.float32)
    conv_out = bell_draw(splits[9], (MID, CIN), MID ** -0.5, 0.25)
    gain_out = jnp.clip(1.0 + 0.1 * jax.random.normal(splits[10], (CIN,), jnp.float32), 0.5, 1.5)
    bias_out = bell_draw(splits[11], (CIN,), 0.3, 1.75, jnp.float32)
    proj_hidden = bell_draw(splits[12], (CIN, PH), CIN ** -0.5, 0.125)
    gain_proj = jnp.clip(1.0 + 0.1 * jax.random.normal(splits[13], (PH,), jnp.float32), 0.5, 1.5)
    bias_proj = bell_draw(splits[14], (PH,), 0.3, 1.75, jnp.float32)
    proj_embed = bell_draw(splits[15], (PH, EMB), PH ** -0.5, 0.1875)
    pair_index = touch_ends(jax.random.randint(splits[16], (PAIRS, 2), 0, SLOTS), jax.random.fold_in(splits[16], 1), 0, SLOTS - 1).astype(jnp.int32)
    return {"crops_seven": crops_seven, "crops_six": crops_six, "crops_five": crops_five, "conv_in": conv_in, "gain_in": gain_in, "bias_in": bias_in, "conv_mid": conv_mid, "gain_mid": gain_mid, "bias_mid": bias_mid, "conv_out": conv_out, "gain_out": gain_out, "bias_out": bias_out, "proj_hidden": proj_hidden, "gain_proj": gain_proj, "bias_proj": bias_proj, "proj_embed": proj_embed, "pair_index": pair_index}


HIGHEST_PREC = lax.Precision.HIGHEST
NORM_EPS = 1e-05
UNIT_EPS = 1e-06

@jax.custom_vjp
def low(v):
    return lax.optimization_barrier(v.astype(jnp.bfloat16)).astype(jnp.float32)

@jax.custom_vjp
def low_back(v):
    return v

def low_keep(v):
    return (low(v), None)

def low_pass(kept, grad):
    return (grad,)

def back_keep(v):
    return (v, None)

def back_low(kept, grad):
    return (low(grad),)
low.defvjp(low_keep, low_pass)
low_back.defvjp(back_keep, back_low)

def split_rows(row_block, channels):
    pieces = []
    offset = 0
    for number, side_len in zip((C7, C6, C5), (7, 6, 5)):
        length = number * side_len * side_len
        pieces.append(row_block[offset:offset + length].reshape(number, side_len, side_len, channels))
        offset = offset + length
    return pieces

def pool_crops(row_block):
    crop_means = [lax.optimization_barrier(jnp.mean(crop_grid.reshape(crop_grid.shape[0], -1, crop_grid.shape[-1]), axis=1)) for crop_grid in split_rows(row_block, row_block.shape[-1])]
    return jnp.concatenate(crop_means, axis=0)

def batch_stats(activity, row_total):
    axes_all = tuple(range(activity.ndim - 1))
    mean_vec = lax.optimization_barrier(jnp.sum(activity, axis=axes_all)) / row_total
    var_vec = lax.optimization_barrier(jnp.sum(activity * activity, axis=axes_all)) / row_total - mean_vec * mean_vec
    return (mean_vec, lax.rsqrt(var_vec + NORM_EPS))

def conv_three(crop_field, kernel):
    return lax.conv_general_dilated(crop_field, kernel, (1, 1), 'SAME', dimension_numbers=('NHWC', 'HWIO', 'NHWC'), precision=HIGHEST_PREC)

def forward(pixel_rows, params, pair_global):
    conv_in, gain_in, bias_in, conv_mid, gain_mid, bias_mid, conv_out, gain_out, bias_out, proj_hidden, gain_proj, bias_proj, proj_embed = params
    pixel_total = float(PIX_DEV * N_DP * N_BLK)
    crop_total = float(CROPS)

    def first_block(inputs):
        return low_back(jnp.dot(inputs, conv_in, precision=HIGHEST_PREC))
    first_pre = lax.map(jax.checkpoint(first_block), pixel_rows)
    mean_one, rstd_one = batch_stats(first_pre, pixel_total)

    def second_block(activity):
        hidden = low(jax.nn.silu(gain_in * (activity - mean_one) * rstd_one + bias_in))
        conv_rows = [conv_three(crop_grid, conv_mid).reshape(-1, MID) for crop_grid in split_rows(hidden, MID)]
        return low_back(jnp.concatenate(conv_rows, axis=0))
    second = lax.map(jax.checkpoint(second_block), first_pre)
    mean_two, rstd_two = batch_stats(second, pixel_total)

    def third_block(activity):
        hidden = low(jax.nn.silu(gain_mid * (activity - mean_two) * rstd_two + bias_mid))
        return low_back(jnp.dot(hidden, conv_out, precision=HIGHEST_PREC))
    third_pre = lax.map(jax.checkpoint(third_block), second)
    mean_three, rstd_three = batch_stats(third_pre, pixel_total)

    def pool_block(block_pair):
        activity = block_pair[0]
        inputs = block_pair[1]
        summed = inputs + gain_out * (activity - mean_three) * rstd_three + bias_out
        return pool_crops(jax.nn.silu(summed))
    pooled = lax.map(jax.checkpoint(pool_block), (third_pre, pixel_rows)).reshape(CROPS, CIN)
    proj_pre = jnp.dot(pooled, proj_hidden, precision=HIGHEST_PREC)
    mean_proj, rstd_proj = batch_stats(proj_pre, crop_total)
    hidden_proj = jax.nn.silu(gain_proj * (proj_pre - mean_proj) * rstd_proj + bias_proj)
    embedding = jnp.dot(hidden_proj, proj_embed, precision=HIGHEST_PREC)
    mean_embed = lax.optimization_barrier(jnp.mean(embedding, axis=0))
    centered = embedding - mean_embed
    covariance = jnp.dot(centered.T, centered, precision=HIGHEST_PREC) / crop_total
    factor_low = jnp.linalg.cholesky(covariance)
    whitened = jax.scipy.linalg.solve_triangular(factor_low, centered.T, lower=True).T
    unit_rows = whitened * lax.rsqrt(lax.optimization_barrier(jnp.sum(whitened * whitened, axis=1, keepdims=True)) + UNIT_EPS)
    pair_gap = unit_rows[pair_global[:, 0]] - unit_rows[pair_global[:, 1]]
    return jnp.sum(pair_gap * pair_gap)

def reference(crops_seven, crops_six, crops_five, conv_in, gain_in, bias_in, conv_mid, gain_mid, bias_mid, conv_out, gain_out, bias_out, proj_hidden, gain_proj, bias_proj, proj_embed, pair_index):
    devices = N_DP * N_BLK
    pixel_rows = jnp.concatenate([crops_seven.reshape(devices, C7 * 49, CIN), crops_six.reshape(devices, C6 * 36, CIN), crops_five.reshape(devices, C5 * 25, CIN)], axis=1).astype(jnp.float32)
    params = tuple((weight.astype(jnp.float32) for weight in (conv_in, gain_in, bias_in, conv_mid, gain_mid, bias_mid, conv_out, gain_out, bias_out, proj_hidden, gain_proj, bias_proj, proj_embed)))
    owners = jnp.arange(PAIRS, dtype=jnp.int32) // PAIRS_DEV * SLOTS
    pair_global = (pair_index + owners[:, None]).astype(jnp.int32)
    total, pull_back = jax.vjp(lambda rows_in, weights_in: forward(rows_in, weights_in, pair_global), pixel_rows, params)
    grad_rows, grad_weights = pull_back(jnp.ones((), jnp.float32))
    seven_len = C7 * 49
    six_len = C6 * 36
    grad_seven = grad_rows[:, :seven_len].reshape(CROPS7, 7, 7, CIN)
    grad_six = grad_rows[:, seven_len:seven_len + six_len].reshape(CROPS6, 6, 6, CIN)
    grad_five = grad_rows[:, seven_len + six_len:].reshape(CROPS5, 5, 5, CIN)
    return (grad_seven, grad_six, grad_five, grad_weights[0], grad_weights[3], grad_weights[6], grad_weights[9], grad_weights[12], grad_weights[1], grad_weights[2], grad_weights[4], grad_weights[5], grad_weights[7], grad_weights[8], grad_weights[10], grad_weights[11])
```

```python
import jax
import jax.numpy as jnp
from jax import lax
from jax.experimental import pallas as pl
from jax.experimental.pallas import tpu as pltpu

F32 = jnp.float32
BF16 = jnp.bfloat16
NORM_EPS = 1e-05
UNIT_EPS = 1e-06
MIB = 1 << 20


def vmem(count):
    return pltpu.CompilerParams(vmem_limit_bytes=count * MIB)


def geometry(shapes):
    parts = []
    first = 0
    for shape in shapes:
        parts.append((shape[0], shape[1], first))
        first += shape[0] * shape[1]
    return parts, first


def silu_parts(q):
    s = 1.0 / (1.0 + jnp.exp(-q))
    return s


def live_rows(rows, width, side):
    return lax.rem(lax.broadcasted_iota(jnp.int32, (rows, width), 0), 8) < side


def moments(st_ref, total):
    mean = st_ref[0:1, :] * (1.0 / total)
    var = st_ref[1:2, :] * (1.0 / total) - mean * mean
    return mean, lax.rsqrt(var + NORM_EPS)


def split3(x):
    h = x.astype(BF16)
    r = x - h.astype(F32)
    m = r.astype(BF16)
    l = (r - m.astype(F32)).astype(BF16)
    return h, m, l


def split2(x):
    h = x.astype(BF16)
    return h, (x - h.astype(F32)).astype(BF16)


def mm(a, b):
    return jnp.dot(a, b, preferred_element_type=F32)


def mm_nt(a, b):
    return lax.dot_general(a, b, (((1,), (1,)), ((), ())), preferred_element_type=F32)


def mm_tn(a, b):
    return lax.dot_general(a, b, (((0,), (0,)), ((), ())), preferred_element_type=F32)


def first_conv(crops, conv_in):
    parts, slabs = geometry([c.shape for c in crops])
    width = conv_in.shape[0]
    chan = conv_in.shape[1]

    def kernel(x7, x6, x5, w_ref, xp_ref, a_ref, st_ref):
        total = jnp.zeros((1, chan), F32)
        squares = jnp.zeros((1, chan), F32)
        for ref, (n, s, first) in zip((x7, x6, x5), parts):
            for c in range(0, n, 2):
                rows = ref[c : c + 2].astype(F32).reshape(2 * s, s, width)
                rows = jnp.concatenate([rows, jnp.zeros((2 * s, 8 - s, width), F32)], axis=1)
                at = (first + c * s) * 8
                xp_ref[at : at + 16 * s, :] = rows.reshape(16 * s, width).astype(BF16)
            at = first * 8
            out = mm(xp_ref[at : at + n * s * 8, :], w_ref[...])
            total = total + jnp.sum(out, axis=0, keepdims=True)
            squares = squares + jnp.sum(out * out, axis=0, keepdims=True)
            out = out.reshape(n * s, 8, chan)
            for c in range(n):
                for i in range(s):
                    a_ref[first + i * n + c] = out[c * s + i]
        st_ref[0:1, :] = total
        st_ref[1:2, :] = squares

    return pl.pallas_call(
        kernel,
        out_shape=(
            jax.ShapeDtypeStruct((slabs * 8, width), BF16),
            jax.ShapeDtypeStruct((slabs, 8, chan), F32),
            jax.ShapeDtypeStruct((2, chan), F32),
        ),
        compiler_params=vmem(48),
        name="first_conv",
    )(*crops, conv_in)


def middle_conv(parts, first_pre, sums, total, gain, bias, kernel_rows):
    slabs, _, chan = first_pre.shape
    rows_all = slabs * 8

    def kernel(a_ref, st_ref, g_ref, b_ref, w_ref, cat_ref, o_ref, so_ref):
        mean, rstd = moments(st_ref, total)
        scale = g_ref[...] * rstd
        shift = b_ref[...] - mean * scale
        tot = jnp.zeros((1, chan), F32)
        squares = jnp.zeros((1, chan), F32)
        for n, s, first in parts:
            rows = n * s * 8
            at = first * 8
            step = n * 8
            keep = live_rows(rows, chan, s)
            q = a_ref[first : first + n * s].reshape(rows, chan) * scale + shift
            y = jnp.where(keep, q * silu_parts(q), 0.0)
            cat_ref[at : at + rows, 0:chan] = pltpu.roll(y, 1, 0).astype(BF16)
            cat_ref[at : at + rows, chan : 2 * chan] = y.astype(BF16)
            cat_ref[at : at + rows, 2 * chan : 3 * chan] = pltpu.roll(y, rows - 1, 0).astype(BF16)
            o_ref[at : at + rows, :] = mm(cat_ref[at : at + rows, :], w_ref[1])
            o_ref[at + step : at + rows, :] += mm(cat_ref[at : at + rows - step, :], w_ref[0])
            o_ref[at : at + rows - step, :] += mm(cat_ref[at + step : at + rows, :], w_ref[2])
            out = jnp.where(keep, o_ref[at : at + rows, :], 0.0)
            o_ref[at : at + rows, :] = out
            tot = tot + jnp.sum(out, axis=0, keepdims=True)
            squares = squares + jnp.sum(out * out, axis=0, keepdims=True)
        so_ref[0:1, :] = tot
        so_ref[1:2, :] = squares

    return pl.pallas_call(
        kernel,
        out_shape=(
            jax.ShapeDtypeStruct((rows_all, 3 * chan), BF16),
            jax.ShapeDtypeStruct((rows_all, chan), F32),
            jax.ShapeDtypeStruct((2, chan), F32),
        ),
        compiler_params=vmem(48),
        name="middle_conv",
    )(first_pre, sums, gain, bias, kernel_rows)


def last_conv(parts, second_pre, sums, total, gain, bias, conv_out):
    slabs, _, chan = second_pre.shape
    rows_all = slabs * 8
    width = conv_out.shape[1]
    block = 512

    def kernel(a_ref, st_ref, g_ref, b_ref, w_ref, y_ref, o_ref, so_ref, scr):
        @pl.when(pl.program_id(0) == 0)
        def _():
            mean, rstd = moments(st_ref, total)
            scale = g_ref[...] * rstd
            shift = b_ref[...] - mean * scale
            for n, s, first in parts:
                rows = n * s * 8
                q = a_ref[first : first + n * s].reshape(rows, chan) * scale + shift
                y = jnp.where(live_rows(rows, chan, s), q * silu_parts(q), 0.0).reshape(n * s, 8, chan)
                for i in range(s):
                    for c in range(n):
                        scr[first + c * s + i] = y[i * n + c]
            y_ref[...] = scr[...].reshape(rows_all, chan).astype(BF16)

        out = mm(y_ref[...], w_ref[...])
        o_ref[...] = out
        so_ref[0:1, :] = jnp.sum(out, axis=0, keepdims=True)
        so_ref[1:2, :] = jnp.sum(out * out, axis=0, keepdims=True)

    whole = lambda shape: pl.BlockSpec(shape, lambda j: (0,) * len(shape))
    return pl.pallas_call(
        kernel,
        grid=(width // block,),
        in_specs=[
            whole((slabs, 8, chan)),
            whole((2, chan)),
            whole((1, chan)),
            whole((1, chan)),
            pl.BlockSpec((chan, block), lambda j: (0, j)),
        ],
        out_specs=[
            whole((rows_all, chan)),
            pl.BlockSpec((rows_all, block), lambda j: (0, j)),
            pl.BlockSpec((2, block), lambda j: (0, j)),
        ],
        out_shape=(
            jax.ShapeDtypeStruct((rows_all, chan), BF16),
            jax.ShapeDtypeStruct((rows_all, width), F32),
            jax.ShapeDtypeStruct((2, width), F32),
        ),
        scratch_shapes=[pltpu.VMEM((slabs, 8, chan), F32)],
        compiler_params=vmem(40),
        name="last_conv",
    )(second_pre, sums, gain, bias, conv_out)


def crop_sums(parts, values, put):
    crop = 0
    for n, s, first in parts:
        block = values[first * 8 : (first + n * s) * 8].reshape(n, s, 8, values.shape[-1])
        block = jnp.sum(block, axis=1)
        put(crop, n, s, jnp.sum(block, axis=1))
        crop += n


def live_mask(parts, width):
    return jnp.concatenate([live_rows(n * s * 8, width, s) for n, s, _ in parts], axis=0)


def pool_embed(parts, slots, third_pre, sums, total, gain, bias, inputs, hidden_map, pair_row):
    rows_all, width = third_pre.shape
    hidden = hidden_map.shape[1]
    block = 256
    steps = width // block

    def kernel(a_ref, st_ref, g_ref, b_ref, x_ref, w_ref, p_ref, e_ref, ap_ref, scr, acc):
        j = pl.program_id(0)
        mean, rstd = moments(st_ref, total)
        scale = g_ref[...] * rstd
        shift = b_ref[...] - mean * scale
        scr[...] = jnp.zeros_like(scr)
        crop = 0
        for n, s, first in parts:
            rows = n * s * 8
            at = first * 8
            r = x_ref[at : at + rows, :].astype(F32) + (a_ref[at : at + rows, :] * scale + shift)
            v = jnp.where(live_rows(rows, block, s), r * silu_parts(r), 0.0)
            v = jnp.sum(jnp.sum(v.reshape(n, s, 8, block), axis=1), axis=1)
            scr[crop : crop + n, :] = v * (1.0 / (s * s))
            crop += n
        e = scr[...]
        e_ref[...] = e[0:slots]
        h, m, l = split3(e)
        out = mm(jnp.concatenate([h, m, l], axis=0), w_ref[...])

        @pl.when(j == 0)
        def _():
            acc[...] = out

        @pl.when(j > 0)
        def _():
            acc[...] += out

        @pl.when(j == steps - 1)
        def _():
            ap_ref[...] = acc[0:slots] + acc[32 : 32 + slots] + acc[64 : 64 + slots]
            ap_ref[crop : crop + 1, :] = p_ref[...]

    lane = lambda rows: pl.BlockSpec((rows, block), lambda j: (0, j))
    return pl.pallas_call(
        kernel,
        grid=(steps,),
        in_specs=[
            lane(rows_all),
            lane(2),
            lane(1),
            lane(1),
            lane(rows_all),
            pl.BlockSpec((block, hidden), lambda j: (j, 0)),
            pl.BlockSpec((1, hidden), lambda j: (0, 0)),
        ],
        out_specs=[lane(slots), pl.BlockSpec((slots, hidden), lambda j: (0, 0))],
        out_shape=(
            jax.ShapeDtypeStruct((slots, width), F32),
            jax.ShapeDtypeStruct((slots, hidden), F32),
        ),
        scratch_shapes=[pltpu.VMEM((32, block), F32), pltpu.VMEM((96, hidden), F32)],
        compiler_params=vmem(40),
        name="pool_embed",
    )(third_pre, sums, gain, bias, inputs, hidden_map, pair_row)


def slope_sums(parts, slots, third_pre, sums, total, gain, bias, inputs):
    rows_all, width = third_pre.shape
    block = 256

    def kernel(a_ref, st_ref, g_ref, b_ref, x_ref, s_ref, p_ref, t_ref):
        mean, rstd = moments(st_ref, total)
        gain_v = g_ref[...]
        bias_v = b_ref[...]
        p_ref[...] = jnp.zeros_like(p_ref)
        t_ref[...] = jnp.zeros_like(t_ref)
        crop = 0
        for n, s, first in parts:
            rows = n * s * 8
            at = first * 8
            normed = (a_ref[at : at + rows, :] - mean) * rstd
            r = x_ref[at : at + rows, :].astype(F32) + (normed * gain_v + bias_v)
            sig = silu_parts(r)
            v = jnp.where(live_rows(rows, block, s), sig * (1.0 + r * (1.0 - sig)), 0.0)
            s_ref[at : at + rows, :] = v.astype(BF16)
            p_ref[crop : crop + n, :] = jnp.sum(jnp.sum(v.reshape(n, s, 8, block), axis=1), axis=1)
            v = v * normed
            t_ref[crop : crop + n, :] = jnp.sum(jnp.sum(v.reshape(n, s, 8, block), axis=1), axis=1)
            crop += n

    lane = lambda rows: pl.BlockSpec((rows, block), lambda j: (0, j))
    return pl.pallas_call(
        kernel,
        grid=(width // block,),
        in_specs=[lane(rows_all), lane(2), lane(1), lane(1), lane(rows_all)],
        out_specs=[lane(rows_all), lane(slots), lane(slots)],
        out_shape=(
            jax.ShapeDtypeStruct((rows_all, width), BF16),
            jax.ShapeDtypeStruct((slots, width), F32),
            jax.ShapeDtypeStruct((slots, width), F32),
        ),
        compiler_params=vmem(32),
        name="slope_sums",
    )(third_pre, sums, gain, bias, inputs)


def projector(counts, pre, gain, bias, embed_map, hidden_map, plain, normed_sums, crop_total):
    blocks, slots, hidden = pre.shape
    emb = embed_map.shape[1]
    width = hidden_map.shape[0]
    crops = sum(n for n, _ in counts)
    rows_all = blocks * slots
    lanes = 256
    cols = hidden // lanes
    inv_total = 1.0 / crop_total
    group = 8
    half = 32

    def kernel(p_ref, g_ref, b_ref, we_ref, wh_ref, s1_ref, s2_ref,
               hp_ref, gap_ref, gz_ref, gg_ref, gb_ref, ge_ref, st_ref,
               n_scr, d_scr, z_scr, a_scr, i_scr, u_scr):
        live3 = lax.broadcasted_iota(jnp.int32, (blocks, slots, lanes), 1) < crops
        live = (lax.broadcasted_iota(jnp.int32, (blocks, slots, emb), 1) < crops).reshape(rows_all, emb)
        rstds = []
        for k in range(cols):
            at = slice(k * lanes, (k + 1) * lanes)
            raw = jnp.where(live3, p_ref[:, :, at], 0.0).reshape(rows_all, lanes)
            mean = jnp.sum(raw, axis=0, keepdims=True) * inv_total
            var = jnp.sum(raw * raw, axis=0, keepdims=True) * inv_total - mean * mean
            rstd = lax.rsqrt(var + NORM_EPS)
            rstds.append(rstd)
            normed = (raw - mean) * rstd
            q = normed * g_ref[:, at] + b_ref[:, at]
            sig = silu_parts(q)
            n_scr[:, at] = normed
            d_scr[:, at] = sig * (1.0 + q * (1.0 - sig))
            hp = jnp.where(live3.reshape(rows_all, lanes), q * sig, 0.0)
            hp_ref[:, at] = hp
            h, m = split2(hp)
            z = mm(h, we_ref[at, :]) + mm(m, we_ref[at, :])
            if k == 0:
                z_scr[...] = z
            else:
                z_scr[...] += z
        z = z_scr[...]
        mu = jnp.sum(z, axis=0, keepdims=True) * inv_total
        zc = jnp.where(live, z - mu, 0.0)
        zh, zm, zl = split3(zc)
        cat = jnp.concatenate([zh, zm, zl], axis=1)
        prod = mm_tn(cat, cat)
        cov = jnp.zeros((emb, emb), F32)
        for u in (2, 1, 0):
            for v in (2, 1, 0):
                cov = cov + prod[u * emb : (u + 1) * emb, v * emb : (v + 1) * emb]
        row_id = lax.broadcasted_iota(jnp.int32, (emb, emb), 0)
        col_id = lax.broadcasted_iota(jnp.int32, (emb, emb), 1)
        a_scr[...] = cov * inv_total
        i_scr[...] = jnp.where(row_id == col_id, 1.0, 0.0)

        def eliminate(j, carry):
            pivot_row = a_scr[pl.ds(j, 1), :]
            image_row = i_scr[pl.ds(j, 1), :]
            a = a_scr[...]
            pick = jnp.full((emb, emb), j, jnp.int32)
            column = jnp.take_along_axis(a, pick, axis=1)
            pivot = jnp.take_along_axis(jnp.broadcast_to(pivot_row, (8, emb)), pick[0:8], axis=1)
            inverse = (1.0 / pivot)[0:1]
            factor = jnp.where(row_id > j, column, 0.0)
            a_scr[...] = a - factor * (pivot_row * inverse)
            i_scr[...] = i_scr[...] - factor * (image_row * inverse)
            return carry

        lax.fori_loop(0, emb, eliminate, 0)
        diag = jnp.sum(jnp.where(row_id == col_id, a_scr[...], 0.0), axis=1, keepdims=True)
        white = i_scr[...] * lax.rsqrt(diag)
        ph, pm, pq = split3(white)
        w = mm_nt(
            jnp.concatenate([zh, zh, zm, zh, zl, zm], axis=1),
            jnp.concatenate([ph, pm, ph, pq, ph, pm], axis=1),
        )
        inv_len = lax.rsqrt(jnp.sum(w * w, axis=1, keepdims=True) + UNIT_EPS)
        u = w * inv_len
        uh, um, ul = split3(u)
        ucat = jnp.concatenate([uh, um, ul], axis=1)
        slot_id = lax.broadcasted_iota(jnp.int32, (slots, emb), 0).astype(F32)
        lane_id = lax.broadcasted_iota(jnp.int32, (slots, emb), 1)
        size = group * slots
        own = lax.broadcasted_iota(jnp.int32, (group, slots, size), 0).reshape(size, size)
        other_lane = lax.broadcasted_iota(jnp.int32, (size, size), 1)
        other = jnp.zeros((size, size), jnp.int32)
        for k in range(1, group):
            other = other + jnp.where(other_lane >= k * slots, 1, 0)
        same = own == other
        for k in range(blocks // group):
            ends = []
            for b in range(group):
                row = p_ref[k * group + b, crops : crops + 1, 0:emb]
                hit = jnp.where(slot_id == row, 1.0, 0.0)
                hit = hit - pltpu.roll(hit, emb - half, 1)
                ends.append(jnp.where(lane_id < half, hit, 0.0))
            ends = jnp.concatenate(ends, axis=0).astype(BF16)
            graph = jnp.where(same, mm_nt(ends, ends), 0.0).astype(BF16)
            at = slice(k * size, (k + 1) * size)
            gu = mm(graph, ucat[at])
            u_scr[at, :] = 2.0 * (gu[:, 0:emb] + (gu[:, emb : 2 * emb] + gu[:, 2 * emb : 3 * emb]))
        gu = u_scr[...]
        gw = (gu - u * jnp.sum(u * gu, axis=1, keepdims=True)) * inv_len
        g_col = jnp.sum(gw, axis=0, keepdims=True)
        wh, wm, _ = split3(w)
        gh, gm = split2(gw)
        prod = mm_tn(jnp.concatenate([gh, gm], axis=1), jnp.concatenate([wh, wm], axis=1))
        moment = (
            prod[emb:, emb:] + prod[0:emb, emb:] + prod[emb:, 0:emb] + prod[0:emb, 0:emb]
        )
        low = jnp.where(row_id >= col_id, moment, 0.0)
        strict = jnp.where(row_id > col_id, moment, 0.0)
        sym = (low + strict.T) * inv_total
        sh, sm = split2(sym)
        back = gw - g_col * inv_total - mm(
            jnp.concatenate([wh, wh, wm], axis=1), jnp.concatenate([sh, sm, sh], axis=0)
        )
        bh, bm = split2(back)
        gz = mm(jnp.concatenate([bh, bh, bm], axis=1), jnp.concatenate([ph, pm, ph], axis=0))
        gz = jnp.where(live, gz, 0.0)
        gz_ref[...] = gz
        zh2, zm2 = split2(gz)
        zcat = jnp.concatenate([zh2, zm2], axis=0)
        live_l = live3.reshape(rows_all, lanes)
        for k in range(cols):
            at = slice(k * lanes, (k + 1) * lanes)
            both = mm_nt(zcat, we_ref[at, :])
            gq = (both[0:rows_all] + both[rows_all:]) * d_scr[:, at]
            gb = jnp.sum(gq, axis=0, keepdims=True)
            gg = jnp.sum(gq * n_scr[:, at], axis=0, keepdims=True)
            gb_ref[:, at] = gb
            gg_ref[:, at] = gg
            gap = (g_ref[:, at] * rstds[k]) * (gq - gb * inv_total - n_scr[:, at] * (gg * inv_total))
            gap_ref[:, at] = jnp.where(live_l, gap, 0.0)
        mine = jnp.concatenate([gap_ref[0:slots, :], jnp.zeros((32 - slots, hidden), F32)], axis=0)
        h, m, l = split3(mine)
        out = mm_nt(jnp.concatenate([h, m, l], axis=0), wh_ref[...])
        ge = out[0:slots] + (out[32 : 32 + slots] + out[64 : 64 + slots])
        crop = 0
        ge_ref[...] = ge
        for n, s in counts:
            ge_ref[crop : crop + n, :] = ge[crop : crop + n] * (1.0 / (s * s))
            crop += n
        ge_ref[crop:, :] = jnp.zeros((slots - crop, width), F32)
        ge = ge_ref[...]
        st_ref[0:1, :] = jnp.sum(ge * s1_ref[...], axis=0, keepdims=True)
        st_ref[1:2, :] = jnp.sum(ge * s2_ref[...], axis=0, keepdims=True)

    return pl.pallas_call(
        kernel,
        out_shape=(
            jax.ShapeDtypeStruct((rows_all, hidden), F32),
            jax.ShapeDtypeStruct((rows_all, hidden), F32),
            jax.ShapeDtypeStruct((rows_all, emb), F32),
            jax.ShapeDtypeStruct((1, hidden), F32),
            jax.ShapeDtypeStruct((1, hidden), F32),
            jax.ShapeDtypeStruct((slots, width), F32),
            jax.ShapeDtypeStruct((2, width), F32),
        ),
        scratch_shapes=[
            pltpu.VMEM((rows_all, hidden), F32),
            pltpu.VMEM((rows_all, hidden), F32),
            pltpu.VMEM((rows_all, emb), F32),
            pltpu.VMEM((emb, emb), F32),
            pltpu.VMEM((emb, emb), F32),
            pltpu.VMEM((rows_all, emb), F32),
        ],
        compiler_params=vmem(56),
        name="projector",
    )(pre, gain, bias, embed_map, hidden_map, plain, normed_sums)


def last_back(parts, slope, share, third_pre, sums, grad_sums, total, gain, conv_out,
              second_pre, mid_sums, mid_gain, mid_bias):
    rows_all, width = third_pre.shape
    slabs, _, chan = second_pre.shape
    block = 256
    steps = width // block

    def kernel(s_ref, e_ref, a_ref, st_ref, gs_ref, g_ref, w_ref, m_ref, ms_ref, mg_ref, mb_ref,
               ga_ref, gq_ref, so_ref, acc):
        j = pl.program_id(0)
        mean, rstd = moments(st_ref, total)
        lift = g_ref[...] * rstd
        gg = gs_ref[1:2, :] * (1.0 / total)
        slant = rstd * gg
        base = gs_ref[0:1, :] * (1.0 / total) - mean * slant
        crop = 0
        for n, s, first in parts:
            rows = n * s * 8
            at = first * 8
            keep = live_rows(rows, block, s)
            share_rows = jnp.concatenate(
                [jnp.broadcast_to(e_ref[crop + c : crop + c + 1, :], (s * 8, block)) for c in range(n)], axis=0
            )
            gr = s_ref[at : at + rows, :].astype(F32) * share_rows
            ga = lift * (gr - base - a_ref[at : at + rows, :] * slant)
            ga_ref[at : at + rows, :] = jnp.where(keep, ga, 0.0).astype(BF16)
            crop += n
        out = mm_nt(ga_ref[...], w_ref[...])

        @pl.when(j == 0)
        def _():
            acc[...] = out

        @pl.when(j > 0)
        def _():
            acc[...] += out

        @pl.when(j == steps - 1)
        def _():
            mean2, rstd2 = moments(ms_ref, total)
            tot = jnp.zeros((1, chan), F32)
            tot_n = jnp.zeros((1, chan), F32)
            for n, s, first in parts:
                rows = n * s * 8
                at = first * 8
                grad = acc[at : at + rows, :].reshape(n * s, 8, chan)
                for c in range(n):
                    for i in range(s):
                        gq_ref[first + i * n + c] = grad[c * s + i]
                normed = (m_ref[first : first + n * s].reshape(rows, chan) - mean2) * rstd2
                q = normed * mg_ref[...] + mb_ref[...]
                sig = silu_parts(q)
                d = jnp.where(live_rows(rows, chan, s), sig * (1.0 + q * (1.0 - sig)), 0.0)
                gq = gq_ref[first : first + n * s].reshape(rows, chan) * d
                gq_ref[first : first + n * s] = gq.reshape(n * s, 8, chan)
                tot = tot + jnp.sum(gq, axis=0, keepdims=True)
                tot_n = tot_n + jnp.sum(gq * normed, axis=0, keepdims=True)
            so_ref[0:1, :] = tot
            so_ref[1:2, :] = tot_n

    lane = lambda rows: pl.BlockSpec((rows, block), lambda j: (0, j))
    whole = lambda *shape: pl.BlockSpec(shape, lambda j: (0,) * len(shape))
    return pl.pallas_call(
        kernel,
        grid=(steps,),
        in_specs=[lane(rows_all), lane(share.shape[0]), lane(rows_all), lane(2), lane(2), lane(1), lane(chan),
                  whole(slabs, 8, chan), whole(2, chan), whole(1, chan), whole(1, chan)],
        out_specs=[lane(rows_all), whole(slabs, 8, chan), whole(2, chan)],
        out_shape=(
            jax.ShapeDtypeStruct((rows_all, width), BF16),
            jax.ShapeDtypeStruct((slabs, 8, chan), F32),
            jax.ShapeDtypeStruct((2, chan), F32),
        ),
        scratch_shapes=[pltpu.VMEM((rows_all, chan), F32)],
        compiler_params=vmem(40),
        name="last_back",
    )(slope, share, third_pre, sums, grad_sums, gain, conv_out, second_pre, mid_sums, mid_gain, mid_bias)


def middle_back(parts, grad, grad_sums, total, second_pre, mid_sums, mid_gain, kernel_taps,
                first_pre, in_sums, in_gain, in_bias):
    slabs, _, chan = grad.shape
    rows_all = slabs * 8

    def kernel(gq_ref, gs_ref, a_ref, ms_ref, mg_ref, w_ref, f_ref, is_ref, ig_ref, ib_ref,
               ga_ref, o_ref, so_ref, acc):
        mean2, rstd2 = moments(ms_ref, total)
        lift = mg_ref[...] * rstd2
        slant = rstd2 * gs_ref[1:2, :] * (1.0 / total)
        base = gs_ref[0:1, :] * (1.0 / total) - mean2 * slant
        mean1, rstd1 = moments(is_ref, total)
        tot = jnp.zeros((1, chan), F32)
        tot_n = jnp.zeros((1, chan), F32)
        for n, s, first in parts:
            rows = n * s * 8
            at = first * 8
            step = n * 8
            keep = live_rows(rows, chan, s)
            ga = lift * (gq_ref[first : first + n * s].reshape(rows, chan) - base
                         - a_ref[first : first + n * s].reshape(rows, chan) * slant)
            ga_ref[at : at + rows, :] = jnp.where(keep, ga, 0.0).astype(BF16)
            total_rows = None
            for t in range(3):
                acc[at : at + rows, :] = mm_nt(ga_ref[at : at + rows, :], w_ref[3 + t])
                acc[at : at + rows - step, :] += mm_nt(ga_ref[at + step : at + rows, :], w_ref[t])
                acc[at + step : at + rows, :] += mm_nt(ga_ref[at : at + rows - step, :], w_ref[6 + t])
                piece = acc[at : at + rows, :]
                if t == 0:
                    piece = pltpu.roll(piece, rows - 1, 0)
                if t == 2:
                    piece = pltpu.roll(piece, 1, 0)
                total_rows = piece if total_rows is None else total_rows + piece
            normed = (f_ref[first : first + n * s].reshape(rows, chan) - mean1) * rstd1
            q = normed * ig_ref[...] + ib_ref[...]
            sig = silu_parts(q)
            gq = jnp.where(keep, total_rows * (sig * (1.0 + q * (1.0 - sig))), 0.0)
            o_ref[first : first + n * s] = gq.reshape(n * s, 8, chan)
            tot = tot + jnp.sum(gq, axis=0, keepdims=True)
            tot_n = tot_n + jnp.sum(gq * normed, axis=0, keepdims=True)
        so_ref[0:1, :] = tot
        so_ref[1:2, :] = tot_n

    return pl.pallas_call(
        kernel,
        out_shape=(
            jax.ShapeDtypeStruct((rows_all, chan), BF16),
            jax.ShapeDtypeStruct((slabs, 8, chan), F32),
            jax.ShapeDtypeStruct((2, chan), F32),
        ),
        scratch_shapes=[pltpu.VMEM((rows_all, chan), F32)],
        compiler_params=vmem(48),
        name="middle_back",
    )(grad, grad_sums, second_pre, mid_sums, mid_gain, kernel_taps, first_pre, in_sums, in_gain, in_bias)


def first_back(parts, grad, grad_sums, total, first_pre, in_sums, in_gain):
    slabs, _, chan = grad.shape
    rows_all = slabs * 8

    def kernel(gq_ref, gs_ref, f_ref, is_ref, ig_ref, ga_ref, scr):
        mean1, rstd1 = moments(is_ref, total)
        lift = ig_ref[...] * rstd1
        slant = rstd1 * gs_ref[1:2, :] * (1.0 / total)
        base = gs_ref[0:1, :] * (1.0 / total) - mean1 * slant
        for n, s, first in parts:
            rows = n * s * 8
            ga = lift * (gq_ref[first : first + n * s].reshape(rows, chan) - base
                         - f_ref[first : first + n * s].reshape(rows, chan) * slant)
            ga = jnp.where(live_rows(rows, chan, s), ga, 0.0).reshape(n * s, 8, chan)
            for i in range(s):
                for c in range(n):
                    scr[first + c * s + i] = ga[i * n + c]
        ga_ref[...] = scr[...].reshape(rows_all, chan).astype(BF16)

    return pl.pallas_call(
        kernel,
        out_shape=jax.ShapeDtypeStruct((rows_all, chan), BF16),
        scratch_shapes=[pltpu.VMEM((slabs, 8, chan), F32)],
        compiler_params=vmem(24),
        name="first_back",
    )(grad, grad_sums, first_pre, in_sums, in_gain)


def input_grads(parts, slope, share, grad_first, conv_in):
    rows_all, width = slope.shape
    chan = grad_first.shape[1]
    block = 256

    def kernel(s_ref, e_ref, g_ref, w_ref, o7, o6, o5):
        crop = 0
        for ref, (n, s, first) in zip((o7, o6, o5), parts):
            rows = n * s * 8
            at = first * 8
            out = mm_nt(g_ref[at : at + rows, :], w_ref[...])
            for c in range(n):
                lo = at + c * s * 8
                gr = s_ref[lo : lo + s * 8, :].astype(F32) * e_ref[crop + c : crop + c + 1, :]
                gx = (gr + out[c * s * 8 : (c + 1) * s * 8]).reshape(s, 8, block)
                ref[c] = gx[:, 0:s, :]
            crop += n

    lane = lambda rows: pl.BlockSpec((rows, block), lambda j: (0, j))
    return pl.pallas_call(
        kernel,
        grid=(width // block,),
        in_specs=[lane(rows_all), lane(share.shape[0]), pl.BlockSpec((rows_all, chan), lambda j: (0, 0)),
                  pl.BlockSpec((block, chan), lambda j: (j, 0))],
        out_specs=[pl.BlockSpec((n, s, s, block), lambda j: (0, 0, 0, j)) for n, s, _ in parts],
        out_shape=tuple(jax.ShapeDtypeStruct((n, s, s, width), F32) for n, s, _ in parts),
        compiler_params=vmem(32),
        name="input_grads",
    )(slope, share, grad_first, conv_in)


def middle_weight(parts, cat, grad):
    rows_all, chan = grad.shape

    def kernel(c_ref, g_ref, o_ref):
        r = pl.program_id(1)

        def add(shift):
            out = None
            for n, s, first in parts:
                step = n * 8
                rows = n * s * 8
                at = first * 8
                lhs = c_ref[at + max(shift, 0) * step : at + rows - max(-shift, 0) * step, :]
                rhs = g_ref[at + max(-shift, 0) * step : at + rows - max(shift, 0) * step, :]
                piece = mm_tn(lhs, rhs)
                out = piece if out is None else out + piece
            o_ref[0, 0] = out

        for k in range(3):
            pl.when(r == k)(lambda k=k: add(k - 1))

    return pl.pallas_call(
        kernel,
        grid=(3, 3),
        in_specs=[pl.BlockSpec((rows_all, chan), lambda t, r: (0, t)),
                  pl.BlockSpec((rows_all, chan), lambda t, r: (0, 0))],
        out_specs=pl.BlockSpec((1, 1, chan, chan), lambda t, r: (r, t, 0, 0)),
        out_shape=jax.ShapeDtypeStruct((3, 3, chan, chan), F32),
        compiler_params=vmem(32),
        name="middle_weight",
    )(cat, grad)


def masks_of(size, lowest=1):
    stages = []
    bit = lowest
    while bit < size:
        if 2 * bit < size:
            stages.append([bit, 2 * bit, 3 * bit])
            bit = 4 * bit
        else:
            stages.append([bit])
            bit = 2 * bit
    return stages


def swap(x, axis, mask):
    size = lax.axis_size(axis)
    return lax.ppermute(x, axis, [(i, i ^ mask) for i in range(size)])


def sum_all(x):
    stages = [("blk", [1])]
    stages += [("dp", m) for m in masks_of(lax.axis_size("dp"))]
    stages += [("blk", m) for m in masks_of(lax.axis_size("blk"), 2)]
    for axis, masks in stages:
        got = [swap(x, axis, m) for m in masks]
        for g in got:
            x = x + g
    return x


def gather_all(x):
    dp = lax.axis_index("dp")
    blk = lax.axis_index("blk")
    nblk = lax.axis_size("blk")
    x = x[None]
    where = [(0, 0)]
    stages = [("blk", m) for m in masks_of(nblk, 2)]
    stages += [("dp", m) for m in masks_of(lax.axis_size("dp"))]
    stages += [("blk", [1])]
    for axis, masks in stages:
        x = jnp.concatenate([x] + [swap(x, axis, m) for m in masks], axis=0)
        base = list(where)
        for m in masks:
            where += [(d ^ m, b) if axis == "dp" else (d, b ^ m) for d, b in base]
    number = jnp.stack([(dp ^ d) * nblk + (blk ^ b) for d, b in where])
    return x, number


def pick(x, index, axis):
    return lax.dynamic_index_in_dim(x, index, axis, keepdims=False)


def share_sum(grad):
    dp = lax.axis_index("dp")
    blk = lax.axis_index("blk")
    ndp = lax.axis_size("dp")
    nblk = lax.axis_size("blk")
    core = blk % 2
    z = blk // 2
    taps, _, rows, lanes = grad.shape
    g = grad.reshape(taps, nblk // 2, 2, ndp, rows // ndp, lanes)
    s = pick(g, core, 2) + swap(pick(g, 1 - core, 2), "blk", 1)
    got = [swap(pick(s, dp ^ k, 2), "dp", k) for k in range(1, ndp)]
    t = pick(s, dp, 2)
    for x in got:
        t = t + x
    got = [swap(pick(t, z ^ k, 1), "blk", 2 * k) for k in range(1, nblk // 2)]
    u = pick(t, z, 1)
    for x in got:
        u = u + x
    near = jnp.stack([u] + [swap(u, "dp", k) for k in range(1, ndp)], axis=1)
    out = jnp.concatenate([lax.dynamic_slice_in_dim(near, dp ^ k, 1, 1) for k in range(ndp)], axis=1)
    return out.reshape(taps, rows, lanes)


def projector_spread(counts, pre, gain, bias, embed_map, hidden_map, plain, normed_sums, crop_total):
    slots = pre.shape[0]
    crops = sum(n for n, _ in counts)
    high = lax.Precision.HIGHEST
    embed_map = embed_map.astype(F32)
    raw = pre[:crops]
    sums = sum_all(jnp.stack([jnp.sum(raw, axis=0), jnp.sum(raw * raw, axis=0)]))
    mean = sums[0] / crop_total
    rstd = lax.rsqrt(sums[1] / crop_total - mean * mean + NORM_EPS)
    normed = (raw - mean) * rstd
    q = gain * normed + bias
    sig = jax.nn.sigmoid(q)
    hp = q * sig
    z = jnp.dot(hp, embed_map, precision=high)
    emb = z.shape[1]
    z = jnp.concatenate([z, pre[crops : crops + 1, :emb], jnp.zeros((slots - crops - 1, emb), F32)], axis=0)
    z, _ = gather_all(z)
    blocks = z.shape[0]
    pairs = z[:, crops, :64]
    z = z[:, :crops].reshape(blocks * crops, emb)
    zc = z - jnp.sum(z, axis=0) / crop_total
    cov = jnp.dot(zc.T, zc, precision=high) / crop_total
    white = jax.scipy.linalg.solve_triangular(jnp.linalg.cholesky(cov), jnp.eye(emb, dtype=F32), lower=True)
    w = jnp.dot(zc, white.T, precision=high)
    inv_len = lax.rsqrt(jnp.sum(w * w, axis=1, keepdims=True) + UNIT_EPS)
    u = w * inv_len
    slot = jnp.arange(crops, dtype=F32)
    ends = (pairs[:, :32, None] == slot).astype(F32) - (pairs[:, 32:, None] == slot).astype(F32)
    gap = jnp.einsum("bpc,bce->bpe", ends, u.reshape(blocks, crops, emb), precision=high)
    gu = 2.0 * jnp.einsum("bpc,bpe->bce", ends, gap, precision=high).reshape(blocks * crops, emb)
    gw = (gu - u * jnp.sum(u * gu, axis=1, keepdims=True)) * inv_len
    moment = jnp.dot(gw.T, w, precision=high)
    sym = jnp.tril(moment) + jnp.tril(moment, -1).T
    back = gw[:crops] - (jnp.sum(gw, axis=0) + jnp.dot(w[:crops], sym, precision=high)) / crop_total
    gz = jnp.dot(back, white, precision=high)
    gq = jnp.dot(gz, embed_map.T, precision=high) * (sig * (1.0 + q * (1.0 - sig)))
    sums = sum_all(jnp.stack([jnp.sum(gq, axis=0), jnp.sum(gq * normed, axis=0)]))
    gap = gain * rstd * (gq - sums[0] / crop_total - normed * (sums[1] / crop_total))
    ge = jnp.dot(gap, hidden_map.astype(F32).T, precision=high)
    area = jnp.concatenate([jnp.full((n, 1), 1.0 / (s * s), F32) for n, s in counts])
    share = jnp.pad(ge * area, ((0, slots - crops), (0, 0)))
    stats = jnp.stack([jnp.sum(share * plain, axis=0), jnp.sum(share * normed_sums, axis=0)])
    return hp, gap, gz, sums[1:2], sums[0:1], share, stats


def body(crops_seven, crops_six, crops_five, conv_in, gain_in, bias_in, conv_mid, gain_mid, bias_mid,
         conv_out, gain_out, bias_out, proj_hidden, gain_proj, bias_proj, proj_embed, pair_index):
    crops_in = (crops_seven, crops_six, crops_five)
    parts, _ = geometry([c.shape for c in crops_in])
    counts = [(n, s) for n, s, _ in parts]
    ndp = lax.axis_size("dp")
    nblk = lax.axis_size("blk")
    blk = lax.axis_index("blk")
    devices = ndp * nblk
    crops = sum(n for n, _ in counts)
    total = float(sum(n * s * s for n, s in counts) * devices)
    crop_total = float(crops * devices)
    slots = 24
    width, chan = conv_in.shape
    hidden, emb = proj_embed.shape
    row = lambda v: v.reshape(1, -1)
    pair_row = jnp.pad(
        jnp.concatenate([pair_index[:, 0], pair_index[:, 1]]).astype(F32), (0, hidden - 2 * pair_index.shape[0])
    )

    inputs, first_pre, sums = first_conv(crops_in, conv_in)
    in_sums = sum_all(sums)
    cat, second_flat, sums = middle_conv(
        parts, first_pre, in_sums, total, row(gain_in), row(bias_in), conv_mid.reshape(3, 3 * chan, chan)
    )
    second_pre = second_flat.reshape(first_pre.shape)
    mid_sums = sum_all(sums)
    hidden_two, third_pre, sums = last_conv(parts, second_pre, mid_sums, total, row(gain_mid), row(bias_mid), conv_out)
    out_sums = sum_all(sums)
    pooled, pre = pool_embed(
        parts, slots, third_pre, out_sums, total, row(gain_out), row(bias_out), inputs, proj_hidden, row(pair_row)
    )
    whole = devices <= 32
    if whole:
        pre_all, number = gather_all(pre)
    slope, plain, normed_sums = slope_sums(parts, slots, third_pre, out_sums, total, row(gain_out), row(bias_out), inputs)
    middle = projector if whole else projector_spread
    hp, gap, gz, gg_proj, gb_proj, share, sums = middle(
        counts, pre_all if whole else pre, row(gain_proj), row(bias_proj), proj_embed, proj_hidden, plain,
        normed_sums, crop_total
    )
    out_back = sum_all(sums)
    grad_third, grad_two, sums = last_back(
        parts, slope, share, third_pre, out_sums, out_back, total, row(gain_out), conv_out,
        second_pre, mid_sums, row(gain_mid), row(bias_mid)
    )
    mid_back = sum_all(sums)
    local_out = lax.dot_general(hidden_two, grad_third, (((0,), (0,)), ((), ())), preferred_element_type=F32)
    grad_second, grad_one, sums = middle_back(
        parts, grad_two, mid_back, total, second_pre, mid_sums, row(gain_mid), conv_mid.reshape(9, chan, chan),
        first_pre, in_sums, row(gain_in), row(bias_in)
    )
    in_back = sum_all(sums)
    local_mid = middle_weight(parts, cat, grad_second)
    grad_first = first_back(parts, grad_one, in_back, total, first_pre, in_sums, row(gain_in))
    local_in = lax.dot_general(inputs, grad_first, (((0,), (0,)), ((), ())), preferred_element_type=F32)
    grads = input_grads(parts, slope, share, grad_first, conv_in)

    conv_out_grad = share_sum(local_out.reshape(1, nblk, chan // nblk, width))[0]
    conv_mid_grad = share_sum(local_mid.reshape(9, nblk, chan // nblk, chan)).reshape(3, 3, chan // nblk, chan)
    conv_in_grad = share_sum(local_in.reshape(1, nblk, width // nblk, chan))[0]

    high = lax.Precision.HIGH
    if whole:
        pooled_all = lax.all_gather(pooled, ("dp", "blk"), axis=0)
        own = width // nblk
        pooled_own = lax.dynamic_slice_in_dim(pooled_all, blk * own, own, 2)[number].reshape(devices * slots, own)
        hidden_grad = lax.dot_general(pooled_own, gap, (((0,), (0,)), ((), ())), precision=high)
        own = hidden // nblk
        embed_grad = lax.dot_general(
            lax.dynamic_slice_in_dim(hp, blk * own, own, 1), gz, (((0,), (0,)), ((), ())), precision=high
        )
    else:
        local = lax.dot_general(pooled[:crops], gap, (((0,), (0,)), ((), ())), precision=high)
        hidden_grad = share_sum(local.reshape(1, nblk, width // nblk, hidden))[0]
        local = lax.dot_general(hp, gz, (((0,), (0,)), ((), ())), precision=high)
        embed_grad = share_sum(local.reshape(1, nblk, hidden // nblk, emb))[0]
    return (
        *grads,
        conv_in_grad,
        conv_mid_grad,
        conv_out_grad,
        hidden_grad,
        embed_grad,
        in_back[1],
        in_back[0],
        mid_back[1],
        mid_back[0],
        out_back[1],
        out_back[0],
        gg_proj[0],
        gb_proj[0],
    )


def solution(mesh):
    from_both = ("dp", "blk")
    crop_spec = jax.sharding.PartitionSpec(from_both, None, None, None)
    spec = jax.sharding.PartitionSpec
    in_specs = (crop_spec,) * 3 + (spec(),) * 13 + (spec(from_both, None),)
    out_specs = (crop_spec,) * 3 + (
        spec("blk", None),
        spec(None, None, "blk", None),
        spec("blk", None),
        spec("blk", None),
        spec("blk", None),
    ) + (spec(),) * 8
    return jax.shard_map(body, mesh=mesh, in_specs=in_specs, out_specs=out_specs, check_vma=False)
```

```python
import jax
import jax.numpy as jnp
from jax import lax
from jax.experimental import pallas as pl
from jax.experimental.pallas import tpu as pltpu

F32 = jnp.float32
BF16 = jnp.bfloat16
NORM_EPS = 1e-05
UNIT_EPS = 1e-06
MIB = 1 << 20
ANY = pl.BlockSpec(memory_space=pl.ANY)
HBM = pl.BlockSpec(memory_space=pltpu.HBM)
SMEM = pl.BlockSpec(memory_space=pltpu.SMEM)
MARK = jax.ShapeDtypeStruct((8, 128), F32)


def params(mib):
    return pltpu.CompilerParams(vmem_limit_bytes=mib * MIB)


def cost(flops, moved, special=0):
    return pl.CostEstimate(flops=0, bytes_accessed=0, transcendentals=0)


class Part:
    def __init__(self, crops, side, first, slot):
        self.crops, self.side, self.first, self.slot = crops, side, first, slot
        self.by_column = crops != 8
        self.slabs = crops * side if self.by_column else side * side
        self.cut = slice(first, first + self.slabs)

    def sources(self, down, right):
        found = []
        for k in range(self.slabs):
            i, j = divmod(k, self.side)
            if self.by_column:
                i, j = j + down, 0
                there = 0 <= i < self.side
                found.append(k + down if there else None)
            else:
                i, j = i + down, j + right
                there = 0 <= i < self.side and 0 <= j < self.side
                found.append(i * self.side + j if there else None)
        return found


def layout(shapes):
    order = sorted(range(len(shapes)), key=lambda k: (shapes[k][0] != 8, -shapes[k][1]))
    parts = [None] * len(shapes)
    first = slot = 0
    for k in order:
        parts[k] = Part(shapes[k][0], shapes[k][1], first, slot)
        first += parts[k].slabs
        slot += shapes[k][0]
    return parts, [parts[k] for k in order], first


def sigmoid(q):
    return 0.5 * jnp.tanh(0.5 * q) + 0.5


def column_live(shape, side):
    return lax.broadcasted_iota(jnp.int32, shape, len(shape) - 2) < side


def live(parts, value):
    pieces = []
    for p in parts:
        piece = value[p.cut]
        if p.by_column:
            piece = jnp.where(column_live(piece.shape, p.side), piece, 0.0)
        pieces.append(piece)
    return jnp.concatenate(pieces, axis=0)


def crop_totals(parts, value, ref):
    for p in parts:
        piece = value[p.cut]
        if p.by_column:
            piece = piece.reshape(p.crops, p.side, 8, piece.shape[-1])
            total = jnp.sum(jnp.sum(piece, axis=1), axis=1)
        else:
            total = jnp.sum(piece, axis=0)
        ref[p.slot : p.slot + p.crops, :] = total


def spread(parts, ref):
    lanes = ref.shape[-1]
    pieces = []
    for p in parts:
        if p.by_column:
            for c in range(p.crops):
                row = ref[p.slot + c : p.slot + c + 1, :]
                pieces.append(jnp.broadcast_to(row[None], (p.side, 8, lanes)))
        else:
            pieces.append(jnp.broadcast_to(ref[p.slot : p.slot + 8, :][None], (p.slabs, 8, lanes)))
    return jnp.concatenate(pieces, axis=0)


def moments(st_ref, total):
    mean = st_ref[0:1, :] * (1.0 / total)
    var = st_ref[1:2, :] * (1.0 / total) - mean * mean
    return mean, lax.rsqrt(var + NORM_EPS)


def put_sums(ref, first, second):
    ref[0:1, :] = jnp.sum(first, axis=0, keepdims=True)
    ref[1:2, :] = jnp.sum(second, axis=0, keepdims=True)


def split3(x):
    h = x.astype(BF16)
    r = x - h.astype(F32)
    m = r.astype(BF16)
    return h, m, (r - m.astype(F32)).astype(BF16)


def split2(x):
    h = x.astype(BF16)
    return h, (x - h.astype(F32)).astype(BF16)


def mm(a, b):
    return jnp.dot(a, b, preferred_element_type=F32)


def mm_nt(a, b):
    return lax.dot_general(a, b, (((1,), (1,)), ((), ())), preferred_element_type=F32)


def mm_tn(a, b):
    return lax.dot_general(a, b, (((0,), (0,)), ((), ())), preferred_element_type=F32)


def whole(*shape):
    return pl.BlockSpec(shape, lambda *_: (0,) * len(shape))


def mark_of(x):
    return x[(0,) * (x.ndim - 2)][0:8, 0:128]


def lanes_of(block, *lead):
    return pl.BlockSpec((*lead, block), lambda j: (0,) * len(lead) + (j,))


def first_conv(parts, order, slabs, crops, conv_in):
    width, chan = conv_in.shape
    block = 512
    steps = width // block

    def kernel(*refs):
        x_refs, w_ref, xp_ref, a_ref, st_ref, scr = refs[:3], *refs[3:]
        j = pl.program_id(0)
        for p, ref in zip(parts, x_refs):
            x = ref[...].astype(F32)
            if p.by_column:
                x = x.reshape(p.slabs, p.side, block)
                x = jnp.concatenate([x, jnp.zeros((p.slabs, 8 - p.side, block), F32)], axis=1)
            scr[p.cut] = x
        xp_ref[...] = scr[...].reshape(slabs * 8, block).astype(BF16)
        out = mm(xp_ref[...], w_ref[...])

        @pl.when(j == 0)
        def _():
            a_ref[...] = out

        @pl.when(j > 0)
        def _():
            a_ref[...] += out

        @pl.when(j == steps - 1)
        def _():
            total = a_ref[...]
            put_sums(st_ref, total, total * total)

    rows = slabs * 8
    x_specs = [
        pl.BlockSpec((p.crops, p.side, p.side, block), lambda j: (0, 0, 0, j)) if p.by_column else lanes_of(block, p.slabs, 8)
        for p in parts
    ]
    return pl.pallas_call(
        kernel,
        grid=(steps,),
        in_specs=[*x_specs, pl.BlockSpec((block, chan), lambda j: (j, 0))],
        out_specs=[lanes_of(block, rows), whole(rows, chan), whole(2, chan)],
        out_shape=(
            jax.ShapeDtypeStruct((rows, width), BF16),
            jax.ShapeDtypeStruct((rows, chan), F32),
            jax.ShapeDtypeStruct((2, chan), F32),
        ),
        scratch_shapes=[pltpu.VMEM((slabs, 8, block), F32)],
        compiler_params=params(20),
        cost_estimate=cost(2 * rows * width * chan, 10 << 20),
        name="first_conv",
    )(*crops, conv_in)


def turn(order, chan, source, turned):
    for p in order:
        if p.by_column:
            value = source[p.cut].reshape(p.slabs * 8, chan)
            turned[0] = pltpu.roll(value, 1, 0).reshape(p.slabs, 8, chan)
            turned[1] = pltpu.roll(value, p.slabs * 8 - 1, 0).reshape(p.slabs, 8, chan)

def shifted(order, chan, source, turned, tap, forward):
    r, t = divmod(tap, 3)
    down, right = (r - 1, t - 1) if forward else (1 - r, 1 - t)
    pieces = []
    for p in order:
        found = p.sources(down, right)
        k = 0
        while k < p.slabs:
            end = k + 1
            if found[k] is None:
                while end < p.slabs and found[end] is None:
                    end += 1
                pieces.append(jnp.zeros((end - k, 8, chan), F32))
            else:
                while end < p.slabs and found[end] == found[k] + end - k:
                    end += 1
                at = found[k]
                if p.by_column and right:
                    pieces.append(turned[0 if right < 0 else 1, at : at + end - k])
                else:
                    pieces.append(source[p.first + at : p.first + at + end - k])
            k = end
    value = jnp.concatenate(pieces, axis=0)
    return value.reshape(value.shape[0] * 8, chan).astype(BF16)


def patch_columns(order, chan, source, turned, cat_ref, forward):
    turn(order, chan, source, turned)
    for tap in range(9):
        cat_ref[:, tap * chan : (tap + 1) * chan] = shifted(order, chan, source, turned, tap, forward)


def turned_shape(order, chan):
    return (2, max([p.slabs for p in order if p.by_column] + [1]), 8, chan)


def middle_conv(order, first_pre, sums, total, gain, bias, kernel_flat):
    rows, chan = first_pre.shape
    slabs = rows // 8

    def kernel(a_ref, st_ref, g_ref, b_ref, w_ref, y_ref, o_ref, so_ref, turned, cat_scr):
        mean, rstd = moments(st_ref, total)
        scale = g_ref[...] * rstd
        q = (a_ref[...] * scale + (b_ref[...] - mean * scale)).reshape(slabs, 8, chan)
        y_ref[...] = live(order, q * sigmoid(q))
        patch_columns(order, chan, y_ref, turned, cat_scr, True)
        out = live(order, mm(cat_scr[...], w_ref[...]).reshape(slabs, 8, chan)).reshape(rows, chan)
        o_ref[...] = out
        put_sums(so_ref, out, out * out)

    return pl.pallas_call(
        kernel,
        in_specs=[whole(rows, chan), whole(2, chan), whole(1, chan), whole(1, chan), whole(9 * chan, chan)],
        out_specs=[whole(slabs, 8, chan), whole(rows, chan), whole(2, chan)],
        out_shape=(
            jax.ShapeDtypeStruct((slabs, 8, chan), F32),
            jax.ShapeDtypeStruct((rows, chan), F32),
            jax.ShapeDtypeStruct((2, chan), F32),
        ),
        scratch_shapes=[
            pltpu.VMEM(turned_shape(order, chan), F32),
            pltpu.VMEM((rows, 9 * chan), BF16),
        ],
        compiler_params=params(24),
        cost_estimate=cost(18 * rows * chan * chan, 20 << 20),
        name="middle_conv",
    )(first_pre, sums, gain, bias, kernel_flat)


def last_conv(order, second_pre, sums, total, gain, bias, conv_out):
    rows, chan = second_pre.shape
    slabs = rows // 8
    width = conv_out.shape[1]
    block = 512

    def kernel(a_ref, st_ref, g_ref, b_ref, w_ref, y_ref, o_ref, so_ref):
        @pl.when(pl.program_id(0) == 0)
        def _():
            mean, rstd = moments(st_ref, total)
            scale = g_ref[...] * rstd
            q = (a_ref[...] * scale + (b_ref[...] - mean * scale)).reshape(slabs, 8, chan)
            y_ref[...] = live(order, q * sigmoid(q)).reshape(rows, chan).astype(BF16)

        out = mm(y_ref[...], w_ref[...])
        o_ref[...] = out
        put_sums(so_ref, out, out * out)

    return pl.pallas_call(
        kernel,
        grid=(width // block,),
        in_specs=[whole(rows, chan), whole(2, chan), whole(1, chan), whole(1, chan), lanes_of(block, chan)],
        out_specs=[whole(rows, chan), lanes_of(block, rows), lanes_of(block, 2)],
        out_shape=(
            jax.ShapeDtypeStruct((rows, chan), BF16),
            jax.ShapeDtypeStruct((rows, width), F32),
            jax.ShapeDtypeStruct((2, width), F32),
        ),
        compiler_params=params(16),
        cost_estimate=cost(2 * rows * width * chan, 12 << 20),
        name="last_conv",
    )(second_pre, sums, gain, bias, conv_out)


def pool_embed(order, slots, third_pre, sums, total, gain, bias, inputs, hidden_map, pair_row):
    rows, width = third_pre.shape
    slabs = rows // 8
    hidden = hidden_map.shape[1]
    crops = sum(p.crops for p in order)
    block = 256
    steps = width // block

    def kernel(a_ref, st_ref, g_ref, b_ref, x_ref, w_ref, p_ref, e_ref, ap_ref, scr, acc):
        j = pl.program_id(0)
        mean, rstd = moments(st_ref, total)
        scale = g_ref[...] * rstd
        shift = b_ref[...] - mean * scale
        r = x_ref[...].astype(F32) + (a_ref[...] * scale + shift)
        v = live(order, (r * sigmoid(r)).reshape(slabs, 8, block))
        scr[...] = jnp.zeros_like(scr)
        crop_totals(order, v, scr)
        for p in order:
            at = slice(p.slot, p.slot + p.crops)
            scr[at, :] = scr[at, :] * (1.0 / (p.side * p.side))
        e = scr[...]
        e_ref[...] = e[0:slots]
        h, m, l = split3(e)
        out = mm(jnp.concatenate([h, m, l], axis=0), w_ref[...])

        @pl.when(j == 0)
        def _():
            acc[...] = out

        @pl.when(j > 0)
        def _():
            acc[...] += out

        @pl.when(j == steps - 1)
        def _():
            ap_ref[...] = acc[0:slots] + acc[32 : 32 + slots] + acc[64 : 64 + slots]
            ap_ref[crops : crops + 1, :] = p_ref[...]

    return pl.pallas_call(
        kernel,
        grid=(steps,),
        in_specs=[
            lanes_of(block, rows), lanes_of(block, 2), lanes_of(block, 1), lanes_of(block, 1), lanes_of(block, rows),
            pl.BlockSpec((block, hidden), lambda j: (j, 0)), whole(1, hidden),
        ],
        out_specs=[lanes_of(block, slots), whole(slots, hidden)],
        out_shape=(jax.ShapeDtypeStruct((slots, width), F32), jax.ShapeDtypeStruct((slots, hidden), F32)),
        scratch_shapes=[pltpu.VMEM((32, block), F32), pltpu.VMEM((96, hidden), F32)],
        compiler_params=params(12),
        cost_estimate=cost(2 * 96 * width * hidden, 16 << 20, 2 * rows * width),
        name="pool_embed",
    )(third_pre, sums, gain, bias, inputs, hidden_map, pair_row)


def slope_sums(order, slots, third_pre, sums, total, gain, bias, inputs, hold=()):
    rows, width = third_pre.shape
    slabs = rows // 8
    block = 256

    def kernel(a_ref, st_ref, g_ref, b_ref, x_ref, *refs):
        s_ref, p_ref, t_ref = refs[len(hold) :][:3]
        for k in range(len(hold)):
            refs[len(hold) + 3 + k][...] = refs[k][...]
        mean, rstd = moments(st_ref, total)
        p_ref[...] = jnp.zeros_like(p_ref)
        t_ref[...] = jnp.zeros_like(t_ref)
        normed = (a_ref[...] - mean) * rstd
        r = x_ref[...].astype(F32) + (normed * g_ref[...] + b_ref[...])
        sig = sigmoid(r)
        v = live(order, (sig * (1.0 + r * (1.0 - sig))).reshape(slabs, 8, block))
        s_ref[...] = v.reshape(rows, block).astype(BF16)
        crop_totals(order, v, p_ref)
        crop_totals(order, v * normed.reshape(slabs, 8, block), t_ref)

    lane = lambda lead: lanes_of(block, lead)
    kept = [whole(*h.shape) for h in hold]
    return pl.pallas_call(
        kernel,
        grid=(width // block,),
        in_specs=[lane(rows), lane(2), lane(1), lane(1), lane(rows)] + kept,
        out_specs=[lane(rows), lane(slots), lane(slots)] + kept,
        out_shape=(
            jax.ShapeDtypeStruct((rows, width), BF16),
            jax.ShapeDtypeStruct((slots, width), F32),
            jax.ShapeDtypeStruct((slots, width), F32),
            *(jax.ShapeDtypeStruct(h.shape, F32) for h in hold),
        ),
        compiler_params=params(14),
        cost_estimate=cost(24 * rows * width, 8 * rows * width, 2 * rows * width),
        name="slope_sums",
    )(third_pre, sums, gain, bias, inputs, *hold)


def join(pieces, token):
    count = len(pieces)
    shape = pieces[0].shape

    def kernel(*refs):
        for k in range(count):
            refs[-1][k] = refs[k][...]

    return pl.pallas_call(
        kernel,
        in_specs=[whole(*shape)] * count + [whole(8, 128)] * len(token),
        out_specs=whole(count, *shape),
        out_shape=jax.ShapeDtypeStruct((count, *shape), F32),
        compiler_params=params(8),
        name="join",
    )(*pieces, *token)


def projector(order, pres, gain, bias, embed_map, hidden_map, plain, normed_sums, crop_total):
    held = [p.shape[0] for p in pres]
    blocks = sum(held)
    _, slots, hidden = pres[0].shape
    emb = embed_map.shape[1]
    width = hidden_map.shape[0]
    crops = sum(p.crops for p in order)
    rows_all = blocks * slots
    lanes = 256
    cols = hidden // lanes
    inv_total = 1.0 / crop_total
    group = 8
    half = 32

    def kernel(*refs):
        p_refs = refs[: len(held)]
        (g_ref, b_ref, we_ref, wh_ref, s1_ref, s2_ref, hp_ref, gap_ref, gz_ref, gg_ref, gb_ref, ge_ref, st_ref,
         n_scr, d_scr, z_scr, a_scr, i_scr, u_scr) = refs[len(held):]
        live_l = (lax.broadcasted_iota(jnp.int32, (blocks, slots, lanes), 1) < crops).reshape(rows_all, lanes)
        live_e = (lax.broadcasted_iota(jnp.int32, (blocks, slots, emb), 1) < crops).reshape(rows_all, emb)
        rstds = []
        for k in range(cols):
            at = slice(k * lanes, (k + 1) * lanes)
            raw = jnp.concatenate([ref[:, :, at].reshape(n * slots, lanes) for ref, n in zip(p_refs, held)], axis=0)
            raw = jnp.where(live_l, raw, 0.0)
            mean = jnp.sum(raw, axis=0, keepdims=True) * inv_total
            var = jnp.sum(raw * raw, axis=0, keepdims=True) * inv_total - mean * mean
            rstd = lax.rsqrt(var + NORM_EPS)
            rstds.append(rstd)
            normed = (raw - mean) * rstd
            q = normed * g_ref[:, at] + b_ref[:, at]
            sig = sigmoid(q)
            n_scr[:, at] = normed
            d_scr[:, at] = sig * (1.0 + q * (1.0 - sig))
            hp = jnp.where(live_l, q * sig, 0.0)
            hp_ref[:, at] = hp
            h, m = split2(hp)
            z = mm(h, we_ref[at, :]) + mm(m, we_ref[at, :])
            if k == 0:
                z_scr[...] = z
            else:
                z_scr[...] += z
        z = z_scr[...]
        mu = jnp.sum(z, axis=0, keepdims=True) * inv_total
        zc = jnp.where(live_e, z - mu, 0.0)
        zh, zm, zl = split3(zc)
        cat = jnp.concatenate([zh, zm, zl], axis=1)
        prod = mm_tn(cat, cat)
        cov = jnp.zeros((emb, emb), F32)
        for u in (2, 1, 0):
            for v in (2, 1, 0):
                cov = cov + prod[u * emb : (u + 1) * emb, v * emb : (v + 1) * emb]
        row_id = lax.broadcasted_iota(jnp.int32, (emb, emb), 0)
        col_id = lax.broadcasted_iota(jnp.int32, (emb, emb), 1)
        a_scr[...] = cov * inv_total
        i_scr[...] = jnp.where(row_id == col_id, 1.0, 0.0)

        def eliminate(step, carry):
            j = 2 * step
            a = a_scr[...]
            image = i_scr[...]
            row0 = a_scr[pl.ds(j, 1), :]
            row1 = a_scr[pl.ds(j + 1, 1), :]
            image0 = i_scr[pl.ds(j, 1), :]
            image1 = i_scr[pl.ds(j + 1, 1), :]
            first = jnp.full((emb, emb), j, jnp.int32)
            second = first + 1
            lane = lambda row, at: jnp.take_along_axis(jnp.broadcast_to(row, (8, emb)), at[0:8], axis=1)[0:1]
            column0 = jnp.take_along_axis(a, first, axis=1)
            column1 = jnp.take_along_axis(a, second, axis=1)
            inverse0 = 1.0 / lane(row0, first)
            ratio = lane(row0, second) * inverse0
            inverse1 = 1.0 / (lane(row1, second) - lane(row1, first) * ratio)
            factor0 = jnp.where(row_id > j, column0, 0.0)
            factor1 = jnp.where(row_id > j + 1, column1 - column0 * ratio, 0.0)
            below = lane(row1, first) * inverse0
            a_scr[...] = a - factor0 * (row0 * inverse0) - factor1 * ((row1 - below * row0) * inverse1)
            i_scr[...] = image - factor0 * (image0 * inverse0) - factor1 * ((image1 - below * image0) * inverse1)
            return carry

        lax.fori_loop(0, emb // 2, eliminate, 0)
        diag = jnp.sum(jnp.where(row_id == col_id, a_scr[...], 0.0), axis=1, keepdims=True)
        white = i_scr[...] * lax.rsqrt(diag)
        ph, pm, pq = split3(white)
        w = mm_nt(
            jnp.concatenate([zh, zh, zm, zh, zl, zm], axis=1),
            jnp.concatenate([ph, pm, ph, pq, ph, pm], axis=1),
        )
        inv_len = lax.rsqrt(jnp.sum(w * w, axis=1, keepdims=True) + UNIT_EPS)
        u = w * inv_len
        uh, um, ul = split3(u)
        ucat = jnp.concatenate([uh, um, ul], axis=1)
        slot_id = lax.broadcasted_iota(jnp.int32, (slots, emb), 0).astype(F32)
        lane_id = lax.broadcasted_iota(jnp.int32, (slots, emb), 1)
        size = group * slots
        own = lax.broadcasted_iota(jnp.int32, (group, slots, size), 0).reshape(size, size)
        other_lane = lax.broadcasted_iota(jnp.int32, (size, size), 1)
        other = jnp.zeros((size, size), jnp.int32)
        for k in range(1, group):
            other = other + jnp.where(other_lane >= k * slots, 1, 0)
        same = own == other
        pair_rows = [ref[b, crops : crops + 1, 0:emb] for ref, n in zip(p_refs, held) for b in range(n)]
        for k in range(blocks // group):
            ends = []
            for b in range(group):
                hit = jnp.where(slot_id == pair_rows[k * group + b], 1.0, 0.0)
                hit = hit - pltpu.roll(hit, emb - half, 1)
                ends.append(jnp.where(lane_id < half, hit, 0.0))
            ends = jnp.concatenate(ends, axis=0).astype(BF16)
            graph = jnp.where(same, mm_nt(ends, ends), 0.0).astype(BF16)
            at = slice(k * size, (k + 1) * size)
            gu = mm(graph, ucat[at])
            u_scr[at, :] = 2.0 * (gu[:, 0:emb] + (gu[:, emb : 2 * emb] + gu[:, 2 * emb : 3 * emb]))
        gu = u_scr[...]
        gw = (gu - u * jnp.sum(u * gu, axis=1, keepdims=True)) * inv_len
        g_col = jnp.sum(gw, axis=0, keepdims=True)
        wh, wm, _ = split3(w)
        gh, gm = split2(gw)
        prod = mm_tn(jnp.concatenate([gh, gm], axis=1), jnp.concatenate([wh, wm], axis=1))
        moment = (
            prod[emb:, emb:] + prod[0:emb, emb:] + prod[emb:, 0:emb] + prod[0:emb, 0:emb]
        )
        low = jnp.where(row_id >= col_id, moment, 0.0)
        strict = jnp.where(row_id > col_id, moment, 0.0)
        sym = (low + strict.T) * inv_total
        sh, sm = split2(sym)
        back = gw - g_col * inv_total - mm(
            jnp.concatenate([wh, wh, wm], axis=1), jnp.concatenate([sh, sm, sh], axis=0)
        )
        bh, bm = split2(back)
        gz = mm(jnp.concatenate([bh, bh, bm], axis=1), jnp.concatenate([ph, pm, ph], axis=0))
        gz = jnp.where(live_e, gz, 0.0)
        gz_ref[...] = gz
        zh2, zm2 = split2(gz)
        zcat = jnp.concatenate([zh2, zm2], axis=0)
        for k in range(cols):
            at = slice(k * lanes, (k + 1) * lanes)
            both = mm_nt(zcat, we_ref[at, :])
            gq = (both[0:rows_all] + both[rows_all:]) * d_scr[:, at]
            gb = jnp.sum(gq, axis=0, keepdims=True)
            gg = jnp.sum(gq * n_scr[:, at], axis=0, keepdims=True)
            gb_ref[:, at] = gb
            gg_ref[:, at] = gg
            gap = (g_ref[:, at] * rstds[k]) * (gq - gb * inv_total - n_scr[:, at] * (gg * inv_total))
            gap_ref[:, at] = jnp.where(live_l, gap, 0.0)
        mine = jnp.concatenate([gap_ref[0:slots, :], jnp.zeros((32 - slots, hidden), F32)], axis=0)
        h, m, l = split3(mine)
        out = mm_nt(jnp.concatenate([h, m, l], axis=0), wh_ref[...])
        ge_ref[...] = out[0:slots] + (out[32 : 32 + slots] + out[64 : 64 + slots])
        for p in order:
            at = slice(p.slot, p.slot + p.crops)
            ge_ref[at, :] = ge_ref[at, :] * (1.0 / (p.side * p.side))
        ge_ref[crops:, :] = jnp.zeros((slots - crops, width), F32)
        ge = ge_ref[...]
        put_sums(st_ref, ge * s1_ref[...], ge * s2_ref[...])

    return pl.pallas_call(
        kernel,
        out_shape=(
            jax.ShapeDtypeStruct((rows_all, hidden), F32),
            jax.ShapeDtypeStruct((rows_all, hidden), F32),
            jax.ShapeDtypeStruct((rows_all, emb), F32),
            jax.ShapeDtypeStruct((1, hidden), F32),
            jax.ShapeDtypeStruct((1, hidden), F32),
            jax.ShapeDtypeStruct((slots, width), F32),
            jax.ShapeDtypeStruct((2, width), F32),
        ),
        scratch_shapes=[
            pltpu.VMEM((rows_all, hidden), F32),
            pltpu.VMEM((rows_all, hidden), F32),
            pltpu.VMEM((rows_all, emb), F32),
            pltpu.VMEM((emb, emb), F32),
            pltpu.VMEM((emb, emb), F32),
            pltpu.VMEM((rows_all, emb), F32),
        ],
        compiler_params=params(30),
        cost_estimate=cost(10 << 30, 20 << 20),
        name="projector",
    )(*pres, gain, bias, embed_map, hidden_map, plain, normed_sums)


def halves(value, core, send, keep):
    for mine in range(2):

        @pl.when(core == mine)
        def _(mine=mine):
            send[...] = value(1 - mine)
            keep[...] = value(mine)


def last_back(order, slope, share, third_pre, sums, grad_sums, total, gain, conv_out,
              second_pre, mid_sums, mid_gain, mid_bias, hidden_two):
    rows, width = third_pre.shape
    slabs = rows // 8
    chan = second_pre.shape[1]
    block = 512
    steps = width // block

    def kernel(s_ref, e_ref, a_ref, st_ref, gs_ref, g_ref, w_ref, m_ref, ms_ref, mg_ref, mb_ref, y_ref,
               gq_ref, so_ref, weight_ref, ga_scr):
        j = pl.program_id(0)
        mean, rstd = moments(st_ref, total)
        lift = g_ref[...] * rstd
        slant = rstd * gs_ref[1:2, :] * (1.0 / total)
        base = gs_ref[0:1, :] * (1.0 / total) - mean * slant
        gr = s_ref[...].astype(F32) * spread(order, e_ref).reshape(rows, block)
        ga = lift * (gr - base - a_ref[...] * slant)
        ga_scr[...] = live(order, ga.reshape(slabs, 8, block)).reshape(rows, block).astype(BF16)
        out = mm_nt(ga_scr[...], w_ref[...])

        @pl.when(j == 0)
        def _():
            gq_ref[...] = out

        @pl.when(j > 0)
        def _():
            gq_ref[...] += out

        weight_ref[...] = mm_tn(y_ref[...], ga_scr[...])

        @pl.when(j == steps - 1)
        def _():
            mean2, rstd2 = moments(ms_ref, total)
            normed = (m_ref[...] - mean2) * rstd2
            q = normed * mg_ref[...] + mb_ref[...]
            sig = sigmoid(q)
            gq = gq_ref[...] * (sig * (1.0 + q * (1.0 - sig)))
            gq_ref[...] = gq
            put_sums(so_ref, gq, gq * normed)

    return pl.pallas_call(
        kernel,
        grid=(steps,),
        in_specs=[lanes_of(block, rows), lanes_of(block, share.shape[0]), lanes_of(block, rows), lanes_of(block, 2),
                  lanes_of(block, 2), lanes_of(block, 1), lanes_of(block, chan),
                  whole(rows, chan), whole(2, chan), whole(1, chan), whole(1, chan), whole(rows, chan)],
        out_specs=[whole(rows, chan), whole(2, chan), lanes_of(block, chan)],
        out_shape=(
            jax.ShapeDtypeStruct((rows, chan), F32),
            jax.ShapeDtypeStruct((2, chan), F32),
            jax.ShapeDtypeStruct((chan, width), F32),
        ),
        scratch_shapes=[pltpu.VMEM((rows, block), BF16)],
        compiler_params=params(40),
        cost_estimate=cost(4 * rows * width * chan, 24 << 20),
        name="last_back",
    )(slope, share, third_pre, sums, grad_sums, gain, conv_out, second_pre, mid_sums, mid_gain, mid_bias, hidden_two)


def middle_back(order, grad, grad_sums, total, second_pre, mid_sums, mid_gain, kernel_taps,
                first_pre, in_sums, in_gain, in_bias, token):
    rows, chan = grad.shape
    slabs = rows // 8

    def kernel(gq_ref, gs_ref, a_ref, ms_ref, mg_ref, w_ref, f_ref, is_ref, ig_ref, ib_ref, *refs):
        ga_ref, o_ref, so_ref, g_scr, turned, cat_scr, w_scr, sems = refs[len(token):]
        copies = [
            pltpu.make_async_copy(w_ref.at[k], w_scr.at[:, pl.ds(k * chan, chan)], sems.at[k]) for k in range(9)
        ]
        for copy in copies:
            copy.start()
        mean2, rstd2 = moments(ms_ref, total)
        lift = mg_ref[...] * rstd2
        slant = rstd2 * gs_ref[1:2, :] * (1.0 / total)
        base = gs_ref[0:1, :] * (1.0 / total) - mean2 * slant
        ga = live(order, (lift * (gq_ref[...] - base - a_ref[...] * slant)).reshape(slabs, 8, chan))
        g_scr[...] = ga
        ga_ref[...] = ga.reshape(rows, chan).astype(BF16)
        patch_columns(order, chan, g_scr, turned, cat_scr, False)
        for copy in copies:
            copy.wait()
        out = mm_nt(cat_scr[...], w_scr[...])
        mean1, rstd1 = moments(is_ref, total)
        normed = (f_ref[...] - mean1) * rstd1
        q = normed * ig_ref[...] + ib_ref[...]
        sig = sigmoid(q)
        gq = live(order, (out * (sig * (1.0 + q * (1.0 - sig)))).reshape(slabs, 8, chan)).reshape(rows, chan)
        o_ref[...] = gq
        put_sums(so_ref, gq, gq * normed)

    return pl.pallas_call(
        kernel,
        in_specs=[whole(rows, chan), whole(2, chan), whole(rows, chan), whole(2, chan), whole(1, chan), ANY,
                  whole(rows, chan), whole(2, chan), whole(1, chan), whole(1, chan)] + [whole(8, 128)] * len(token),
        out_specs=[whole(rows, chan), whole(rows, chan), whole(2, chan)],
        out_shape=(
            jax.ShapeDtypeStruct((rows, chan), BF16),
            jax.ShapeDtypeStruct((rows, chan), F32),
            jax.ShapeDtypeStruct((2, chan), F32),
        ),
        scratch_shapes=[
            pltpu.VMEM((slabs, 8, chan), F32),
            pltpu.VMEM(turned_shape(order, chan), F32),
            pltpu.VMEM((rows, 9 * chan), BF16),
            pltpu.VMEM((chan, 9 * chan), BF16),
            pltpu.SemaphoreType.DMA((9,)),
        ],
        compiler_params=params(28),
        cost_estimate=cost(18 * rows * chan * chan, 20 << 20),
        name="middle_back",
    )(grad, grad_sums, second_pre, mid_sums, mid_gain, kernel_taps, first_pre, in_sums, in_gain, in_bias, *token)


def middle_weight(order, hidden_one, grad, where, nblk, taps, token, hold=()):
    rows, chan = grad.shape
    slabs = rows // 8
    start, count = taps
    own = chan // nblk

    def kernel(at_ref, y_ref, g_ref, *refs):
        send_ref, keep_ref = refs[len(hold) + len(token) :][:2]
        mark, turned, lhs = refs[-3:]
        mark[...] = jnp.zeros_like(mark)
        k = pl.program_id(0)

        @pl.when(k == 0)
        def _():
            turn(order, chan, y_ref, turned)

        for tap in range(count):

            @pl.when(k == tap)
            def _(tap=tap):
                lhs[...] = shifted(order, chan, y_ref, turned, start + tap, True)

        weight = mm_tn(lhs[...], g_ref[...]).reshape(1, nblk // 2, 2, own, chan)
        halves(lambda c: weight[:, :, c], at_ref[0], send_ref, keep_ref)
        if hold:
            refs[-4][...] = refs[0][...]

    half = pl.BlockSpec((1, nblk // 2, own, chan), lambda k: (k, 0, 0, 0))
    kept = [whole(*h.shape) for h in hold]
    return pl.pallas_call(
        kernel,
        grid=(count,),
        in_specs=[SMEM, whole(slabs, 8, chan), whole(rows, chan)] + kept + [whole(8, 128)] * len(token),
        out_specs=[half, half] + kept + [whole(8, 128)],
        out_shape=(jax.ShapeDtypeStruct((count, nblk // 2, own, chan), F32),) * 2
        + tuple(jax.ShapeDtypeStruct(h.shape, F32) for h in hold)
        + (MARK,),
        scratch_shapes=[pltpu.VMEM(turned_shape(order, chan), F32), pltpu.VMEM((rows, chan), BF16)],
        compiler_params=params(14),
        cost_estimate=cost(2 * rows * chan * chan * count, 2 << 20),
        name="middle_weight",
    )(where, hidden_one, grad, *hold, *token)


def first_back(order, grad, grad_sums, total, first_pre, in_sums, in_gain, inputs, where, nblk, token):
    rows, chan = grad.shape
    slabs = rows // 8
    width = inputs.shape[1]
    own = width // nblk
    each = 2 * own
    merge = max(1, 512 // each)
    units = 4

    def kernel(at_ref, gq_ref, gs_ref, f_ref, is_ref, ig_ref, x_ref, *refs):
        ga_ref, send_ref, keep_ref, mark = refs[len(token):]
        mark[...] = jnp.zeros_like(mark)

        @pl.when(pl.program_id(0) == 0)
        def _():
            mean1, rstd1 = moments(is_ref, total)
            lift = ig_ref[...] * rstd1
            slant = rstd1 * gs_ref[1:2, :] * (1.0 / total)
            base = gs_ref[0:1, :] * (1.0 / total) - mean1 * slant
            ga = lift * (gq_ref[...] - base - f_ref[...] * slant)
            ga_ref[...] = live(order, ga.reshape(slabs, 8, chan)).reshape(rows, chan).astype(BF16)

        weight = mm_tn(x_ref[...], ga_ref[...]).reshape(merge, 2, units, own // units, chan)
        halves(lambda c: jnp.swapaxes(weight[:, c], 0, 1), at_ref[0], send_ref, keep_ref)

    half = pl.BlockSpec((units, merge, own // units, chan), lambda j: (0, j, 0, 0))
    return pl.pallas_call(
        kernel,
        grid=(width // (each * merge),),
        in_specs=[SMEM, whole(rows, chan), whole(2, chan), whole(rows, chan), whole(2, chan), whole(1, chan),
                  lanes_of(each * merge, rows)] + [whole(8, 128)] * len(token),
        out_specs=[whole(rows, chan), half, half, whole(8, 128)],
        out_shape=(
            jax.ShapeDtypeStruct((rows, chan), BF16),
            jax.ShapeDtypeStruct((units, nblk // 2, own // units, chan), F32),
            jax.ShapeDtypeStruct((units, nblk // 2, own // units, chan), F32),
            MARK,
        ),
        compiler_params=params(16),
        cost_estimate=cost(2 * rows * width * chan, 10 << 20),
        name="first_back",
    )(where, grad, grad_sums, first_pre, in_sums, in_gain, inputs, *token)


def input_grads(parts, order, slope, share, grad_first, conv_in, token):
    rows, width = slope.shape
    slabs = rows // 8
    chan = grad_first.shape[1]
    block = 512

    def kernel(s_ref, e_ref, g_ref, w_ref, *refs):
        gr = s_ref[...].astype(F32) * spread(order, e_ref).reshape(rows, block)
        gx = (gr + mm_nt(g_ref[...], w_ref[...])).reshape(slabs, 8, block)
        refs[-1][...] = jnp.zeros((8, 128), F32)
        for p, ref in zip(parts, refs[-4:-1]):
            piece = gx[p.cut]
            if p.by_column:
                ref[...] = piece.reshape(p.crops, p.side, 8, block)[:, :, 0 : p.side, :]
            else:
                ref[...] = piece

    out_specs = []
    out_shape = []
    for p in parts:
        if p.by_column:
            out_specs.append(pl.BlockSpec((p.crops, p.side, p.side, block), lambda j: (0, 0, 0, j)))
            out_shape.append(jax.ShapeDtypeStruct((p.crops, p.side, p.side, width), F32))
        else:
            out_specs.append(lanes_of(block, p.slabs, 8))
            out_shape.append(jax.ShapeDtypeStruct((p.slabs, 8, width), F32))
    return pl.pallas_call(
        kernel,
        grid=(width // block,),
        in_specs=[lanes_of(block, rows), lanes_of(block, share.shape[0]), whole(rows, chan),
                  pl.BlockSpec((block, chan), lambda j: (j, 0))] + [whole(8, 128)] * len(token),
        out_specs=out_specs + [whole(8, 128)],
        out_shape=(*out_shape, MARK),
        compiler_params=params(18),
        cost_estimate=cost(2 * rows * width * chan, 14 << 20),
        name="input_grads",
    )(slope, share, grad_first, conv_in, *token)


def masks_of(size, lowest=1):
    stages = []
    bit = lowest
    while bit < size:
        if 2 * bit < size:
            stages.append([bit, 2 * bit, 3 * bit])
            bit = 4 * bit
        else:
            stages.append([bit])
            bit = 2 * bit
    return stages


def swap(x, axis, mask):
    size = lax.axis_size(axis)
    return lax.ppermute(x, axis, [(i, i ^ mask) for i in range(size)])


def sum_stages(x, axis, stages):
    for masks in stages:
        got = [swap(x, axis, m) for m in masks]
        for g in got:
            x = x + g
    return x


def sum_core(x):
    return sum_stages(x, "blk", [[1]])


def sum_near(x):
    return sum_stages(x, "dp", masks_of(lax.axis_size("dp")))


def sum_far(x):
    return sum_stages(x, "blk", masks_of(lax.axis_size("blk"), 2))


def sum_all(x):
    return sum_far(sum_near(sum_core(x)))


def gather_all(x, between=None):
    dp = lax.axis_index("dp")
    blk = lax.axis_index("blk")
    nblk = lax.axis_size("blk")
    ndp = lax.axis_size("dp")
    joined = x[None]
    where = [0]
    for masks in masks_of(nblk, 2):
        joined = join([joined] + [swap(joined, "blk", m) for m in masks], []).reshape(-1, *x.shape)
        where = where + [w ^ m for m in masks for w in where]
    rows = [joined] + [swap(joined, "dp", k) for k in range(1, ndp)]
    extra = ()
    if between is not None:
        *extra, rows[0] = between(joined)
    rows += [swap(r, "blk", 1) for r in rows]
    number = [
        (dp ^ k) * nblk + (blk ^ (w ^ c)) for c in range(2) for k in range(ndp) for w in where
    ]
    return rows, jnp.stack(number), extra


def fold(kernel, count, where, ins, outs, token, hold, name):
    ins_n, outs_n, hold_n = len(ins), len(outs), len(hold)

    def whole_kernel(at_ref, *refs):
        kernel(at_ref, refs[:ins_n], refs[ins_n + hold_n + len(token) :][:outs_n])
        for k in range(hold_n):
            refs[len(refs) - 1 - hold_n + k][...] = refs[ins_n + k][...]
        refs[-1][...] = jnp.zeros((8, 128), F32)

    def unit(shape):
        if len(shape) == 3:
            return pl.BlockSpec((*shape[:2], shape[2] // count), lambda i: (0, 0, i))
        return pl.BlockSpec((1, *shape[1:]), lambda i: (i,) + (0,) * (len(shape) - 1))

    kept = [whole(*h.shape) for h in hold]
    result = pl.pallas_call(
        whole_kernel,
        grid=(count,),
        in_specs=[SMEM] + [unit(x.shape) for x in ins] + kept + [whole(8, 128)] * len(token),
        out_specs=[unit(x) for x in outs] + kept + [whole(8, 128)],
        out_shape=[jax.ShapeDtypeStruct(x, F32) for x in outs] + [jax.ShapeDtypeStruct(h.shape, F32) for h in hold] + [MARK],
        compiler_params=params(12),
        cost_estimate=cost(0, 0),
        name=name,
    )(where, *ins, *hold, *token)
    return result[:outs_n], result[outs_n:-1], result[-1]


def fold_first(keep, got, way, where, token, hold, extra=None):
    t, nz, _, r, n = keep.shape
    h = r // 2 if way == "both" else r
    ways = {"x": [0], "y": [1], "both": [0, 1]}[way]
    more = 0 if extra is None else 1

    def kernel(at_ref, ins, outs):
        x = at_ref[1] & 1
        y = at_ref[1] >> 1
        for k, w in enumerate(ways):
            rows = slice(k * h, k * h + h)
            for o in range(2):
                for out, q in (
                    (outs[2 * k], 2 * (1 - y) + o if w else 2 * o + 1 - x),
                    (outs[2 * k + 1], 2 * y + o if w else 2 * o + x),
                ):
                    out[0, 0:nz, o] = ins[0][0, :, q, rows, :] + ins[1][0, :, q, rows, :]
                    if more:
                        out[0, nz, o] = ins[2][q, rows, :]

    ins = [keep, got] + ([extra.reshape(4, r, t * n)] if more else [])
    return fold(kernel, t, where, ins, [(t, nz + more, 2, h, n)] * (2 * len(ways)), token, hold, "fold_first")


def fold_second(sums, way, where, token, hold):
    t, nz, _, h, n = sums[0].shape
    ways = {"x": [0], "y": [1], "both": [0, 1]}[way]

    def kernel(at_ref, ins, outs):
        for k, w in enumerate(ways):
            at = at_ref[1] & 1 if w else at_ref[1] >> 1
            add = lambda q: ins[2 * k][0, :, q] + ins[2 * k + 1][0, :, q]
            outs[2 * k][0] = add(1 - at)
            outs[2 * k + 1][0] = add(at)

    return fold(kernel, t, where, sums, [(t, nz, h, n)] * len(sums), token, hold, "fold_second")


def far_masks(nz):
    if nz == 4:
        return [1, 3]
    return [1 << k for k in range(nz.bit_length() - 1)]


def span(masks):
    offsets = [0]
    for m in masks:
        offsets = offsets + [o ^ m for o in offsets]
    return offsets


def fold_far_first(chains, masks, where, token, more):
    rest = span(masks[1:])
    ins = [x for chain in chains for x in chain]
    full = len(chains[0]) // 2 * chains[0][0].shape[2]
    n = ins[0].shape[-1]
    total = sum(chain[0].shape[0] for chain in chains)

    def kernel(at_ref, *refs):
        outs = refs[len(ins) + len(token) :]
        send, keep, mark = outs[:3]
        mark[...] = jnp.zeros_like(mark)
        first = at = 0
        for chain in chains:
            t, nz, h, _ = chain[0].shape
            for w in range(len(chain) // 2):
                a, b = refs[at : at + 2]
                at += 2
                rows = slice(w * h, w * h + h)
                for k, o in enumerate(rest):
                    send[first : first + t, k, rows, :] = a[:, at_ref[2] ^ o ^ masks[0]] + b[:, at_ref[2] ^ o ^ masks[0]]
                    keep[first : first + t, k, rows, :] = a[:, at_ref[2] ^ o] + b[:, at_ref[2] ^ o]
                if more:
                    outs[3][first : first + t, rows, :] = a[:, nz - 1] + b[:, nz - 1]
            first += t

    shape = (total, len(rest), full, n)
    whole_shape = [(total, full, n)] if more else []
    return pl.pallas_call(
        kernel,
        in_specs=[SMEM] + [whole(*x.shape) for x in ins] + [whole(8, 128)] * len(token),
        out_specs=[whole(*shape)] * 2 + [whole(8, 128)] + [whole(*x) for x in whole_shape],
        out_shape=[jax.ShapeDtypeStruct(shape, F32)] * 2 + [MARK] + [jax.ShapeDtypeStruct(x, F32) for x in whole_shape],
        compiler_params=params(14),
        cost_estimate=cost(0, 0),
        name="fold_far_first",
    )(where, *ins, *token)


def fold_far(keep, got, step, masks, where, token):
    rest = span(masks[step + 1 :])
    before = span(masks[step:])
    t, _, r, n = keep.shape

    def kernel(at_ref, a, b, *refs):
        send, stay, mark = refs[-3:]
        mark[...] = jnp.zeros_like(mark)
        for k, o in enumerate(rest):
            for out, offset in ((send, o ^ masks[step]), (stay, o)):
                out[:, k] = a[:, before.index(offset)] + b[:, before.index(offset)]

    shape = (t, len(rest), r, n)
    return pl.pallas_call(
        kernel,
        in_specs=[SMEM] + [whole(*keep.shape)] * 2 + [whole(8, 128)] * len(token),
        out_specs=[whole(*shape)] * 2 + [whole(8, 128)],
        out_shape=[jax.ShapeDtypeStruct(shape, F32)] * 2 + [MARK],
        compiler_params=params(12),
        cost_estimate=cost(0, 0),
        name="fold_far",
    )(where, keep, got, *token)


def place(pieces, where):
    t, r, n = pieces[0].shape
    count = len(pieces)

    def kernel(at_ref, *refs):
        for k in range(count):
            refs[-1][:, at_ref[1] ^ k] = refs[k][...]

    return pl.pallas_call(
        kernel,
        in_specs=[SMEM] + [whole(t, r, n)] * count,
        out_specs=whole(t, count, r, n),
        out_shape=jax.ShapeDtypeStruct((t, count, r, n), F32),
        compiler_params=params(8),
        name="place",
    )(where, *pieces)


def total_of(groups, token):
    total = sum(g[0].shape[0] for g in groups)
    r, n = groups[0][0].shape[-2:]
    ins = [x.reshape(x.shape[0], r, n) for g in groups for x in g]

    def kernel(*refs):
        at = row = 0
        for g in groups:
            t = g[0].shape[0]
            out = refs[at][...]
            for k in range(1, len(g)):
                out = out + refs[at + k][...]
            at += len(g)
            refs[-2][row : row + t] = out
            row += t
        refs[-1][...] = jnp.zeros((8, 128), F32)

    return pl.pallas_call(
        kernel,
        in_specs=[whole(*x.shape) for x in ins] + [whole(8, 128)] * len(token),
        out_specs=[whole(total, r, n), whole(8, 128)],
        out_shape=[jax.ShapeDtypeStruct((total, r, n), F32), MARK],
        compiler_params=params(8),
        name="total_of",
    )(*ins, *token)


class Reduce:
    def __init__(self, send, keep, mark, way, where, extra=None):
        self.where = where
        self.extra = extra
        self.mark = mark
        self.way = way
        t, nz, rows, n = keep.shape
        ndp = lax.axis_size("dp")
        cut = (t, nz, ndp, rows // ndp, n)
        self.keep = keep.reshape(cut)
        self.got = swap(send, "blk", 1).reshape(cut)
        self.masks = far_masks(nz)
        self.first_way = {"x": [1], "y": [2], "both": [1, 2]}[way]

    def near(self, folded, masks):
        outs, kept, self.mark = folded
        self.sums = []
        for k, mask in enumerate(masks):
            self.sums += [outs[2 * k + 1], swap(outs[2 * k], "dp", mask)]
        return kept

    def first(self, token=(), hold=()):
        return self.near(fold_first(self.keep, self.got, self.way, self.where, token, hold, self.extra), self.first_way)

    def second(self, token=(), hold=()):
        return self.near(fold_second(self.sums, self.way, self.where, token, hold), [3 - m for m in self.first_way])


class Spread:
    def __init__(self, chains, token=()):
        self.where = chains[0].where
        self.masks = chains[0].masks
        more = chains[0].extra is not None
        folded = fold_far_first([c.sums for c in chains], self.masks, self.where, token, more)
        self.extra = folded[3] if more else None
        self.next(folded[:3], 0)

    def next(self, folded, step):
        send, keep, self.mark = folded
        self.sums = [keep, swap(send, "blk", 2 * self.masks[step])]

    def far(self, token=()):
        for step in range(1, len(self.masks)):
            self.next(fold_far(*self.sums, step, self.masks, self.where, token), step)


class Gather:
    def __init__(self, parts, token=()):
        self.where = parts[0].where
        out, self.mark = total_of([p.sums if isinstance(p, Spread) else [p] for p in parts], token)
        self.pieces = [out] + [swap(out, "dp", k) for k in range(1, lax.axis_size("dp"))]

    def last(self):
        t, r, n = self.pieces[0].shape
        return place(self.pieces, self.where).reshape(t, len(self.pieces) * r, n)


def share_sum(local, where):
    nblk, rows, n = local.shape
    local = local.reshape(1, nblk // 2, 2, rows, n)
    pick = lambda c: lax.dynamic_index_in_dim(local, c, 2, keepdims=False)
    whole_sum = Reduce(pick(1 - where[0]), pick(where[0]), None, "x", where)
    whole_sum.first()
    whole_sum.second()
    out = Spread([whole_sum])
    out.far()
    return Gather([out]).last()[0]


def projector_spread(order, pre, gain, bias, embed_map, hidden_map, plain, normed_sums, crop_total):
    slots = pre.shape[0]
    crops = sum(p.crops for p in order)
    high = lax.Precision.HIGHEST
    embed_map = embed_map.astype(F32)
    raw = pre[:crops]
    sums = sum_all(jnp.stack([jnp.sum(raw, axis=0), jnp.sum(raw * raw, axis=0)]))
    mean = sums[0] / crop_total
    rstd = lax.rsqrt(sums[1] / crop_total - mean * mean + NORM_EPS)
    normed = (raw - mean) * rstd
    q = gain * normed + bias
    sig = jax.nn.sigmoid(q)
    hp = q * sig
    z = jnp.dot(hp, embed_map, precision=high)
    emb = z.shape[1]
    z = jnp.concatenate([z, pre[crops : crops + 1, :emb], jnp.zeros((slots - crops - 1, emb), F32)], axis=0)
    z, _, _ = gather_all(z)
    z = jnp.concatenate(z, axis=0)
    blocks = z.shape[0]
    pairs = z[:, crops, :64]
    z = z[:, :crops].reshape(blocks * crops, emb)
    zc = z - jnp.sum(z, axis=0) / crop_total
    cov = jnp.dot(zc.T, zc, precision=high) / crop_total
    white = jax.scipy.linalg.solve_triangular(jnp.linalg.cholesky(cov), jnp.eye(emb, dtype=F32), lower=True)
    w = jnp.dot(zc, white.T, precision=high)
    inv_len = lax.rsqrt(jnp.sum(w * w, axis=1, keepdims=True) + UNIT_EPS)
    u = w * inv_len
    slot = jnp.arange(crops, dtype=F32)
    ends = (pairs[:, :32, None] == slot).astype(F32) - (pairs[:, 32:, None] == slot).astype(F32)
    gap = jnp.einsum("bpc,bce->bpe", ends, u.reshape(blocks, crops, emb), precision=high)
    gu = 2.0 * jnp.einsum("bpc,bpe->bce", ends, gap, precision=high).reshape(blocks * crops, emb)
    gw = (gu - u * jnp.sum(u * gu, axis=1, keepdims=True)) * inv_len
    moment = jnp.dot(gw.T, w, precision=high)
    sym = jnp.tril(moment) + jnp.tril(moment, -1).T
    back = gw[:crops] - (jnp.sum(gw, axis=0) + jnp.dot(w[:crops], sym, precision=high)) / crop_total
    gz = jnp.dot(back, white, precision=high)
    gq = jnp.dot(gz, embed_map.T, precision=high) * (sig * (1.0 + q * (1.0 - sig)))
    sums = sum_all(jnp.stack([jnp.sum(gq, axis=0), jnp.sum(gq * normed, axis=0)]))
    gap = gain * rstd * (gq - sums[0] / crop_total - normed * (sums[1] / crop_total))
    ge = jnp.dot(gap, hidden_map.astype(F32).T, precision=high)
    area = jnp.concatenate([jnp.full((p.crops, 1), 1.0 / (p.side * p.side), F32) for p in order])
    share = jnp.pad(ge * area, ((0, slots - crops), (0, 0)))
    stats = jnp.stack([jnp.sum(share * plain, axis=0), jnp.sum(share * normed_sums, axis=0)])
    return hp, gap, gz, sums[1:2], sums[0:1], share, stats


def body(crops_seven, crops_six, crops_five, conv_in, gain_in, bias_in, conv_mid, gain_mid, bias_mid,
         conv_out, gain_out, bias_out, proj_hidden, gain_proj, bias_proj, proj_embed, pair_index):
    crops_in = (crops_seven, crops_six, crops_five)
    parts, order, slabs = layout([c.shape for c in crops_in])
    ndp = lax.axis_size("dp")
    nblk = lax.axis_size("blk")
    dp = lax.axis_index("dp")
    blk = lax.axis_index("blk")
    devices = ndp * nblk
    crops = sum(p.crops for p in parts)
    total = float(sum(p.crops * p.side * p.side for p in parts) * devices)
    crop_total = float(crops * devices)
    slots = 24
    width, chan = conv_in.shape
    hidden, emb = proj_embed.shape
    row = lambda v: v.reshape(1, -1)
    where = jnp.stack([blk % 2, dp, blk // 2]).astype(jnp.int32)
    first_crop = 0
    pair_slot = pair_index
    for p in parts:
        mine = (pair_index >= first_crop) & (pair_index < first_crop + p.crops)
        pair_slot = jnp.where(mine, pair_index - first_crop + p.slot, pair_slot)
        first_crop += p.crops
    pair_row = jnp.pad(
        jnp.concatenate([pair_slot[:, 0], pair_slot[:, 1]]).astype(F32), (0, hidden - 2 * pair_index.shape[0])
    )
    laid = [
        c if p.by_column else jnp.transpose(c, (1, 2, 0, 3)).reshape(p.slabs, 8, width) for c, p in zip(crops_in, parts)
    ]

    inputs, first_pre, sums = first_conv(parts, order, slabs, laid, conv_in)
    in_sums = sum_all(sums)
    hidden_one, second_pre, sums = middle_conv(
        order, first_pre, in_sums, total, row(gain_in), row(bias_in), conv_mid.reshape(9 * chan, chan)
    )
    mid_sums = sum_all(sums)
    hidden_two, third_pre, sums = last_conv(order, second_pre, mid_sums, total, row(gain_mid), row(bias_mid), conv_out)
    out_sums = sum_all(sums)
    gain_o, bias_o = row(gain_out), row(bias_out)
    pooled, pre = pool_embed(
        order, slots, third_pre, out_sums, total, gain_o, bias_o, inputs, proj_hidden, row(pair_row)
    )
    small = devices <= 32
    slopes = lambda *hold: slope_sums(
        order, slots, third_pre, out_sums, total, gain_o, bias_o, inputs, hold
    )
    if small:
        pre, number, (slope, plain, normed_sums) = gather_all(pre, slopes)
    else:
        slope, plain, normed_sums = slopes()
    middle = projector if small else projector_spread
    hp, gap, gz, gg_proj, gb_proj, share, sums = middle(
        order, pre, row(gain_proj), row(bias_proj), proj_embed, proj_hidden, plain, normed_sums, crop_total
    )
    out_back = sum_all(sums)
    grad_two, sums, local_out = last_back(
        order, slope, share, third_pre, out_sums, out_back, total, gain_o, conv_out,
        second_pre, mid_sums, row(gain_mid), row(bias_mid), hidden_two
    )
    pooled_all = lax.all_gather(pooled, ("dp", "blk"), axis=0) if small else pooled
    out_part = lax.psum_scatter(local_out, "blk", scatter_dimension=0, tiled=True)
    mid_back = sum_all(sums)
    grad_second, grad_one, sums = middle_back(
        order, grad_two, mid_back, total, second_pre, mid_sums, row(gain_mid), conv_mid.reshape(9, chan, chan),
        first_pre, in_sums, row(gain_in), row(bias_in), [mark_of(pooled_all)]
    )
    send, keep, core, mark = middle_weight(
        order, hidden_one, grad_second, where, nblk, (0, 5), [], [sum_core(sums)]
    )
    m0 = Reduce(send, keep, mark, "both", where)
    (near,) = m0.first(hold=[sum_near(core)])
    in_back = sum_stages(near, "blk", [[1 << k] for k in range(1, nblk.bit_length() - 1)])
    grad_first, send, keep, mark = first_back(
        order, grad_one, in_back, total, first_pre, in_sums, row(gain_in), inputs, where, nblk, []
    )
    i = Reduce(send, keep, mark, "both", where, out_part)
    m1 = Reduce(*middle_weight(order, hidden_one, grad_second, where, nblk, (5, 4), []), "both", where)
    i.first()
    *grads, mark = input_grads(parts, order, slope, share, grad_first, conv_in, [i.mark])
    m0.second()
    m1.first()

    high = lax.Precision.HIGH
    if small:
        own = width // nblk
        pooled_own = lax.dynamic_slice_in_dim(pooled_all, blk * own, own, 2)[number].reshape(devices * slots, own)
        hidden_grad = lax.dot_general(pooled_own, gap, (((0,), (0,)), ((), ())), precision=high)
        own = hidden // nblk
        embed_grad = lax.dot_general(
            lax.dynamic_slice_in_dim(hp, blk * own, own, 1), gz, (((0,), (0,)), ((), ())), precision=high
        )
    else:
        local = lax.dot_general(pooled[:crops], gap, (((0,), (0,)), ((), ())), precision=high)
        hidden_grad = share_sum(local.reshape(nblk, width // nblk, hidden), where)
        local = lax.dot_general(hp, gz, (((0,), (0,)), ((), ())), precision=high)
        embed_grad = share_sum(local.reshape(nblk, hidden // nblk, emb), where)

    i.second([mark])
    last = Spread([i], [])
    far0 = Spread([m0], [mark_of(hidden_grad), mark_of(embed_grad)])
    m1.second()
    last.far()
    far0.far()
    far1 = Spread([m1], [])
    early = Gather([last, last.extra], [])
    far1.far()
    late = Gather([far0, far1], [])
    early = early.last()
    conv_in_grad, out_grad = early[0:4].reshape(width // nblk, chan), early[4:8]
    out_grad = jnp.concatenate(list(out_grad), axis=1)
    mid_grad = late.last()
    grads = [
        g if p.by_column else jnp.transpose(g.reshape(p.side, p.side, 8, width), (2, 0, 1, 3))
        for g, p in zip(grads, parts)
    ]
    return (
        *grads,
        conv_in_grad,
        mid_grad.reshape(3, 3, chan // nblk, chan),
        out_grad,
        hidden_grad,
        embed_grad,
        in_back[1],
        in_back[0],
        mid_back[1],
        mid_back[0],
        out_back[1],
        out_back[0],
        gg_proj[0],
        gb_proj[0],
    )


def solution(mesh):
    from_both = ("dp", "blk")
    crop_spec = jax.sharding.PartitionSpec(from_both, None, None, None)
    spec = jax.sharding.PartitionSpec
    in_specs = (crop_spec,) * 3 + (spec(),) * 13 + (spec(from_both, None),)
    out_specs = (crop_spec,) * 3 + (
        spec("blk", None),
        spec(None, None, "blk", None),
        spec("blk", None),
        spec("blk", None),
        spec("blk", None),
    ) + (spec(),) * 8
    return jax.shard_map(body, mesh=mesh, in_specs=in_specs, out_specs=out_specs, check_vma=False)
```

```python
import jax
import jax.numpy as jnp
from jax import lax
from jax.experimental import pallas as pl
from jax.experimental.pallas import tpu as pltpu

F32 = jnp.float32
BF16 = jnp.bfloat16
NORM_EPS = 1e-05
UNIT_EPS = 1e-06
MIB = 1 << 20
ANY = pl.BlockSpec(memory_space=pl.ANY)
HBM = pl.BlockSpec(memory_space=pltpu.HBM)
SMEM = pl.BlockSpec(memory_space=pltpu.SMEM)
MARK = jax.ShapeDtypeStruct((8, 128), F32)


def params(mib):
    return pltpu.CompilerParams(vmem_limit_bytes=mib * MIB)


def cost(flops, moved, special=0):
    return pl.CostEstimate(flops=int(flops), bytes_accessed=int(moved), transcendentals=int(special))


class Part:
    def __init__(self, crops, side, first, slot):
        self.crops, self.side, self.first, self.slot = crops, side, first, slot
        self.by_column = crops != 8
        self.slabs = crops * side if self.by_column else side * side
        self.cut = slice(first, first + self.slabs)

    def sources(self, down, right):
        found = []
        for k in range(self.slabs):
            i, j = divmod(k, self.side)
            if self.by_column:
                i, j = j + down, 0
                there = 0 <= i < self.side
                found.append(k + down if there else None)
            else:
                i, j = i + down, j + right
                there = 0 <= i < self.side and 0 <= j < self.side
                found.append(i * self.side + j if there else None)
        return found


def layout(shapes):
    order = sorted(range(len(shapes)), key=lambda k: (shapes[k][0] != 8, -shapes[k][1]))
    parts = [None] * len(shapes)
    first = slot = 0
    for k in order:
        parts[k] = Part(shapes[k][0], shapes[k][1], first, slot)
        first += parts[k].slabs
        slot += shapes[k][0]
    return parts, [parts[k] for k in order], first


def sigmoid(q):
    return 0.5 * jnp.tanh(0.5 * q) + 0.5


def column_live(shape, side):
    return lax.broadcasted_iota(jnp.int32, shape, len(shape) - 2) < side


def live(parts, value):
    pieces = []
    for p in parts:
        piece = value[p.cut]
        if p.by_column:
            piece = jnp.where(column_live(piece.shape, p.side), piece, 0.0)
        pieces.append(piece)
    return jnp.concatenate(pieces, axis=0)


def crop_totals(parts, value, ref):
    for p in parts:
        piece = value[p.cut]
        if p.by_column:
            piece = piece.reshape(p.crops, p.side, 8, piece.shape[-1])
            total = jnp.sum(jnp.sum(piece, axis=1), axis=1)
        else:
            total = jnp.sum(piece, axis=0)
        ref[p.slot : p.slot + p.crops, :] = total


def spread(parts, ref):
    lanes = ref.shape[-1]
    pieces = []
    for p in parts:
        if p.by_column:
            for c in range(p.crops):
                row = ref[p.slot + c : p.slot + c + 1, :]
                pieces.append(jnp.broadcast_to(row[None], (p.side, 8, lanes)))
        else:
            pieces.append(jnp.broadcast_to(ref[p.slot : p.slot + 8, :][None], (p.slabs, 8, lanes)))
    return jnp.concatenate(pieces, axis=0)


def moments(st_ref, total):
    mean = st_ref[0:1, :] * (1.0 / total)
    var = st_ref[1:2, :] * (1.0 / total) - mean * mean
    return mean, lax.rsqrt(var + NORM_EPS)


def put_sums(ref, first, second):
    ref[0:1, :] = jnp.sum(first, axis=0, keepdims=True)
    ref[1:2, :] = jnp.sum(second, axis=0, keepdims=True)


def split3(x):
    h = x.astype(BF16)
    r = x - h.astype(F32)
    m = r.astype(BF16)
    return h, m, (r - m.astype(F32)).astype(BF16)


def split2(x):
    h = x.astype(BF16)
    return h, (x - h.astype(F32)).astype(BF16)


def mm(a, b):
    return jnp.dot(a, b, preferred_element_type=F32)


def mm_nt(a, b):
    return lax.dot_general(a, b, (((1,), (1,)), ((), ())), preferred_element_type=F32)


def mm_tn(a, b):
    return lax.dot_general(a, b, (((0,), (0,)), ((), ())), preferred_element_type=F32)


def whole(*shape):
    return pl.BlockSpec(shape, lambda *_: (0,) * len(shape))


def mark_of(x):
    return x[(0,) * (x.ndim - 2)][0:8, 0:128]


def lanes_of(block, *lead):
    return pl.BlockSpec((*lead, block), lambda j: (0,) * len(lead) + (j,))


def first_conv(parts, order, slabs, crops, conv_in):
    width, chan = conv_in.shape
    block = 512
    steps = width // block

    def kernel(*refs):
        x_refs, w_ref, xp_ref, a_ref, st_ref, scr = refs[:3], *refs[3:]
        j = pl.program_id(0)
        for p, ref in zip(parts, x_refs):
            x = ref[...].astype(F32)
            if p.by_column:
                x = x.reshape(p.slabs, p.side, block)
                x = jnp.concatenate([x, jnp.zeros((p.slabs, 8 - p.side, block), F32)], axis=1)
            scr[p.cut] = x
        xp_ref[...] = scr[...].reshape(slabs * 8, block).astype(BF16)
        out = mm(xp_ref[...], w_ref[...])

        @pl.when(j == 0)
        def _():
            a_ref[...] = out

        @pl.when(j > 0)
        def _():
            a_ref[...] += out

        @pl.when(j == steps - 1)
        def _():
            total = a_ref[...]
            put_sums(st_ref, total, total * total)

    rows = slabs * 8
    x_specs = [
        pl.BlockSpec((p.crops, p.side, p.side, block), lambda j: (0, 0, 0, j)) if p.by_column else lanes_of(block, p.slabs, 8)
        for p in parts
    ]
    return pl.pallas_call(
        kernel,
        grid=(steps,),
        in_specs=[*x_specs, pl.BlockSpec((block, chan), lambda j: (j, 0))],
        out_specs=[lanes_of(block, rows), whole(rows, chan), whole(2, chan)],
        out_shape=(
            jax.ShapeDtypeStruct((rows, width), BF16),
            jax.ShapeDtypeStruct((rows, chan), F32),
            jax.ShapeDtypeStruct((2, chan), F32),
        ),
        scratch_shapes=[pltpu.VMEM((slabs, 8, block), F32)],
        compiler_params=params(20),
        cost_estimate=cost(2 * rows * width * chan, 10 << 20),
        name="first_conv",
    )(*crops, conv_in)


def turn(order, chan, source, turned):
    for p in order:
        if p.by_column:
            value = source[p.cut].reshape(p.slabs * 8, chan)
            turned[0] = pltpu.roll(value, 1, 0).reshape(p.slabs, 8, chan)
            turned[1] = pltpu.roll(value, p.slabs * 8 - 1, 0).reshape(p.slabs, 8, chan)

def shifted(order, chan, source, turned, tap, forward):
    r, t = divmod(tap, 3)
    down, right = (r - 1, t - 1) if forward else (1 - r, 1 - t)
    pieces = []
    for p in order:
        found = p.sources(down, right)
        k = 0
        while k < p.slabs:
            end = k + 1
            if found[k] is None:
                while end < p.slabs and found[end] is None:
                    end += 1
                pieces.append(jnp.zeros((end - k, 8, chan), F32))
            else:
                while end < p.slabs and found[end] == found[k] + end - k:
                    end += 1
                at = found[k]
                if p.by_column and right:
                    pieces.append(turned[0 if right < 0 else 1, at : at + end - k])
                else:
                    pieces.append(source[p.first + at : p.first + at + end - k])
            k = end
    value = jnp.concatenate(pieces, axis=0)
    return value.reshape(value.shape[0] * 8, chan).astype(BF16)


def patch_columns(order, chan, source, turned, cat_ref, forward):
    turn(order, chan, source, turned)
    for tap in range(9):
        cat_ref[:, tap * chan : (tap + 1) * chan] = shifted(order, chan, source, turned, tap, forward)


def turned_shape(order, chan):
    return (2, max([p.slabs for p in order if p.by_column] + [1]), 8, chan)


def middle_conv(order, first_pre, sums, total, gain, bias, kernel_flat):
    rows, chan = first_pre.shape
    slabs = rows // 8

    def kernel(a_ref, st_ref, g_ref, b_ref, w_ref, y_ref, o_ref, so_ref, turned, cat_scr):
        mean, rstd = moments(st_ref, total)
        scale = g_ref[...] * rstd
        q = (a_ref[...] * scale + (b_ref[...] - mean * scale)).reshape(slabs, 8, chan)
        y_ref[...] = live(order, q * sigmoid(q))
        patch_columns(order, chan, y_ref, turned, cat_scr, True)
        out = live(order, mm(cat_scr[...], w_ref[...]).reshape(slabs, 8, chan)).reshape(rows, chan)
        o_ref[...] = out
        put_sums(so_ref, out, out * out)

    return pl.pallas_call(
        kernel,
        in_specs=[whole(rows, chan), whole(2, chan), whole(1, chan), whole(1, chan), whole(9 * chan, chan)],
        out_specs=[whole(slabs, 8, chan), whole(rows, chan), whole(2, chan)],
        out_shape=(
            jax.ShapeDtypeStruct((slabs, 8, chan), F32),
            jax.ShapeDtypeStruct((rows, chan), F32),
            jax.ShapeDtypeStruct((2, chan), F32),
        ),
        scratch_shapes=[
            pltpu.VMEM(turned_shape(order, chan), F32),
            pltpu.VMEM((rows, 9 * chan), BF16),
        ],
        compiler_params=params(24),
        cost_estimate=cost(18 * rows * chan * chan, 20 << 20),
        name="middle_conv",
    )(first_pre, sums, gain, bias, kernel_flat)


def last_conv(order, second_pre, sums, total, gain, bias, conv_out):
    rows, chan = second_pre.shape
    slabs = rows // 8
    width = conv_out.shape[1]
    block = 512

    def kernel(a_ref, st_ref, g_ref, b_ref, w_ref, y_ref, o_ref, so_ref):
        @pl.when(pl.program_id(0) == 0)
        def _():
            mean, rstd = moments(st_ref, total)
            scale = g_ref[...] * rstd
            q = (a_ref[...] * scale + (b_ref[...] - mean * scale)).reshape(slabs, 8, chan)
            y_ref[...] = live(order, q * sigmoid(q)).reshape(rows, chan).astype(BF16)

        out = mm(y_ref[...], w_ref[...])
        o_ref[...] = out
        put_sums(so_ref, out, out * out)

    return pl.pallas_call(
        kernel,
        grid=(width // block,),
        in_specs=[whole(rows, chan), whole(2, chan), whole(1, chan), whole(1, chan), lanes_of(block, chan)],
        out_specs=[whole(rows, chan), lanes_of(block, rows), lanes_of(block, 2)],
        out_shape=(
            jax.ShapeDtypeStruct((rows, chan), BF16),
            jax.ShapeDtypeStruct((rows, width), F32),
            jax.ShapeDtypeStruct((2, width), F32),
        ),
        compiler_params=params(16),
        cost_estimate=cost(2 * rows * width * chan, 12 << 20),
        name="last_conv",
    )(second_pre, sums, gain, bias, conv_out)


def pool_embed(order, slots, third_pre, sums, total, gain, bias, inputs, hidden_map, pair_row):
    rows, width = third_pre.shape
    slabs = rows // 8
    hidden = hidden_map.shape[1]
    crops = sum(p.crops for p in order)
    block = 256
    steps = width // block

    def kernel(a_ref, st_ref, g_ref, b_ref, x_ref, w_ref, p_ref, e_ref, ap_ref, scr, acc):
        j = pl.program_id(0)
        mean, rstd = moments(st_ref, total)
        scale = g_ref[...] * rstd
        shift = b_ref[...] - mean * scale
        r = x_ref[...].astype(F32) + (a_ref[...] * scale + shift)
        v = live(order, (r * sigmoid(r)).reshape(slabs, 8, block))
        scr[...] = jnp.zeros_like(scr)
        crop_totals(order, v, scr)
        for p in order:
            at = slice(p.slot, p.slot + p.crops)
            scr[at, :] = scr[at, :] * (1.0 / (p.side * p.side))
        e = scr[...]
        e_ref[...] = e[0:slots]
        h, m, l = split3(e)
        out = mm(jnp.concatenate([h, m, l], axis=0), w_ref[...])

        @pl.when(j == 0)
        def _():
            acc[...] = out

        @pl.when(j > 0)
        def _():
            acc[...] += out

        @pl.when(j == steps - 1)
        def _():
            ap_ref[...] = acc[0:slots] + acc[32 : 32 + slots] + acc[64 : 64 + slots]
            ap_ref[crops : crops + 1, :] = p_ref[...]

    return pl.pallas_call(
        kernel,
        grid=(steps,),
        in_specs=[
            lanes_of(block, rows), lanes_of(block, 2), lanes_of(block, 1), lanes_of(block, 1), lanes_of(block, rows),
            pl.BlockSpec((block, hidden), lambda j: (j, 0)), whole(1, hidden),
        ],
        out_specs=[lanes_of(block, slots), whole(slots, hidden)],
        out_shape=(jax.ShapeDtypeStruct((slots, width), F32), jax.ShapeDtypeStruct((slots, hidden), F32)),
        scratch_shapes=[pltpu.VMEM((32, block), F32), pltpu.VMEM((96, hidden), F32)],
        compiler_params=params(12),
        cost_estimate=cost(2 * 96 * width * hidden, 16 << 20, 2 * rows * width),
        name="pool_embed",
    )(third_pre, sums, gain, bias, inputs, hidden_map, pair_row)


def slope_sums(order, slots, third_pre, sums, total, gain, bias, inputs, hold=()):
    rows, width = third_pre.shape
    slabs = rows // 8
    block = 256

    def kernel(a_ref, st_ref, g_ref, b_ref, x_ref, *refs):
        s_ref, p_ref, t_ref = refs[len(hold) :][:3]
        for k in range(len(hold)):
            refs[len(hold) + 3 + k][...] = refs[k][...]
        mean, rstd = moments(st_ref, total)
        p_ref[...] = jnp.zeros_like(p_ref)
        t_ref[...] = jnp.zeros_like(t_ref)
        normed = (a_ref[...] - mean) * rstd
        r = x_ref[...].astype(F32) + (normed * g_ref[...] + b_ref[...])
        sig = sigmoid(r)
        v = live(order, (sig * (1.0 + r * (1.0 - sig))).reshape(slabs, 8, block))
        s_ref[...] = v.reshape(rows, block).astype(BF16)
        crop_totals(order, v, p_ref)
        crop_totals(order, v * normed.reshape(slabs, 8, block), t_ref)

    lane = lambda lead: lanes_of(block, lead)
    kept = [whole(*h.shape) for h in hold]
    return pl.pallas_call(
        kernel,
        grid=(width // block,),
        in_specs=[lane(rows), lane(2), lane(1), lane(1), lane(rows)] + kept,
        out_specs=[lane(rows), lane(slots), lane(slots)] + kept,
        out_shape=(
            jax.ShapeDtypeStruct((rows, width), BF16),
            jax.ShapeDtypeStruct((slots, width), F32),
            jax.ShapeDtypeStruct((slots, width), F32),
            *(jax.ShapeDtypeStruct(h.shape, F32) for h in hold),
        ),
        compiler_params=params(14),
        cost_estimate=cost(24 * rows * width, 8 * rows * width, 2 * rows * width),
        name="slope_sums",
    )(third_pre, sums, gain, bias, inputs, *hold)


def join(pieces, token):
    count = len(pieces)
    shape = pieces[0].shape

    def kernel(*refs):
        for k in range(count):
            refs[-1][k] = refs[k][...]

    return pl.pallas_call(
        kernel,
        in_specs=[whole(*shape)] * count + [whole(8, 128)] * len(token),
        out_specs=whole(count, *shape),
        out_shape=jax.ShapeDtypeStruct((count, *shape), F32),
        compiler_params=params(8),
        name="join",
    )(*pieces, *token)


def projector(order, pres, gain, bias, embed_map, hidden_map, plain, normed_sums, crop_total):
    held = [p.shape[0] for p in pres]
    blocks = sum(held)
    _, slots, hidden = pres[0].shape
    emb = embed_map.shape[1]
    width = hidden_map.shape[0]
    crops = sum(p.crops for p in order)
    rows_all = blocks * slots
    lanes = 256
    cols = hidden // lanes
    inv_total = 1.0 / crop_total
    group = 8
    half = 32

    def kernel(*refs):
        p_refs = refs[: len(held)]
        (g_ref, b_ref, we_ref, wh_ref, s1_ref, s2_ref, hp_ref, gap_ref, gz_ref, gg_ref, gb_ref, ge_ref, st_ref,
         n_scr, d_scr, z_scr, a_scr, i_scr, u_scr) = refs[len(held):]
        live_l = (lax.broadcasted_iota(jnp.int32, (blocks, slots, lanes), 1) < crops).reshape(rows_all, lanes)
        live_e = (lax.broadcasted_iota(jnp.int32, (blocks, slots, emb), 1) < crops).reshape(rows_all, emb)
        rstds = []
        for k in range(cols):
            at = slice(k * lanes, (k + 1) * lanes)
            raw = jnp.concatenate([ref[:, :, at].reshape(n * slots, lanes) for ref, n in zip(p_refs, held)], axis=0)
            raw = jnp.where(live_l, raw, 0.0)
            mean = jnp.sum(raw, axis=0, keepdims=True) * inv_total
            var = jnp.sum(raw * raw, axis=0, keepdims=True) * inv_total - mean * mean
            rstd = lax.rsqrt(var + NORM_EPS)
            rstds.append(rstd)
            normed = (raw - mean) * rstd
            q = normed * g_ref[:, at] + b_ref[:, at]
            sig = sigmoid(q)
            n_scr[:, at] = normed
            d_scr[:, at] = sig * (1.0 + q * (1.0 - sig))
            hp = jnp.where(live_l, q * sig, 0.0)
            hp_ref[:, at] = hp
            h, m = split2(hp)
            z = mm(h, we_ref[at, :]) + mm(m, we_ref[at, :])
            if k == 0:
                z_scr[...] = z
            else:
                z_scr[...] += z
        z = z_scr[...]
        mu = jnp.sum(z, axis=0, keepdims=True) * inv_total
        zc = jnp.where(live_e, z - mu, 0.0)
        zh, zm, zl = split3(zc)
        cat = jnp.concatenate([zh, zm, zl], axis=1)
        prod = mm_tn(cat, cat)
        cov = jnp.zeros((emb, emb), F32)
        for u in (2, 1, 0):
            for v in (2, 1, 0):
                cov = cov + prod[u * emb : (u + 1) * emb, v * emb : (v + 1) * emb]
        row_id = lax.broadcasted_iota(jnp.int32, (emb, emb), 0)
        col_id = lax.broadcasted_iota(jnp.int32, (emb, emb), 1)
        a_scr[...] = cov * inv_total
        i_scr[...] = jnp.where(row_id == col_id, 1.0, 0.0)

        def eliminate(step, carry):
            j = 2 * step
            a = a_scr[...]
            image = i_scr[...]
            row0 = a_scr[pl.ds(j, 1), :]
            row1 = a_scr[pl.ds(j + 1, 1), :]
            image0 = i_scr[pl.ds(j, 1), :]
            image1 = i_scr[pl.ds(j + 1, 1), :]
            first = jnp.full((emb, emb), j, jnp.int32)
            second = first + 1
            lane = lambda row, at: jnp.take_along_axis(jnp.broadcast_to(row, (8, emb)), at[0:8], axis=1)[0:1]
            column0 = jnp.take_along_axis(a, first, axis=1)
            column1 = jnp.take_along_axis(a, second, axis=1)
            inverse0 = 1.0 / lane(row0, first)
            ratio = lane(row0, second) * inverse0
            inverse1 = 1.0 / (lane(row1, second) - lane(row1, first) * ratio)
            factor0 = jnp.where(row_id > j, column0, 0.0)
            factor1 = jnp.where(row_id > j + 1, column1 - column0 * ratio, 0.0)
            below = lane(row1, first) * inverse0
            a_scr[...] = a - factor0 * (row0 * inverse0) - factor1 * ((row1 - below * row0) * inverse1)
            i_scr[...] = image - factor0 * (image0 * inverse0) - factor1 * ((image1 - below * image0) * inverse1)
            return carry

        lax.fori_loop(0, emb // 2, eliminate, 0)
        diag = jnp.sum(jnp.where(row_id == col_id, a_scr[...], 0.0), axis=1, keepdims=True)
        white = i_scr[...] * lax.rsqrt(diag)
        ph, pm, pq = split3(white)
        w = mm_nt(
            jnp.concatenate([zh, zh, zm, zh, zl, zm], axis=1),
            jnp.concatenate([ph, pm, ph, pq, ph, pm], axis=1),
        )
        inv_len = lax.rsqrt(jnp.sum(w * w, axis=1, keepdims=True) + UNIT_EPS)
        u = w * inv_len
        uh, um, ul = split3(u)
        ucat = jnp.concatenate([uh, um, ul], axis=1)
        slot_id = lax.broadcasted_iota(jnp.int32, (slots, emb), 0).astype(F32)
        lane_id = lax.broadcasted_iota(jnp.int32, (slots, emb), 1)
        size = group * slots
        own = lax.broadcasted_iota(jnp.int32, (group, slots, size), 0).reshape(size, size)
        other_lane = lax.broadcasted_iota(jnp.int32, (size, size), 1)
        other = jnp.zeros((size, size), jnp.int32)
        for k in range(1, group):
            other = other + jnp.where(other_lane >= k * slots, 1, 0)
        same = own == other
        pair_rows = [ref[b, crops : crops + 1, 0:emb] for ref, n in zip(p_refs, held) for b in range(n)]
        for k in range(blocks // group):
            ends = []
            for b in range(group):
                hit = jnp.where(slot_id == pair_rows[k * group + b], 1.0, 0.0)
                hit = hit - pltpu.roll(hit, emb - half, 1)
                ends.append(jnp.where(lane_id < half, hit, 0.0))
            ends = jnp.concatenate(ends, axis=0).astype(BF16)
            graph = jnp.where(same, mm_nt(ends, ends), 0.0).astype(BF16)
            at = slice(k * size, (k + 1) * size)
            gu = mm(graph, ucat[at])
            u_scr[at, :] = 2.0 * (gu[:, 0:emb] + (gu[:, emb : 2 * emb] + gu[:, 2 * emb : 3 * emb]))
        gu = u_scr[...]
        gw = (gu - u * jnp.sum(u * gu, axis=1, keepdims=True)) * inv_len
        g_col = jnp.sum(gw, axis=0, keepdims=True)
        wh, wm, _ = split3(w)
        gh, gm = split2(gw)
        prod = mm_tn(jnp.concatenate([gh, gm], axis=1), jnp.concatenate([wh, wm], axis=1))
        moment = (
            prod[emb:, emb:] + prod[0:emb, emb:] + prod[emb:, 0:emb] + prod[0:emb, 0:emb]
        )
        low = jnp.where(row_id >= col_id, moment, 0.0)
        strict = jnp.where(row_id > col_id, moment, 0.0)
        sym = (low + strict.T) * inv_total
        sh, sm = split2(sym)
        back = gw - g_col * inv_total - mm(
            jnp.concatenate([wh, wh, wm], axis=1), jnp.concatenate([sh, sm, sh], axis=0)
        )
        bh, bm = split2(back)
        gz = mm(jnp.concatenate([bh, bh, bm], axis=1), jnp.concatenate([ph, pm, ph], axis=0))
        gz = jnp.where(live_e, gz, 0.0)
        gz_ref[...] = gz
        zh2, zm2 = split2(gz)
        zcat = jnp.concatenate([zh2, zm2], axis=0)
        for k in range(cols):
            at = slice(k * lanes, (k + 1) * lanes)
            both = mm_nt(zcat, we_ref[at, :])
            gq = (both[0:rows_all] + both[rows_all:]) * d_scr[:, at]
            gb = jnp.sum(gq, axis=0, keepdims=True)
            gg = jnp.sum(gq * n_scr[:, at], axis=0, keepdims=True)
            gb_ref[:, at] = gb
            gg_ref[:, at] = gg
            gap = (g_ref[:, at] * rstds[k]) * (gq - gb * inv_total - n_scr[:, at] * (gg * inv_total))
            gap_ref[:, at] = jnp.where(live_l, gap, 0.0)
        mine = jnp.concatenate([gap_ref[0:slots, :], jnp.zeros((32 - slots, hidden), F32)], axis=0)
        h, m, l = split3(mine)
        out = mm_nt(jnp.concatenate([h, m, l], axis=0), wh_ref[...])
        ge_ref[...] = out[0:slots] + (out[32 : 32 + slots] + out[64 : 64 + slots])
        for p in order:
            at = slice(p.slot, p.slot + p.crops)
            ge_ref[at, :] = ge_ref[at, :] * (1.0 / (p.side * p.side))
        ge_ref[crops:, :] = jnp.zeros((slots - crops, width), F32)
        ge = ge_ref[...]
        put_sums(st_ref, ge * s1_ref[...], ge * s2_ref[...])

    return pl.pallas_call(
        kernel,
        out_shape=(
            jax.ShapeDtypeStruct((rows_all, hidden), F32),
            jax.ShapeDtypeStruct((rows_all, hidden), F32),
            jax.ShapeDtypeStruct((rows_all, emb), F32),
            jax.ShapeDtypeStruct((1, hidden), F32),
            jax.ShapeDtypeStruct((1, hidden), F32),
            jax.ShapeDtypeStruct((slots, width), F32),
            jax.ShapeDtypeStruct((2, width), F32),
        ),
        scratch_shapes=[
            pltpu.VMEM((rows_all, hidden), F32),
            pltpu.VMEM((rows_all, hidden), F32),
            pltpu.VMEM((rows_all, emb), F32),
            pltpu.VMEM((emb, emb), F32),
            pltpu.VMEM((emb, emb), F32),
            pltpu.VMEM((rows_all, emb), F32),
        ],
        compiler_params=params(30),
        cost_estimate=cost(10 << 30, 20 << 20),
        name="projector",
    )(*pres, gain, bias, embed_map, hidden_map, plain, normed_sums)


def projector_weights(pooled_all, order_of, blk, gap, hp, gz, nblk, token):
    blocks, slots, width = pooled_all.shape
    rows, hidden = gap.shape
    emb = gz.shape[1]
    own, own_hidden = width // nblk, hidden // nblk
    lanes = 256

    def kernel(at_ref, p_ref, ga_ref, hp_ref, gz_ref, *refs):
        o_ref, e_ref, mark, scr, high, low = refs[len(token) :]

        @pl.when(pl.program_id(0) == 0)
        def _():
            mark[...] = jnp.zeros_like(mark)
            for b in range(blocks):
                scr[b * slots : (b + 1) * slots, :] = p_ref[at_ref[1 + b]]
            h, m = split2(scr[...])
            high[...] = h
            low[...] = m
            hh, hm = split2(hp_ref[...])
            gh, gm = split2(gz_ref[...])
            e_ref[...] = mm_tn(hh, gh) + (mm_tn(hh, gm) + mm_tn(hm, gh))

        gh, gm = split2(ga_ref[...])
        o_ref[...] = mm_tn(high[...], gh) + (mm_tn(high[...], gm) + mm_tn(low[...], gh))

    return pl.pallas_call(
        kernel,
        grid_spec=pltpu.PrefetchScalarGridSpec(
            num_scalar_prefetch=1,
            grid=(hidden // lanes,),
            in_specs=[
                pl.BlockSpec((blocks, slots, own), lambda j, at: (0, 0, at[0])),
                pl.BlockSpec((rows, lanes), lambda j, at: (0, j)),
                pl.BlockSpec((rows, own_hidden), lambda j, at: (0, at[0])),
                pl.BlockSpec((rows, emb), lambda j, at: (0, 0)),
            ]
            + [pl.BlockSpec((8, 128), lambda j, at: (0, 0))] * len(token),
            out_specs=[
                pl.BlockSpec((own, lanes), lambda j, at: (0, j)),
                pl.BlockSpec((own_hidden, emb), lambda j, at: (0, 0)),
                pl.BlockSpec((8, 128), lambda j, at: (0, 0)),
            ],
            scratch_shapes=[pltpu.VMEM((rows, own), F32), pltpu.VMEM((rows, own), BF16), pltpu.VMEM((rows, own), BF16)],
        ),
        out_shape=(
            jax.ShapeDtypeStruct((own, hidden), F32),
            jax.ShapeDtypeStruct((own_hidden, emb), F32),
            MARK,
        ),
        compiler_params=params(58),
        cost_estimate=cost(2 << 30, 16 << 20),
        name="projector_weights",
    )(jnp.concatenate([blk[None], order_of]).astype(jnp.int32), pooled_all, gap, hp, gz, *token)


def halves(value, core, send, keep):
    for mine in range(2):

        @pl.when(core == mine)
        def _(mine=mine):
            send[...] = value(1 - mine)
            keep[...] = value(mine)


def last_back(order, slope, share, third_pre, sums, grad_sums, total, gain, conv_out,
              second_pre, mid_sums, mid_gain, mid_bias, hidden_two):
    rows, width = third_pre.shape
    slabs = rows // 8
    chan = second_pre.shape[1]
    block = 512
    steps = width // block

    def kernel(s_ref, e_ref, a_ref, st_ref, gs_ref, g_ref, w_ref, m_ref, ms_ref, mg_ref, mb_ref, y_ref,
               gq_ref, so_ref, weight_ref, ga_scr):
        j = pl.program_id(0)
        mean, rstd = moments(st_ref, total)
        lift = g_ref[...] * rstd
        slant = rstd * gs_ref[1:2, :] * (1.0 / total)
        base = gs_ref[0:1, :] * (1.0 / total) - mean * slant
        gr = s_ref[...].astype(F32) * spread(order, e_ref).reshape(rows, block)
        ga = lift * (gr - base - a_ref[...] * slant)
        ga_scr[...] = live(order, ga.reshape(slabs, 8, block)).reshape(rows, block).astype(BF16)
        out = mm_nt(ga_scr[...], w_ref[...])

        @pl.when(j == 0)
        def _():
            gq_ref[...] = out

        @pl.when(j > 0)
        def _():
            gq_ref[...] += out

        weight_ref[...] = mm_tn(y_ref[...], ga_scr[...])

        @pl.when(j == steps - 1)
        def _():
            mean2, rstd2 = moments(ms_ref, total)
            normed = (m_ref[...] - mean2) * rstd2
            q = normed * mg_ref[...] + mb_ref[...]
            sig = sigmoid(q)
            gq = gq_ref[...] * (sig * (1.0 + q * (1.0 - sig)))
            gq_ref[...] = gq
            put_sums(so_ref, gq, gq * normed)

    return pl.pallas_call(
        kernel,
        grid=(steps,),
        in_specs=[lanes_of(block, rows), lanes_of(block, share.shape[0]), lanes_of(block, rows), lanes_of(block, 2),
                  lanes_of(block, 2), lanes_of(block, 1), lanes_of(block, chan),
                  whole(rows, chan), whole(2, chan), whole(1, chan), whole(1, chan), whole(rows, chan)],
        out_specs=[whole(rows, chan), whole(2, chan), lanes_of(block, chan)],
        out_shape=(
            jax.ShapeDtypeStruct((rows, chan), F32),
            jax.ShapeDtypeStruct((2, chan), F32),
            jax.ShapeDtypeStruct((chan, width), F32),
        ),
        scratch_shapes=[pltpu.VMEM((rows, block), BF16)],
        compiler_params=params(40),
        cost_estimate=cost(4 * rows * width * chan, 24 << 20),
        name="last_back",
    )(slope, share, third_pre, sums, grad_sums, gain, conv_out, second_pre, mid_sums, mid_gain, mid_bias, hidden_two)


def middle_back(order, grad, grad_sums, total, second_pre, mid_sums, mid_gain, kernel_taps,
                first_pre, in_sums, in_gain, in_bias, token):
    rows, chan = grad.shape
    slabs = rows // 8

    def kernel(gq_ref, gs_ref, a_ref, ms_ref, mg_ref, w_ref, f_ref, is_ref, ig_ref, ib_ref, *refs):
        ga_ref, o_ref, so_ref, g_scr, turned, cat_scr, w_scr, sems = refs[len(token):]
        copies = [
            pltpu.make_async_copy(w_ref.at[k], w_scr.at[:, pl.ds(k * chan, chan)], sems.at[k]) for k in range(9)
        ]
        for copy in copies:
            copy.start()
        mean2, rstd2 = moments(ms_ref, total)
        lift = mg_ref[...] * rstd2
        slant = rstd2 * gs_ref[1:2, :] * (1.0 / total)
        base = gs_ref[0:1, :] * (1.0 / total) - mean2 * slant
        ga = live(order, (lift * (gq_ref[...] - base - a_ref[...] * slant)).reshape(slabs, 8, chan))
        g_scr[...] = ga
        ga_ref[...] = ga.reshape(rows, chan).astype(BF16)
        patch_columns(order, chan, g_scr, turned, cat_scr, False)
        for copy in copies:
            copy.wait()
        out = mm_nt(cat_scr[...], w_scr[...])
        mean1, rstd1 = moments(is_ref, total)
        normed = (f_ref[...] - mean1) * rstd1
        q = normed * ig_ref[...] + ib_ref[...]
        sig = sigmoid(q)
        gq = live(order, (out * (sig * (1.0 + q * (1.0 - sig)))).reshape(slabs, 8, chan)).reshape(rows, chan)
        o_ref[...] = gq
        put_sums(so_ref, gq, gq * normed)

    return pl.pallas_call(
        kernel,
        in_specs=[whole(rows, chan), whole(2, chan), whole(rows, chan), whole(2, chan), whole(1, chan), ANY,
                  whole(rows, chan), whole(2, chan), whole(1, chan), whole(1, chan)] + [whole(8, 128)] * len(token),
        out_specs=[whole(rows, chan), whole(rows, chan), whole(2, chan)],
        out_shape=(
            jax.ShapeDtypeStruct((rows, chan), BF16),
            jax.ShapeDtypeStruct((rows, chan), F32),
            jax.ShapeDtypeStruct((2, chan), F32),
        ),
        scratch_shapes=[
            pltpu.VMEM((slabs, 8, chan), F32),
            pltpu.VMEM(turned_shape(order, chan), F32),
            pltpu.VMEM((rows, 9 * chan), BF16),
            pltpu.VMEM((chan, 9 * chan), BF16),
            pltpu.SemaphoreType.DMA((9,)),
        ],
        compiler_params=params(28),
        cost_estimate=cost(18 * rows * chan * chan, 20 << 20),
        name="middle_back",
    )(grad, grad_sums, second_pre, mid_sums, mid_gain, kernel_taps, first_pre, in_sums, in_gain, in_bias, *token)


def middle_weight(order, hidden_one, grad, where, nblk, taps, token, hold=()):
    rows, chan = grad.shape
    slabs = rows // 8
    start, count = taps
    own = chan // nblk

    def kernel(at_ref, y_ref, g_ref, *refs):
        send_ref, keep_ref = refs[len(hold) + len(token) :][:2]
        mark, turned, lhs = refs[-3:]
        mark[...] = jnp.zeros_like(mark)
        k = pl.program_id(0)

        @pl.when(k == 0)
        def _():
            turn(order, chan, y_ref, turned)

        for tap in range(count):

            @pl.when(k == tap)
            def _(tap=tap):
                lhs[...] = shifted(order, chan, y_ref, turned, start + tap, True)

        weight = mm_tn(lhs[...], g_ref[...]).reshape(1, nblk // 2, 2, own, chan)
        halves(lambda c: weight[:, :, c], at_ref[0], send_ref, keep_ref)
        if hold:
            refs[-4][...] = refs[0][...]

    half = pl.BlockSpec((1, nblk // 2, own, chan), lambda k: (k, 0, 0, 0))
    kept = [whole(*h.shape) for h in hold]
    return pl.pallas_call(
        kernel,
        grid=(count,),
        in_specs=[SMEM, whole(slabs, 8, chan), whole(rows, chan)] + kept + [whole(8, 128)] * len(token),
        out_specs=[half, half] + kept + [whole(8, 128)],
        out_shape=(jax.ShapeDtypeStruct((count, nblk // 2, own, chan), F32),) * 2
        + tuple(jax.ShapeDtypeStruct(h.shape, F32) for h in hold)
        + (MARK,),
        scratch_shapes=[pltpu.VMEM(turned_shape(order, chan), F32), pltpu.VMEM((rows, chan), BF16)],
        compiler_params=params(14),
        cost_estimate=cost(2 * rows * chan * chan * count, 12 << 20),
        name="middle_weight",
    )(where, hidden_one, grad, *hold, *token)


def first_back(order, grad, grad_sums, total, first_pre, in_sums, in_gain, inputs, where, nblk, token):
    rows, chan = grad.shape
    slabs = rows // 8
    width = inputs.shape[1]
    own = width // nblk
    each = 2 * own
    merge = max(1, 512 // each)
    units = 4

    def kernel(at_ref, gq_ref, gs_ref, f_ref, is_ref, ig_ref, x_ref, *refs):
        ga_ref, send_ref, keep_ref, mark = refs[len(token):]
        mark[...] = jnp.zeros_like(mark)

        @pl.when(pl.program_id(0) == 0)
        def _():
            mean1, rstd1 = moments(is_ref, total)
            lift = ig_ref[...] * rstd1
            slant = rstd1 * gs_ref[1:2, :] * (1.0 / total)
            base = gs_ref[0:1, :] * (1.0 / total) - mean1 * slant
            ga = lift * (gq_ref[...] - base - f_ref[...] * slant)
            ga_ref[...] = live(order, ga.reshape(slabs, 8, chan)).reshape(rows, chan).astype(BF16)

        weight = mm_tn(x_ref[...], ga_ref[...]).reshape(merge, 2, units, own // units, chan)
        halves(lambda c: jnp.swapaxes(weight[:, c], 0, 1), at_ref[0], send_ref, keep_ref)

    half = pl.BlockSpec((units, merge, own // units, chan), lambda j: (0, j, 0, 0))
    return pl.pallas_call(
        kernel,
        grid=(width // (each * merge),),
        in_specs=[SMEM, whole(rows, chan), whole(2, chan), whole(rows, chan), whole(2, chan), whole(1, chan),
                  lanes_of(each * merge, rows)] + [whole(8, 128)] * len(token),
        out_specs=[whole(rows, chan), half, half, whole(8, 128)],
        out_shape=(
            jax.ShapeDtypeStruct((rows, chan), BF16),
            jax.ShapeDtypeStruct((units, nblk // 2, own // units, chan), F32),
            jax.ShapeDtypeStruct((units, nblk // 2, own // units, chan), F32),
            MARK,
        ),
        compiler_params=params(16),
        cost_estimate=cost(2 * rows * width * chan, 10 << 20),
        name="first_back",
    )(where, grad, grad_sums, first_pre, in_sums, in_gain, inputs, *token)


def input_grads(parts, order, slope, share, grad_first, conv_in, token):
    rows, width = slope.shape
    slabs = rows // 8
    chan = grad_first.shape[1]
    block = 512

    def kernel(s_ref, e_ref, g_ref, w_ref, *refs):
        gr = s_ref[...].astype(F32) * spread(order, e_ref).reshape(rows, block)
        gx = (gr + mm_nt(g_ref[...], w_ref[...])).reshape(slabs, 8, block)
        refs[-1][...] = jnp.zeros((8, 128), F32)
        for p, ref in zip(parts, refs[-4:-1]):
            piece = gx[p.cut]
            if p.by_column:
                ref[...] = piece.reshape(p.crops, p.side, 8, block)[:, :, 0 : p.side, :]
            else:
                ref[...] = piece

    out_specs = []
    out_shape = []
    for p in parts:
        if p.by_column:
            out_specs.append(pl.BlockSpec((p.crops, p.side, p.side, block), lambda j: (0, 0, 0, j)))
            out_shape.append(jax.ShapeDtypeStruct((p.crops, p.side, p.side, width), F32))
        else:
            out_specs.append(lanes_of(block, p.slabs, 8))
            out_shape.append(jax.ShapeDtypeStruct((p.slabs, 8, width), F32))
    return pl.pallas_call(
        kernel,
        grid=(width // block,),
        in_specs=[lanes_of(block, rows), lanes_of(block, share.shape[0]), whole(rows, chan),
                  pl.BlockSpec((block, chan), lambda j: (j, 0))] + [whole(8, 128)] * len(token),
        out_specs=out_specs + [whole(8, 128)],
        out_shape=(*out_shape, MARK),
        compiler_params=params(18),
        cost_estimate=cost(2 * rows * width * chan, 16 << 20),
        name="input_grads",
    )(slope, share, grad_first, conv_in, *token)


def masks_of(size, lowest=1):
    stages = []
    bit = lowest
    while bit < size:
        if 2 * bit < size:
            stages.append([bit, 2 * bit, 3 * bit])
            bit = 4 * bit
        else:
            stages.append([bit])
            bit = 2 * bit
    return stages


def swap(x, axis, mask):
    size = lax.axis_size(axis)
    return lax.ppermute(x, axis, [(i, i ^ mask) for i in range(size)])


def sum_stages(x, axis, stages):
    for masks in stages:
        got = [swap(x, axis, m) for m in masks]
        for g in got:
            x = x + g
    return x


def sum_core(x):
    return sum_stages(x, "blk", [[1]])


def sum_near(x):
    return sum_stages(x, "dp", masks_of(lax.axis_size("dp")))


def sum_far(x):
    return sum_stages(x, "blk", masks_of(lax.axis_size("blk"), 2))


def sum_all(x):
    return sum_far(sum_near(sum_core(x)))


def gather_all(x, between=None):
    dp = lax.axis_index("dp")
    blk = lax.axis_index("blk")
    nblk = lax.axis_size("blk")
    ndp = lax.axis_size("dp")
    joined = x[None]
    where = [0]
    for masks in masks_of(nblk, 2):
        joined = join([joined] + [swap(joined, "blk", m) for m in masks], []).reshape(-1, *x.shape)
        where = where + [w ^ m for m in masks for w in where]
    rows = [joined] + [swap(joined, "dp", k) for k in range(1, ndp)]
    extra = ()
    if between is not None:
        *extra, rows[0] = between(joined)
    rows += [swap(r, "blk", 1) for r in rows]
    number = [
        (dp ^ k) * nblk + (blk ^ (w ^ c)) for c in range(2) for k in range(ndp) for w in where
    ]
    return rows, jnp.stack(number), extra


def fold(kernel, count, where, ins, outs, token, hold, name):
    ins_n, outs_n, hold_n = len(ins), len(outs), len(hold)

    def whole_kernel(at_ref, *refs):
        kernel(at_ref, refs[:ins_n], refs[ins_n + hold_n + len(token) :][:outs_n])
        for k in range(hold_n):
            refs[len(refs) - 1 - hold_n + k][...] = refs[ins_n + k][...]
        refs[-1][...] = jnp.zeros((8, 128), F32)

    def unit(shape):
        if len(shape) == 3:
            return pl.BlockSpec((*shape[:2], shape[2] // count), lambda i: (0, 0, i))
        return pl.BlockSpec((1, *shape[1:]), lambda i: (i,) + (0,) * (len(shape) - 1))

    kept = [whole(*h.shape) for h in hold]
    result = pl.pallas_call(
        whole_kernel,
        grid=(count,),
        in_specs=[SMEM] + [unit(x.shape) for x in ins] + kept + [whole(8, 128)] * len(token),
        out_specs=[unit(x) for x in outs] + kept + [whole(8, 128)],
        out_shape=[jax.ShapeDtypeStruct(x, F32) for x in outs] + [jax.ShapeDtypeStruct(h.shape, F32) for h in hold] + [MARK],
        compiler_params=params(12),
        cost_estimate=cost(0, 8 << 20),
        name=name,
    )(where, *ins, *hold, *token)
    return result[:outs_n], result[outs_n:-1], result[-1]


def fold_first(keep, got, way, where, token, hold, extra=None):
    t, nz, _, r, n = keep.shape
    h = r // 2 if way == "both" else r
    ways = {"x": [0], "y": [1], "both": [0, 1]}[way]
    more = 0 if extra is None else 1

    def kernel(at_ref, ins, outs):
        x = at_ref[1] & 1
        y = at_ref[1] >> 1
        for k, w in enumerate(ways):
            rows = slice(k * h, k * h + h)
            for o in range(2):
                for out, q in (
                    (outs[2 * k], 2 * (1 - y) + o if w else 2 * o + 1 - x),
                    (outs[2 * k + 1], 2 * y + o if w else 2 * o + x),
                ):
                    out[0, 0:nz, o] = ins[0][0, :, q, rows, :] + ins[1][0, :, q, rows, :]
                    if more:
                        out[0, nz, o] = ins[2][q, rows, :]

    ins = [keep, got] + ([extra.reshape(4, r, t * n)] if more else [])
    return fold(kernel, t, where, ins, [(t, nz + more, 2, h, n)] * (2 * len(ways)), token, hold, "fold_first")


def fold_second(sums, way, where, token, hold):
    t, nz, _, h, n = sums[0].shape
    ways = {"x": [0], "y": [1], "both": [0, 1]}[way]

    def kernel(at_ref, ins, outs):
        for k, w in enumerate(ways):
            at = at_ref[1] & 1 if w else at_ref[1] >> 1
            add = lambda q: ins[2 * k][0, :, q] + ins[2 * k + 1][0, :, q]
            outs[2 * k][0] = add(1 - at)
            outs[2 * k + 1][0] = add(at)

    return fold(kernel, t, where, sums, [(t, nz, h, n)] * len(sums), token, hold, "fold_second")


def far_masks(nz):
    if nz == 4:
        return [1, 3]
    return [1 << k for k in range(nz.bit_length() - 1)]


def span(masks):
    offsets = [0]
    for m in masks:
        offsets = offsets + [o ^ m for o in offsets]
    return offsets


def fold_far_first(chains, masks, where, token, more):
    rest = span(masks[1:])
    ins = [x for chain in chains for x in chain]
    full = len(chains[0]) // 2 * chains[0][0].shape[2]
    n = ins[0].shape[-1]
    total = sum(chain[0].shape[0] for chain in chains)

    def kernel(at_ref, *refs):
        outs = refs[len(ins) + len(token) :]
        send, keep, mark = outs[:3]
        mark[...] = jnp.zeros_like(mark)
        first = at = 0
        for chain in chains:
            t, nz, h, _ = chain[0].shape
            for w in range(len(chain) // 2):
                a, b = refs[at : at + 2]
                at += 2
                rows = slice(w * h, w * h + h)
                for k, o in enumerate(rest):
                    send[first : first + t, k, rows, :] = a[:, at_ref[2] ^ o ^ masks[0]] + b[:, at_ref[2] ^ o ^ masks[0]]
                    keep[first : first + t, k, rows, :] = a[:, at_ref[2] ^ o] + b[:, at_ref[2] ^ o]
                if more:
                    outs[3][first : first + t, rows, :] = a[:, nz - 1] + b[:, nz - 1]
            first += t

    shape = (total, len(rest), full, n)
    whole_shape = [(total, full, n)] if more else []
    return pl.pallas_call(
        kernel,
        in_specs=[SMEM] + [whole(*x.shape) for x in ins] + [whole(8, 128)] * len(token),
        out_specs=[whole(*shape)] * 2 + [whole(8, 128)] + [whole(*x) for x in whole_shape],
        out_shape=[jax.ShapeDtypeStruct(shape, F32)] * 2 + [MARK] + [jax.ShapeDtypeStruct(x, F32) for x in whole_shape],
        compiler_params=params(14),
        cost_estimate=cost(0, 8 << 20),
        name="fold_far_first",
    )(where, *ins, *token)


def fold_far(keep, got, step, masks, where, token):
    rest = span(masks[step + 1 :])
    before = span(masks[step:])
    t, _, r, n = keep.shape

    def kernel(at_ref, a, b, *refs):
        send, stay, mark = refs[-3:]
        mark[...] = jnp.zeros_like(mark)
        for k, o in enumerate(rest):
            for out, offset in ((send, o ^ masks[step]), (stay, o)):
                out[:, k] = a[:, before.index(offset)] + b[:, before.index(offset)]

    shape = (t, len(rest), r, n)
    return pl.pallas_call(
        kernel,
        in_specs=[SMEM] + [whole(*keep.shape)] * 2 + [whole(8, 128)] * len(token),
        out_specs=[whole(*shape)] * 2 + [whole(8, 128)],
        out_shape=[jax.ShapeDtypeStruct(shape, F32)] * 2 + [MARK],
        compiler_params=params(12),
        cost_estimate=cost(0, 8 << 20),
        name="fold_far",
    )(where, keep, got, *token)


def place(pieces, where, side=0):
    t, r, n = pieces[0].shape
    count = len(pieces)
    rest = t - side

    def kernel(at_ref, *refs):
        for k in range(count):
            to = at_ref[1] ^ k
            refs[count][:, to] = refs[k][0:rest]
            for u in range(side):
                refs[-1][to, :, u * n : (u + 1) * n] = refs[k][rest + u]

    shapes = [(rest, count, r, n)] + ([(count, r, side * n)] if side else [])
    out = pl.pallas_call(
        kernel,
        in_specs=[SMEM] + [whole(t, r, n)] * count,
        out_specs=[whole(*x) for x in shapes],
        out_shape=[jax.ShapeDtypeStruct(x, F32) for x in shapes],
        compiler_params=params(12),
        name="place",
    )(where, *pieces)
    first = out[0].reshape(rest, count * r, n)
    return (first, out[1].reshape(count * r, side * n)) if side else first


def place_taps(pieces, where, first, taps, before=None):
    t, r, n = pieces[0].shape
    count = len(pieces)

    def kernel(at_ref, *refs):
        for k in range(count):
            refs[-2][0, at_ref[1] ^ k] = refs[k][0]
        refs[-1][...] = jnp.zeros((8, 128), F32)

    kept = [] if before is None else [before]
    return pl.pallas_call(
        kernel,
        grid=(t,),
        in_specs=[SMEM] + [pl.BlockSpec((1, r, n), lambda i: (i, 0, 0))] * count + [ANY] * len(kept),
        out_specs=[pl.BlockSpec((1, count, r, n), lambda i: (i + first, 0, 0, 0)), whole(8, 128)],
        out_shape=[jax.ShapeDtypeStruct((taps, count, r, n), F32), MARK],
        input_output_aliases={1 + count: 0} if kept else {},
        compiler_params=params(8),
        name="place_taps",
    )(where, *pieces, *kept)


def total_of(groups, token):
    total = sum(g[0].shape[0] for g in groups)
    r, n = groups[0][0].shape[-2:]
    ins = [x.reshape(x.shape[0], r, n) for g in groups for x in g]

    def kernel(*refs):
        at = row = 0
        for g in groups:
            t = g[0].shape[0]
            out = refs[at][...]
            for k in range(1, len(g)):
                out = out + refs[at + k][...]
            at += len(g)
            refs[-2][row : row + t] = out
            row += t
        refs[-1][...] = jnp.zeros((8, 128), F32)

    return pl.pallas_call(
        kernel,
        in_specs=[whole(*x.shape) for x in ins] + [whole(8, 128)] * len(token),
        out_specs=[whole(total, r, n), whole(8, 128)],
        out_shape=[jax.ShapeDtypeStruct((total, r, n), F32), MARK],
        compiler_params=params(8),
        cost_estimate=cost(0, 3 << 20),
        name="total_of",
    )(*ins, *token)


class Reduce:
    def __init__(self, send, keep, mark, way, where, extra=None):
        self.where = where
        self.extra = extra
        self.mark = mark
        self.way = way
        t, nz, rows, n = keep.shape
        ndp = lax.axis_size("dp")
        cut = (t, nz, ndp, rows // ndp, n)
        self.keep = keep.reshape(cut)
        self.got = swap(send, "blk", 1).reshape(cut)
        self.masks = far_masks(nz)
        self.first_way = {"x": [1], "y": [2], "both": [1, 2]}[way]

    def near(self, folded, masks):
        outs, kept, self.mark = folded
        self.sums = []
        for k, mask in enumerate(masks):
            self.sums += [outs[2 * k + 1], swap(outs[2 * k], "dp", mask)]
        return kept

    def first(self, token=(), hold=()):
        return self.near(fold_first(self.keep, self.got, self.way, self.where, token, hold, self.extra), self.first_way)

    def second(self, token=(), hold=()):
        return self.near(fold_second(self.sums, self.way, self.where, token, hold), [3 - m for m in self.first_way])


class Spread:
    def __init__(self, chains, token=()):
        self.where = chains[0].where
        self.masks = chains[0].masks
        more = chains[0].extra is not None
        folded = fold_far_first([c.sums for c in chains], self.masks, self.where, token, more)
        self.extra = folded[3] if more else None
        self.next(folded[:3], 0)

    def next(self, folded, step):
        send, keep, self.mark = folded
        self.sums = [keep, swap(send, "blk", 2 * self.masks[step])]

    def far(self, token=()):
        for step in range(1, len(self.masks)):
            self.next(fold_far(*self.sums, step, self.masks, self.where, token), step)


class Gather:
    def __init__(self, parts, token=()):
        self.where = parts[0].where
        out, self.mark = total_of([p.sums if isinstance(p, Spread) else [p] for p in parts], token)
        self.pieces = [out] + [swap(out, "dp", k) for k in range(1, lax.axis_size("dp"))]


def share_sum(local, where):
    nblk, rows, n = local.shape
    local = local.reshape(1, nblk // 2, 2, rows, n)
    pick = lambda c: lax.dynamic_index_in_dim(local, c, 2, keepdims=False)
    whole_sum = Reduce(pick(1 - where[0]), pick(where[0]), None, "x", where)
    whole_sum.first()
    whole_sum.second()
    out = Spread([whole_sum])
    out.far()
    return place(Gather([out]).pieces, where)[0]


def projector_spread(order, pre, gain, bias, embed_map, hidden_map, plain, normed_sums, crop_total):
    slots = pre.shape[0]
    crops = sum(p.crops for p in order)
    high = lax.Precision.HIGHEST
    embed_map = embed_map.astype(F32)
    raw = pre[:crops]
    sums = sum_all(jnp.stack([jnp.sum(raw, axis=0), jnp.sum(raw * raw, axis=0)]))
    mean = sums[0] / crop_total
    rstd = lax.rsqrt(sums[1] / crop_total - mean * mean + NORM_EPS)
    normed = (raw - mean) * rstd
    q = gain * normed + bias
    sig = jax.nn.sigmoid(q)
    hp = q * sig
    z = jnp.dot(hp, embed_map, precision=high)
    emb = z.shape[1]
    z = jnp.concatenate([z, pre[crops : crops + 1, :emb], jnp.zeros((slots - crops - 1, emb), F32)], axis=0)
    z, _, _ = gather_all(z)
    z = jnp.concatenate(z, axis=0)
    blocks = z.shape[0]
    pairs = z[:, crops, :64]
    z = z[:, :crops].reshape(blocks * crops, emb)
    zc = z - jnp.sum(z, axis=0) / crop_total
    cov = jnp.dot(zc.T, zc, precision=high) / crop_total
    white = jax.scipy.linalg.solve_triangular(jnp.linalg.cholesky(cov), jnp.eye(emb, dtype=F32), lower=True)
    w = jnp.dot(zc, white.T, precision=high)
    inv_len = lax.rsqrt(jnp.sum(w * w, axis=1, keepdims=True) + UNIT_EPS)
    u = w * inv_len
    slot = jnp.arange(crops, dtype=F32)
    ends = (pairs[:, :32, None] == slot).astype(F32) - (pairs[:, 32:, None] == slot).astype(F32)
    gap = jnp.einsum("bpc,bce->bpe", ends, u.reshape(blocks, crops, emb), precision=high)
    gu = 2.0 * jnp.einsum("bpc,bpe->bce", ends, gap, precision=high).reshape(blocks * crops, emb)
    gw = (gu - u * jnp.sum(u * gu, axis=1, keepdims=True)) * inv_len
    moment = jnp.dot(gw.T, w, precision=high)
    sym = jnp.tril(moment) + jnp.tril(moment, -1).T
    back = gw[:crops] - (jnp.sum(gw, axis=0) + jnp.dot(w[:crops], sym, precision=high)) / crop_total
    gz = jnp.dot(back, white, precision=high)
    gq = jnp.dot(gz, embed_map.T, precision=high) * (sig * (1.0 + q * (1.0 - sig)))
    sums = sum_all(jnp.stack([jnp.sum(gq, axis=0), jnp.sum(gq * normed, axis=0)]))
    gap = gain * rstd * (gq - sums[0] / crop_total - normed * (sums[1] / crop_total))
    ge = jnp.dot(gap, hidden_map.astype(F32).T, precision=high)
    area = jnp.concatenate([jnp.full((p.crops, 1), 1.0 / (p.side * p.side), F32) for p in order])
    share = jnp.pad(ge * area, ((0, slots - crops), (0, 0)))
    stats = jnp.stack([jnp.sum(share * plain, axis=0), jnp.sum(share * normed_sums, axis=0)])
    return hp, gap, gz, sums[1:2], sums[0:1], share, stats


def body(crops_seven, crops_six, crops_five, conv_in, gain_in, bias_in, conv_mid, gain_mid, bias_mid,
         conv_out, gain_out, bias_out, proj_hidden, gain_proj, bias_proj, proj_embed, pair_index):
    crops_in = (crops_seven, crops_six, crops_five)
    parts, order, slabs = layout([c.shape for c in crops_in])
    ndp = lax.axis_size("dp")
    nblk = lax.axis_size("blk")
    dp = lax.axis_index("dp")
    blk = lax.axis_index("blk")
    devices = ndp * nblk
    crops = sum(p.crops for p in parts)
    total = float(sum(p.crops * p.side * p.side for p in parts) * devices)
    crop_total = float(crops * devices)
    slots = 24
    width, chan = conv_in.shape
    hidden, emb = proj_embed.shape
    row = lambda v: v.reshape(1, -1)
    where = jnp.stack([blk % 2, dp, blk // 2]).astype(jnp.int32)
    first_crop = 0
    pair_slot = pair_index
    for p in parts:
        mine = (pair_index >= first_crop) & (pair_index < first_crop + p.crops)
        pair_slot = jnp.where(mine, pair_index - first_crop + p.slot, pair_slot)
        first_crop += p.crops
    pair_row = jnp.pad(
        jnp.concatenate([pair_slot[:, 0], pair_slot[:, 1]]).astype(F32), (0, hidden - 2 * pair_index.shape[0])
    )
    laid = [
        c if p.by_column else jnp.transpose(c, (1, 2, 0, 3)).reshape(p.slabs, 8, width) for c, p in zip(crops_in, parts)
    ]

    inputs, first_pre, sums = first_conv(parts, order, slabs, laid, conv_in)
    in_sums = sum_all(sums)
    hidden_one, second_pre, sums = middle_conv(
        order, first_pre, in_sums, total, row(gain_in), row(bias_in), conv_mid.reshape(9 * chan, chan)
    )
    mid_sums = sum_all(sums)
    hidden_two, third_pre, sums = last_conv(order, second_pre, mid_sums, total, row(gain_mid), row(bias_mid), conv_out)
    out_sums = sum_all(sums)
    gain_o, bias_o = row(gain_out), row(bias_out)
    pooled, pre = pool_embed(
        order, slots, third_pre, out_sums, total, gain_o, bias_o, inputs, proj_hidden, row(pair_row)
    )
    small = devices <= 32
    slopes = lambda *hold: slope_sums(
        order, slots, third_pre, out_sums, total, gain_o, bias_o, inputs, hold
    )
    if small:
        pre, number, (slope, plain, normed_sums) = gather_all(pre, slopes)
    else:
        slope, plain, normed_sums = slopes()
    middle = projector if small else projector_spread
    hp, gap, gz, gg_proj, gb_proj, share, sums = middle(
        order, pre, row(gain_proj), row(bias_proj), proj_embed, proj_hidden, plain, normed_sums, crop_total
    )
    out_back = sum_all(sums)
    grad_two, sums, local_out = last_back(
        order, slope, share, third_pre, out_sums, out_back, total, gain_o, conv_out,
        second_pre, mid_sums, row(gain_mid), row(bias_mid), hidden_two
    )
    pooled_all = lax.all_gather(pooled, ("dp", "blk"), axis=0) if small else pooled
    out_part = lax.psum_scatter(local_out, "blk", scatter_dimension=0, tiled=True)
    mid_back = sum_all(sums)
    grad_second, grad_one, sums = middle_back(
        order, grad_two, mid_back, total, second_pre, mid_sums, row(gain_mid), conv_mid.reshape(9, chan, chan),
        first_pre, in_sums, row(gain_in), row(bias_in), [mark_of(pooled_all)]
    )
    send, keep, core, mark = middle_weight(
        order, hidden_one, grad_second, where, nblk, (0, 5), [], [sum_core(sums)]
    )
    m0 = Reduce(send, keep, mark, "both", where)
    (near,) = m0.first(hold=[sum_near(core)])
    in_back = sum_stages(near, "blk", [[1 << k] for k in range(1, nblk.bit_length() - 1)])
    grad_first, send, keep, mark = first_back(
        order, grad_one, in_back, total, first_pre, in_sums, row(gain_in), inputs, where, nblk, []
    )
    i = Reduce(send, keep, mark, "both", where, out_part)
    m0.second([mark])
    m1 = Reduce(*middle_weight(order, hidden_one, grad_second, where, nblk, (5, 4), [m0.mark]), "both", where)
    i.first([m1.mark])
    far0 = Spread([m0], [i.mark])
    high = lax.Precision.HIGH
    if small:
        hidden_grad, embed_grad, mark = projector_weights(
            pooled_all, number, blk, gap, hp, gz, nblk, [far0.mark]
        )
    else:
        local = lax.dot_general(pooled[:crops], gap, (((0,), (0,)), ((), ())), precision=high)
        hidden_grad = share_sum(local.reshape(nblk, width // nblk, hidden), where)
        local = lax.dot_general(hp, gz, (((0,), (0,)), ((), ())), precision=high)
        embed_grad = share_sum(local.reshape(nblk, hidden // nblk, emb), where)
    m1.first([mark])
    far0.far([m1.mark])
    *grads, mark = input_grads(parts, order, slope, share, grad_first, conv_in, [far0.mark])
    grads = [
        g if p.by_column else jnp.transpose(g.reshape(p.side, p.side, 8, width), (2, 0, 1, 3))
        for g, p in zip(grads, parts)
    ]
    i.second([mark])
    m1.second([i.mark])
    early = Gather([far0], [m1.mark])
    last = Spread([i], [early.mark])
    far1 = Spread([m1], [last.mark])
    taps = m0.keep.shape[0] + m1.keep.shape[0]
    mid_grad, mark = place_taps(early.pieces, where, 0, taps)
    last.far([far1.mark, mark])
    far1.far([last.mark])
    middle = Gather([last, last.extra], [far1.mark])
    late = Gather([far1], [middle.mark])
    conv_in_grad, out_grad = place(middle.pieces, where, 4)
    conv_in_grad = conv_in_grad.reshape(width // nblk, chan)
    mid_grad, _ = place_taps(late.pieces, where, m0.keep.shape[0], taps, mid_grad)
    return (
        *grads,
        conv_in_grad,
        mid_grad.reshape(3, 3, chan // nblk, chan),
        out_grad,
        hidden_grad,
        embed_grad,
        in_back[1],
        in_back[0],
        mid_back[1],
        mid_back[0],
        out_back[1],
        out_back[0],
        gg_proj[0],
        gb_proj[0],
    )


def solution(mesh):
    from_both = ("dp", "blk")
    crop_spec = jax.sharding.PartitionSpec(from_both, None, None, None)
    spec = jax.sharding.PartitionSpec
    in_specs = (crop_spec,) * 3 + (spec(),) * 13 + (spec(from_both, None),)
    out_specs = (crop_spec,) * 3 + (
        spec("blk", None),
        spec(None, None, "blk", None),
        spec("blk", None),
        spec("blk", None),
        spec("blk", None),
    ) + (spec(),) * 8
    return jax.shard_map(body, mesh=mesh, in_specs=in_specs, out_specs=out_specs, check_vma=False)
```

```python
import jax
import jax.numpy as jnp
from jax import lax
from jax.experimental import pallas as pl
from jax.experimental.pallas import tpu as pltpu

F32 = jnp.float32
BF16 = jnp.bfloat16
NORM_EPS = 1e-05
UNIT_EPS = 1e-06
MIB = 1 << 20
ANY = pl.BlockSpec(memory_space=pl.ANY)
HBM = pl.BlockSpec(memory_space=pltpu.HBM)
SMEM = pl.BlockSpec(memory_space=pltpu.SMEM)
MARK = jax.ShapeDtypeStruct((8, 128), F32)


def params(mib):
    return pltpu.CompilerParams(vmem_limit_bytes=mib * MIB)


def cost(flops, moved, special=0):
    return pl.CostEstimate(flops=int(flops), bytes_accessed=int(moved), transcendentals=int(special))


class Part:
    def __init__(self, crops, side, first, slot):
        self.crops, self.side, self.first, self.slot = crops, side, first, slot
        self.by_column = crops != 8
        self.slabs = crops * side if self.by_column else side * side
        self.cut = slice(first, first + self.slabs)

    def sources(self, down, right):
        found = []
        for k in range(self.slabs):
            i, j = divmod(k, self.side)
            if self.by_column:
                i, j = j + down, 0
                there = 0 <= i < self.side
                found.append(k + down if there else None)
            else:
                i, j = i + down, j + right
                there = 0 <= i < self.side and 0 <= j < self.side
                found.append(i * self.side + j if there else None)
        return found


def layout(shapes):
    order = sorted(range(len(shapes)), key=lambda k: (shapes[k][0] != 8, -shapes[k][1]))
    parts = [None] * len(shapes)
    first = slot = 0
    for k in order:
        parts[k] = Part(shapes[k][0], shapes[k][1], first, slot)
        first += parts[k].slabs
        slot += shapes[k][0]
    return parts, [parts[k] for k in order], first


def sigmoid(q):
    return 0.5 * jnp.tanh(0.5 * q) + 0.5


def column_live(shape, side):
    return lax.broadcasted_iota(jnp.int32, shape, len(shape) - 2) < side


def live(parts, value):
    pieces = []
    for p in parts:
        piece = value[p.cut]
        if p.by_column:
            piece = jnp.where(column_live(piece.shape, p.side), piece, 0.0)
        pieces.append(piece)
    return jnp.concatenate(pieces, axis=0)


def crop_totals(parts, value, ref):
    for p in parts:
        piece = value[p.cut]
        if p.by_column:
            piece = piece.reshape(p.crops, p.side, 8, piece.shape[-1])
            total = jnp.sum(jnp.sum(piece, axis=1), axis=1)
        else:
            total = jnp.sum(piece, axis=0)
        ref[p.slot : p.slot + p.crops, :] = total


def spread(parts, ref):
    lanes = ref.shape[-1]
    pieces = []
    for p in parts:
        if p.by_column:
            for c in range(p.crops):
                row = ref[p.slot + c : p.slot + c + 1, :]
                pieces.append(jnp.broadcast_to(row[None], (p.side, 8, lanes)))
        else:
            pieces.append(jnp.broadcast_to(ref[p.slot : p.slot + 8, :][None], (p.slabs, 8, lanes)))
    return jnp.concatenate(pieces, axis=0)


def moments(st_ref, total):
    mean = st_ref[0:1, :] * (1.0 / total)
    var = st_ref[1:2, :] * (1.0 / total) - mean * mean
    return mean, lax.rsqrt(var + NORM_EPS)


def put_sums(ref, first, second):
    ref[0:1, :] = jnp.sum(first, axis=0, keepdims=True)
    ref[1:2, :] = jnp.sum(second, axis=0, keepdims=True)


def split3(x):
    h = x.astype(BF16)
    r = x - h.astype(F32)
    m = r.astype(BF16)
    return h, m, (r - m.astype(F32)).astype(BF16)


def split2(x):
    h = x.astype(BF16)
    return h, (x - h.astype(F32)).astype(BF16)


def mm(a, b):
    return jnp.dot(a, b, preferred_element_type=F32)


def mm_nt(a, b):
    return lax.dot_general(a, b, (((1,), (1,)), ((), ())), preferred_element_type=F32)


def mm_tn(a, b):
    return lax.dot_general(a, b, (((0,), (0,)), ((), ())), preferred_element_type=F32)


def whole(*shape):
    return pl.BlockSpec(shape, lambda *_: (0,) * len(shape))


def mark_of(x):
    return x[(0,) * (x.ndim - 2)][0:8, 0:128]


def lanes_of(block, *lead):
    return pl.BlockSpec((*lead, block), lambda j: (0,) * len(lead) + (j,))


def first_conv(parts, order, slabs, crops, conv_in):
    width, chan = conv_in.shape
    block = 512
    steps = width // block

    def kernel(*refs):
        x_refs, w_ref, xp_ref, a_ref, st_ref, scr = refs[:3], *refs[3:]
        j = pl.program_id(0)
        for p, ref in zip(parts, x_refs):
            x = ref[...].astype(F32)
            if p.by_column:
                x = x.reshape(p.slabs, p.side, block)
                x = jnp.concatenate([x, jnp.zeros((p.slabs, 8 - p.side, block), F32)], axis=1)
            scr[p.cut] = x
        xp_ref[...] = scr[...].reshape(slabs * 8, block).astype(BF16)
        out = mm(xp_ref[...], w_ref[...])

        @pl.when(j == 0)
        def _():
            a_ref[...] = out

        @pl.when(j > 0)
        def _():
            a_ref[...] += out

        @pl.when(j == steps - 1)
        def _():
            total = a_ref[...]
            put_sums(st_ref, total, total * total)

    rows = slabs * 8
    x_specs = [
        pl.BlockSpec((p.crops, p.side, p.side, block), lambda j: (0, 0, 0, j)) if p.by_column else lanes_of(block, p.slabs, 8)
        for p in parts
    ]
    return pl.pallas_call(
        kernel,
        grid=(steps,),
        in_specs=[*x_specs, pl.BlockSpec((block, chan), lambda j: (j, 0))],
        out_specs=[lanes_of(block, rows), whole(rows, chan), whole(2, chan)],
        out_shape=(
            jax.ShapeDtypeStruct((rows, width), BF16),
            jax.ShapeDtypeStruct((rows, chan), F32),
            jax.ShapeDtypeStruct((2, chan), F32),
        ),
        scratch_shapes=[pltpu.VMEM((slabs, 8, block), F32)],
        compiler_params=params(20),
        cost_estimate=cost(2 * rows * width * chan, 10 << 20),
        name="first_conv",
    )(*crops, conv_in)


def turn(order, chan, source, turned):
    for p in order:
        if p.by_column:
            value = source[p.cut].reshape(p.slabs * 8, chan)
            turned[0] = pltpu.roll(value, 1, 0).reshape(p.slabs, 8, chan)
            turned[1] = pltpu.roll(value, p.slabs * 8 - 1, 0).reshape(p.slabs, 8, chan)

def shifted(order, chan, source, turned, tap, forward):
    r, t = divmod(tap, 3)
    down, right = (r - 1, t - 1) if forward else (1 - r, 1 - t)
    pieces = []
    for p in order:
        found = p.sources(down, right)
        k = 0
        while k < p.slabs:
            end = k + 1
            if found[k] is None:
                while end < p.slabs and found[end] is None:
                    end += 1
                pieces.append(jnp.zeros((end - k, 8, chan), F32))
            else:
                while end < p.slabs and found[end] == found[k] + end - k:
                    end += 1
                at = found[k]
                if p.by_column and right:
                    pieces.append(turned[0 if right < 0 else 1, at : at + end - k])
                else:
                    pieces.append(source[p.first + at : p.first + at + end - k])
            k = end
    value = jnp.concatenate(pieces, axis=0)
    return value.reshape(value.shape[0] * 8, chan).astype(BF16)


def patch_columns(order, chan, source, turned, cat_ref, forward):
    turn(order, chan, source, turned)
    for tap in range(9):
        cat_ref[:, tap * chan : (tap + 1) * chan] = shifted(order, chan, source, turned, tap, forward)


def turned_shape(order, chan):
    return (2, max([p.slabs for p in order if p.by_column] + [1]), 8, chan)


def middle_conv(order, first_pre, sums, total, gain, bias, kernel_flat):
    rows, chan = first_pre.shape
    slabs = rows // 8

    def kernel(a_ref, st_ref, g_ref, b_ref, w_ref, y_ref, o_ref, so_ref, turned, cat_scr):
        mean, rstd = moments(st_ref, total)
        scale = g_ref[...] * rstd
        q = (a_ref[...] * scale + (b_ref[...] - mean * scale)).reshape(slabs, 8, chan)
        y_ref[...] = live(order, q * sigmoid(q))
        patch_columns(order, chan, y_ref, turned, cat_scr, True)
        out = live(order, mm(cat_scr[...], w_ref[...]).reshape(slabs, 8, chan)).reshape(rows, chan)
        o_ref[...] = out
        put_sums(so_ref, out, out * out)

    return pl.pallas_call(
        kernel,
        in_specs=[whole(rows, chan), whole(2, chan), whole(1, chan), whole(1, chan), whole(9 * chan, chan)],
        out_specs=[whole(slabs, 8, chan), whole(rows, chan), whole(2, chan)],
        out_shape=(
            jax.ShapeDtypeStruct((slabs, 8, chan), F32),
            jax.ShapeDtypeStruct((rows, chan), F32),
            jax.ShapeDtypeStruct((2, chan), F32),
        ),
        scratch_shapes=[
            pltpu.VMEM(turned_shape(order, chan), F32),
            pltpu.VMEM((rows, 9 * chan), BF16),
        ],
        compiler_params=params(24),
        cost_estimate=cost(18 * rows * chan * chan, 20 << 20),
        name="middle_conv",
    )(first_pre, sums, gain, bias, kernel_flat)


def last_conv(order, second_pre, sums, total, gain, bias, conv_out):
    rows, chan = second_pre.shape
    slabs = rows // 8
    width = conv_out.shape[1]
    block = 512

    def kernel(a_ref, st_ref, g_ref, b_ref, w_ref, y_ref, o_ref, so_ref):
        @pl.when(pl.program_id(0) == 0)
        def _():
            mean, rstd = moments(st_ref, total)
            scale = g_ref[...] * rstd
            q = (a_ref[...] * scale + (b_ref[...] - mean * scale)).reshape(slabs, 8, chan)
            y_ref[...] = live(order, q * sigmoid(q)).reshape(rows, chan).astype(BF16)

        out = mm(y_ref[...], w_ref[...])
        o_ref[...] = out
        put_sums(so_ref, out, out * out)

    return pl.pallas_call(
        kernel,
        grid=(width // block,),
        in_specs=[whole(rows, chan), whole(2, chan), whole(1, chan), whole(1, chan), lanes_of(block, chan)],
        out_specs=[whole(rows, chan), lanes_of(block, rows), lanes_of(block, 2)],
        out_shape=(
            jax.ShapeDtypeStruct((rows, chan), BF16),
            jax.ShapeDtypeStruct((rows, width), F32),
            jax.ShapeDtypeStruct((2, width), F32),
        ),
        compiler_params=params(16),
        cost_estimate=cost(2 * rows * width * chan, 12 << 20),
        name="last_conv",
    )(second_pre, sums, gain, bias, conv_out)


def pool_embed(order, slots, third_pre, sums, total, gain, bias, inputs, hidden_map, pair_row):
    rows, width = third_pre.shape
    slabs = rows // 8
    hidden = hidden_map.shape[1]
    crops = sum(p.crops for p in order)
    block = 512
    steps = width // block

    def kernel(a_ref, st_ref, g_ref, b_ref, x_ref, w_ref, p_ref, e_ref, ap_ref, scr, acc):
        j = pl.program_id(0)
        mean, rstd = moments(st_ref, total)
        scale = g_ref[...] * rstd
        shift = b_ref[...] - mean * scale
        r = x_ref[...].astype(F32) + (a_ref[...] * scale + shift)
        v = live(order, (r * sigmoid(r)).reshape(slabs, 8, block))
        scr[...] = jnp.zeros_like(scr)
        crop_totals(order, v, scr)
        for p in order:
            at = slice(p.slot, p.slot + p.crops)
            scr[at, :] = scr[at, :] * (1.0 / (p.side * p.side))
        e = scr[...]
        e_ref[...] = e[0:slots]
        h, m, l = split3(e)
        out = mm(jnp.concatenate([h, m, l], axis=0), w_ref[...])

        @pl.when(j == 0)
        def _():
            acc[...] = out

        @pl.when(j > 0)
        def _():
            acc[...] += out

        @pl.when(j == steps - 1)
        def _():
            ap_ref[...] = acc[0:slots] + acc[32 : 32 + slots] + acc[64 : 64 + slots]
            ap_ref[crops : crops + 1, :] = p_ref[...]

    return pl.pallas_call(
        kernel,
        grid=(steps,),
        in_specs=[
            lanes_of(block, rows), lanes_of(block, 2), lanes_of(block, 1), lanes_of(block, 1), lanes_of(block, rows),
            pl.BlockSpec((block, hidden), lambda j: (j, 0)), whole(1, hidden),
        ],
        out_specs=[lanes_of(block, slots), whole(slots, hidden)],
        out_shape=(jax.ShapeDtypeStruct((slots, width), F32), jax.ShapeDtypeStruct((slots, hidden), F32)),
        scratch_shapes=[pltpu.VMEM((32, block), F32), pltpu.VMEM((96, hidden), F32)],
        compiler_params=params(20),
        cost_estimate=cost(2 * 96 * width * hidden, 16 << 20, 2 * rows * width),
        name="pool_embed",
    )(third_pre, sums, gain, bias, inputs, hidden_map, pair_row)


def slope_sums(order, slots, third_pre, sums, total, gain, bias, inputs, hold=()):
    rows, width = third_pre.shape
    slabs = rows // 8
    block = 256

    def kernel(a_ref, st_ref, g_ref, b_ref, x_ref, *refs):
        s_ref, p_ref, t_ref = refs[len(hold) :][:3]
        for k in range(len(hold)):
            refs[len(hold) + 3 + k][...] = refs[k][...]
        mean, rstd = moments(st_ref, total)
        p_ref[...] = jnp.zeros_like(p_ref)
        t_ref[...] = jnp.zeros_like(t_ref)
        normed = (a_ref[...] - mean) * rstd
        r = x_ref[...].astype(F32) + (normed * g_ref[...] + b_ref[...])
        sig = sigmoid(r)
        v = live(order, (sig * (1.0 + r * (1.0 - sig))).reshape(slabs, 8, block))
        s_ref[...] = v.reshape(rows, block).astype(BF16)
        crop_totals(order, v, p_ref)
        crop_totals(order, v * normed.reshape(slabs, 8, block), t_ref)

    lane = lambda lead: lanes_of(block, lead)
    kept = [whole(*h.shape) for h in hold]
    return pl.pallas_call(
        kernel,
        grid=(width // block,),
        in_specs=[lane(rows), lane(2), lane(1), lane(1), lane(rows)] + kept,
        out_specs=[lane(rows), lane(slots), lane(slots)] + kept,
        out_shape=(
            jax.ShapeDtypeStruct((rows, width), BF16),
            jax.ShapeDtypeStruct((slots, width), F32),
            jax.ShapeDtypeStruct((slots, width), F32),
            *(jax.ShapeDtypeStruct(h.shape, F32) for h in hold),
        ),
        compiler_params=params(14),
        cost_estimate=cost(24 * rows * width, 8 * rows * width, 2 * rows * width),
        name="slope_sums",
    )(third_pre, sums, gain, bias, inputs, *hold)


def join(pieces, token):
    count = len(pieces)
    shape = pieces[0].shape

    def kernel(*refs):
        for k in range(count):
            refs[-1][k] = refs[k][...]

    return pl.pallas_call(
        kernel,
        in_specs=[whole(*shape)] * count + [whole(8, 128)] * len(token),
        out_specs=whole(count, *shape),
        out_shape=jax.ShapeDtypeStruct((count, *shape), F32),
        compiler_params=params(8),
        name="join",
    )(*pieces, *token)


def projector(order, pres, gain, bias, embed_map, hidden_map, plain, normed_sums, crop_total):
    held = [p.shape[0] for p in pres]
    blocks = sum(held)
    _, slots, hidden = pres[0].shape
    emb = embed_map.shape[1]
    width = hidden_map.shape[0]
    crops = sum(p.crops for p in order)
    rows_all = blocks * slots
    lanes = 256
    cols = hidden // lanes
    inv_total = 1.0 / crop_total
    group = 8
    half = 32

    def kernel(*refs):
        p_refs = refs[: len(held)]
        (g_ref, b_ref, we_ref, wh_ref, s1_ref, s2_ref, hp_ref, gap_ref, gz_ref, gg_ref, gb_ref, ge_ref, st_ref,
         n_scr, d_scr, z_scr, a_scr, i_scr, u_scr) = refs[len(held):]
        live_l = (lax.broadcasted_iota(jnp.int32, (blocks, slots, lanes), 1) < crops).reshape(rows_all, lanes)
        live_e = (lax.broadcasted_iota(jnp.int32, (blocks, slots, emb), 1) < crops).reshape(rows_all, emb)
        rstds = []
        for k in range(cols):
            at = slice(k * lanes, (k + 1) * lanes)
            raw = jnp.concatenate([ref[:, :, at].reshape(n * slots, lanes) for ref, n in zip(p_refs, held)], axis=0)
            raw = jnp.where(live_l, raw, 0.0)
            mean = jnp.sum(raw, axis=0, keepdims=True) * inv_total
            var = jnp.sum(raw * raw, axis=0, keepdims=True) * inv_total - mean * mean
            rstd = lax.rsqrt(var + NORM_EPS)
            rstds.append(rstd)
            normed = (raw - mean) * rstd
            q = normed * g_ref[:, at] + b_ref[:, at]
            sig = sigmoid(q)
            n_scr[:, at] = normed
            d_scr[:, at] = sig * (1.0 + q * (1.0 - sig))
            hp = jnp.where(live_l, q * sig, 0.0)
            hp_ref[:, at] = hp
            h, m = split2(hp)
            z = mm(h, we_ref[at, :]) + mm(m, we_ref[at, :])
            if k == 0:
                z_scr[...] = z
            else:
                z_scr[...] += z
        z = z_scr[...]
        mu = jnp.sum(z, axis=0, keepdims=True) * inv_total
        zc = jnp.where(live_e, z - mu, 0.0)
        zh, zm, zl = split3(zc)
        cat = jnp.concatenate([zh, zm, zl], axis=1)
        prod = mm_tn(cat, cat)
        cov = jnp.zeros((emb, emb), F32)
        for u in (2, 1, 0):
            for v in (2, 1, 0):
                cov = cov + prod[u * emb : (u + 1) * emb, v * emb : (v + 1) * emb]
        row_id = lax.broadcasted_iota(jnp.int32, (emb, emb), 0)
        col_id = lax.broadcasted_iota(jnp.int32, (emb, emb), 1)
        a_scr[...] = cov * inv_total
        i_scr[...] = jnp.where(row_id == col_id, 1.0, 0.0)

        def eliminate(step, carry):
            j = 4 * step
            a = a_scr[...]
            image = i_scr[...]
            at = [jnp.full((emb, emb), j + q, jnp.int32) for q in range(4)]
            lane = lambda row, q: jnp.take_along_axis(jnp.broadcast_to(row, (8, emb)), at[q][0:8], axis=1)[0:1]
            rows = [a_scr[pl.ds(j + p, 1), :] for p in range(4)]
            images = [i_scr[pl.ds(j + p, 1), :] for p in range(4)]
            entry = [[lane(rows[p], q) for q in range(4)] for p in range(4)]
            columns = [jnp.take_along_axis(a, at[q], axis=1) for q in range(4)]
            inverse = []
            for q in range(4):
                inverse.append(1.0 / entry[q][q])
                for p in range(q + 1, 4):
                    ratio = entry[p][q] * inverse[q]
                    rows[p] = rows[p] - ratio * rows[q]
                    images[p] = images[p] - ratio * images[q]
                    for c in range(q + 1, 4):
                        entry[p][c] = entry[p][c] - ratio * entry[q][c]
            for q in range(4):
                column = columns[q]
                for p in range(q):
                    column = column - columns[p] * entry[p][q]
                columns[q] = jnp.where(row_id > j + q, column * inverse[q], 0.0)
                a = a - columns[q] * rows[q]
                image = image - columns[q] * images[q]
            a_scr[...] = a
            i_scr[...] = image
            return carry

        lax.fori_loop(0, emb // 4, eliminate, 0)
        diag = jnp.sum(jnp.where(row_id == col_id, a_scr[...], 0.0), axis=1, keepdims=True)
        white = i_scr[...] * lax.rsqrt(diag)
        ph, pm, pq = split3(white)
        w = mm_nt(
            jnp.concatenate([zh, zh, zm, zh, zl, zm], axis=1),
            jnp.concatenate([ph, pm, ph, pq, ph, pm], axis=1),
        )
        inv_len = lax.rsqrt(jnp.sum(w * w, axis=1, keepdims=True) + UNIT_EPS)
        u = w * inv_len
        uh, um, ul = split3(u)
        ucat = jnp.concatenate([uh, um, ul], axis=1)
        slot_id = lax.broadcasted_iota(jnp.int32, (slots, emb), 0).astype(F32)
        lane_id = lax.broadcasted_iota(jnp.int32, (slots, emb), 1)
        size = group * slots
        own = lax.broadcasted_iota(jnp.int32, (group, slots, size), 0).reshape(size, size)
        other_lane = lax.broadcasted_iota(jnp.int32, (size, size), 1)
        other = jnp.zeros((size, size), jnp.int32)
        for k in range(1, group):
            other = other + jnp.where(other_lane >= k * slots, 1, 0)
        same = own == other
        pair_rows = [ref[b, crops : crops + 1, 0:emb] for ref, n in zip(p_refs, held) for b in range(n)]
        for k in range(blocks // group):
            ends = []
            for b in range(group):
                hit = jnp.where(slot_id == pair_rows[k * group + b], 1.0, 0.0)
                hit = hit - pltpu.roll(hit, emb - half, 1)
                ends.append(jnp.where(lane_id < half, hit, 0.0))
            ends = jnp.concatenate(ends, axis=0).astype(BF16)
            graph = jnp.where(same, mm_nt(ends, ends), 0.0).astype(BF16)
            at = slice(k * size, (k + 1) * size)
            gu = mm(graph, ucat[at])
            u_scr[at, :] = 2.0 * (gu[:, 0:emb] + (gu[:, emb : 2 * emb] + gu[:, 2 * emb : 3 * emb]))
        gu = u_scr[...]
        gw = (gu - u * jnp.sum(u * gu, axis=1, keepdims=True)) * inv_len
        g_col = jnp.sum(gw, axis=0, keepdims=True)
        wh, wm, _ = split3(w)
        gh, gm = split2(gw)
        prod = mm_tn(jnp.concatenate([gh, gm], axis=1), jnp.concatenate([wh, wm], axis=1))
        moment = (
            prod[emb:, emb:] + prod[0:emb, emb:] + prod[emb:, 0:emb] + prod[0:emb, 0:emb]
        )
        low = jnp.where(row_id >= col_id, moment, 0.0)
        strict = jnp.where(row_id > col_id, moment, 0.0)
        sym = (low + strict.T) * inv_total
        sh, sm = split2(sym)
        back = gw - g_col * inv_total - mm(
            jnp.concatenate([wh, wh, wm], axis=1), jnp.concatenate([sh, sm, sh], axis=0)
        )
        bh, bm = split2(back)
        gz = mm(jnp.concatenate([bh, bh, bm], axis=1), jnp.concatenate([ph, pm, ph], axis=0))
        gz = jnp.where(live_e, gz, 0.0)
        gz_ref[...] = gz
        zh2, zm2 = split2(gz)
        zcat = jnp.concatenate([zh2, zm2], axis=0)
        for k in range(cols):
            at = slice(k * lanes, (k + 1) * lanes)
            both = mm_nt(zcat, we_ref[at, :])
            gq = (both[0:rows_all] + both[rows_all:]) * d_scr[:, at]
            gb = jnp.sum(gq, axis=0, keepdims=True)
            gg = jnp.sum(gq * n_scr[:, at], axis=0, keepdims=True)
            gb_ref[:, at] = gb
            gg_ref[:, at] = gg
            gap = (g_ref[:, at] * rstds[k]) * (gq - gb * inv_total - n_scr[:, at] * (gg * inv_total))
            gap_ref[:, at] = jnp.where(live_l, gap, 0.0)
        mine = jnp.concatenate([gap_ref[0:slots, :], jnp.zeros((32 - slots, hidden), F32)], axis=0)
        h, m, l = split3(mine)
        out = mm_nt(jnp.concatenate([h, m, l], axis=0), wh_ref[...])
        ge_ref[...] = out[0:slots] + (out[32 : 32 + slots] + out[64 : 64 + slots])
        for p in order:
            at = slice(p.slot, p.slot + p.crops)
            ge_ref[at, :] = ge_ref[at, :] * (1.0 / (p.side * p.side))
        ge_ref[crops:, :] = jnp.zeros((slots - crops, width), F32)
        ge = ge_ref[...]
        put_sums(st_ref, ge * s1_ref[...], ge * s2_ref[...])

    return pl.pallas_call(
        kernel,
        out_shape=(
            jax.ShapeDtypeStruct((rows_all, hidden), F32),
            jax.ShapeDtypeStruct((rows_all, hidden), F32),
            jax.ShapeDtypeStruct((rows_all, emb), F32),
            jax.ShapeDtypeStruct((1, hidden), F32),
            jax.ShapeDtypeStruct((1, hidden), F32),
            jax.ShapeDtypeStruct((slots, width), F32),
            jax.ShapeDtypeStruct((2, width), F32),
        ),
        scratch_shapes=[
            pltpu.VMEM((rows_all, hidden), F32),
            pltpu.VMEM((rows_all, hidden), F32),
            pltpu.VMEM((rows_all, emb), F32),
            pltpu.VMEM((emb, emb), F32),
            pltpu.VMEM((emb, emb), F32),
            pltpu.VMEM((rows_all, emb), F32),
        ],
        compiler_params=params(30),
        cost_estimate=cost(10 << 30, 20 << 20),
        name="projector",
    )(*pres, gain, bias, embed_map, hidden_map, plain, normed_sums)


def projector_weights(pooled_all, order_of, blk, gap, hp, gz, nblk, token):
    blocks, slots, width = pooled_all.shape
    rows, hidden = gap.shape
    emb = gz.shape[1]
    own, own_hidden = width // nblk, hidden // nblk
    lanes = 256

    def kernel(at_ref, p_ref, ga_ref, hp_ref, gz_ref, *refs):
        o_ref, e_ref, mark, scr, high, low = refs[len(token) :]

        @pl.when(pl.program_id(0) == 0)
        def _():
            mark[...] = jnp.zeros_like(mark)
            for b in range(blocks):
                scr[b * slots : (b + 1) * slots, :] = p_ref[at_ref[1 + b]]
            h, m = split2(scr[...])
            high[...] = h
            low[...] = m
            hh, hm = split2(hp_ref[...])
            gh, gm = split2(gz_ref[...])
            e_ref[...] = mm_tn(hh, gh) + (mm_tn(hh, gm) + mm_tn(hm, gh))

        gh, gm = split2(ga_ref[...])
        o_ref[...] = mm_tn(high[...], gh) + (mm_tn(high[...], gm) + mm_tn(low[...], gh))

    return pl.pallas_call(
        kernel,
        grid_spec=pltpu.PrefetchScalarGridSpec(
            num_scalar_prefetch=1,
            grid=(hidden // lanes,),
            in_specs=[
                pl.BlockSpec((blocks, slots, own), lambda j, at: (0, 0, at[0])),
                pl.BlockSpec((rows, lanes), lambda j, at: (0, j)),
                pl.BlockSpec((rows, own_hidden), lambda j, at: (0, at[0])),
                pl.BlockSpec((rows, emb), lambda j, at: (0, 0)),
            ]
            + [pl.BlockSpec((8, 128), lambda j, at: (0, 0))] * len(token),
            out_specs=[
                pl.BlockSpec((own, lanes), lambda j, at: (0, j)),
                pl.BlockSpec((own_hidden, emb), lambda j, at: (0, 0)),
                pl.BlockSpec((8, 128), lambda j, at: (0, 0)),
            ],
            scratch_shapes=[pltpu.VMEM((rows, own), F32), pltpu.VMEM((rows, own), BF16), pltpu.VMEM((rows, own), BF16)],
        ),
        out_shape=(
            jax.ShapeDtypeStruct((own, hidden), F32),
            jax.ShapeDtypeStruct((own_hidden, emb), F32),
            MARK,
        ),
        compiler_params=params(58),
        cost_estimate=cost(2 << 30, 16 << 20),
        name="projector_weights",
    )(jnp.concatenate([blk[None], order_of]).astype(jnp.int32), pooled_all, gap, hp, gz, *token)


def halves(value, core, send, keep):
    for mine in range(2):

        @pl.when(core == mine)
        def _(mine=mine):
            send[...] = value(1 - mine)
            keep[...] = value(mine)


def last_back(order, slope, share, third_pre, sums, grad_sums, total, gain, conv_out,
              second_pre, mid_sums, mid_gain, mid_bias, hidden_two):
    rows, width = third_pre.shape
    slabs = rows // 8
    chan = second_pre.shape[1]
    block = 512
    steps = width // block

    def kernel(s_ref, e_ref, a_ref, st_ref, gs_ref, g_ref, w_ref, m_ref, ms_ref, mg_ref, mb_ref, y_ref,
               gq_ref, so_ref, weight_ref, ga_scr):
        j = pl.program_id(0)
        mean, rstd = moments(st_ref, total)
        lift = g_ref[...] * rstd
        slant = rstd * gs_ref[1:2, :] * (1.0 / total)
        base = gs_ref[0:1, :] * (1.0 / total) - mean * slant
        gr = s_ref[...].astype(F32) * spread(order, e_ref).reshape(rows, block)
        ga = lift * (gr - base - a_ref[...] * slant)
        ga_scr[...] = live(order, ga.reshape(slabs, 8, block)).reshape(rows, block).astype(BF16)
        out = mm_nt(ga_scr[...], w_ref[...])

        @pl.when(j == 0)
        def _():
            gq_ref[...] = out

        @pl.when(j > 0)
        def _():
            gq_ref[...] += out

        weight_ref[...] = mm_tn(y_ref[...], ga_scr[...])

        @pl.when(j == steps - 1)
        def _():
            mean2, rstd2 = moments(ms_ref, total)
            normed = (m_ref[...] - mean2) * rstd2
            q = normed * mg_ref[...] + mb_ref[...]
            sig = sigmoid(q)
            gq = gq_ref[...] * (sig * (1.0 + q * (1.0 - sig)))
            gq_ref[...] = gq
            put_sums(so_ref, gq, gq * normed)

    return pl.pallas_call(
        kernel,
        grid=(steps,),
        in_specs=[lanes_of(block, rows), lanes_of(block, share.shape[0]), lanes_of(block, rows), lanes_of(block, 2),
                  lanes_of(block, 2), lanes_of(block, 1), lanes_of(block, chan),
                  whole(rows, chan), whole(2, chan), whole(1, chan), whole(1, chan), whole(rows, chan)],
        out_specs=[whole(rows, chan), whole(2, chan), lanes_of(block, chan)],
        out_shape=(
            jax.ShapeDtypeStruct((rows, chan), F32),
            jax.ShapeDtypeStruct((2, chan), F32),
            jax.ShapeDtypeStruct((chan, width), F32),
        ),
        scratch_shapes=[pltpu.VMEM((rows, block), BF16)],
        compiler_params=params(40),
        cost_estimate=cost(4 * rows * width * chan, 24 << 20),
        name="last_back",
    )(slope, share, third_pre, sums, grad_sums, gain, conv_out, second_pre, mid_sums, mid_gain, mid_bias, hidden_two)


def middle_back(order, grad, grad_sums, total, second_pre, mid_sums, mid_gain, kernel_taps,
                first_pre, in_sums, in_gain, in_bias, token):
    rows, chan = grad.shape
    slabs = rows // 8

    def kernel(gq_ref, gs_ref, a_ref, ms_ref, mg_ref, w_ref, f_ref, is_ref, ig_ref, ib_ref, *refs):
        ga_ref, o_ref, so_ref, g_scr, turned, cat_scr, w_scr, sems = refs[len(token):]
        copies = [
            pltpu.make_async_copy(w_ref.at[k], w_scr.at[:, pl.ds(k * chan, chan)], sems.at[k]) for k in range(9)
        ]
        for copy in copies:
            copy.start()
        mean2, rstd2 = moments(ms_ref, total)
        lift = mg_ref[...] * rstd2
        slant = rstd2 * gs_ref[1:2, :] * (1.0 / total)
        base = gs_ref[0:1, :] * (1.0 / total) - mean2 * slant
        ga = live(order, (lift * (gq_ref[...] - base - a_ref[...] * slant)).reshape(slabs, 8, chan))
        g_scr[...] = ga
        ga_ref[...] = ga.reshape(rows, chan).astype(BF16)
        patch_columns(order, chan, g_scr, turned, cat_scr, False)
        for copy in copies:
            copy.wait()
        out = mm_nt(cat_scr[...], w_scr[...])
        mean1, rstd1 = moments(is_ref, total)
        normed = (f_ref[...] - mean1) * rstd1
        q = normed * ig_ref[...] + ib_ref[...]
        sig = sigmoid(q)
        gq = live(order, (out * (sig * (1.0 + q * (1.0 - sig)))).reshape(slabs, 8, chan)).reshape(rows, chan)
        o_ref[...] = gq
        put_sums(so_ref, gq, gq * normed)

    return pl.pallas_call(
        kernel,
        in_specs=[whole(rows, chan), whole(2, chan), whole(rows, chan), whole(2, chan), whole(1, chan), ANY,
                  whole(rows, chan), whole(2, chan), whole(1, chan), whole(1, chan)] + [whole(8, 128)] * len(token),
        out_specs=[whole(rows, chan), whole(rows, chan), whole(2, chan)],
        out_shape=(
            jax.ShapeDtypeStruct((rows, chan), BF16),
            jax.ShapeDtypeStruct((rows, chan), F32),
            jax.ShapeDtypeStruct((2, chan), F32),
        ),
        scratch_shapes=[
            pltpu.VMEM((slabs, 8, chan), F32),
            pltpu.VMEM(turned_shape(order, chan), F32),
            pltpu.VMEM((rows, 9 * chan), BF16),
            pltpu.VMEM((chan, 9 * chan), BF16),
            pltpu.SemaphoreType.DMA((9,)),
        ],
        compiler_params=params(28),
        cost_estimate=cost(18 * rows * chan * chan, 20 << 20),
        name="middle_back",
    )(grad, grad_sums, second_pre, mid_sums, mid_gain, kernel_taps, first_pre, in_sums, in_gain, in_bias, *token)


def middle_weight(order, hidden_one, grad, where, nblk, taps, token, hold=()):
    rows, chan = grad.shape
    slabs = rows // 8
    start, count = taps
    own = chan // nblk

    def kernel(at_ref, y_ref, g_ref, *refs):
        send_ref, keep_ref = refs[len(hold) + len(token) :][:2]
        mark, turned, lhs = refs[-3:]
        mark[...] = jnp.zeros_like(mark)
        k = pl.program_id(0)

        @pl.when(k == 0)
        def _():
            turn(order, chan, y_ref, turned)

        for tap in range(count):

            @pl.when(k == tap)
            def _(tap=tap):
                lhs[...] = shifted(order, chan, y_ref, turned, start + tap, True)

        weight = mm_tn(lhs[...], g_ref[...]).reshape(1, nblk // 2, 2, own, chan)
        halves(lambda c: weight[:, :, c], at_ref[0], send_ref, keep_ref)
        if hold:
            refs[-4][...] = refs[0][...]

    half = pl.BlockSpec((1, nblk // 2, own, chan), lambda k: (k, 0, 0, 0))
    kept = [whole(*h.shape) for h in hold]
    return pl.pallas_call(
        kernel,
        grid=(count,),
        in_specs=[SMEM, whole(slabs, 8, chan), whole(rows, chan)] + kept + [whole(8, 128)] * len(token),
        out_specs=[half, half] + kept + [whole(8, 128)],
        out_shape=(jax.ShapeDtypeStruct((count, nblk // 2, own, chan), F32),) * 2
        + tuple(jax.ShapeDtypeStruct(h.shape, F32) for h in hold)
        + (MARK,),
        scratch_shapes=[pltpu.VMEM(turned_shape(order, chan), F32), pltpu.VMEM((rows, chan), BF16)],
        compiler_params=params(14),
        cost_estimate=cost(2 * rows * chan * chan * count, 12 << 20),
        name="middle_weight",
    )(where, hidden_one, grad, *hold, *token)


def first_back(order, grad, grad_sums, total, first_pre, in_sums, in_gain, inputs, where, nblk, token):
    rows, chan = grad.shape
    slabs = rows // 8
    width = inputs.shape[1]
    own = width // nblk
    each = 2 * own
    merge = max(1, 512 // each)
    units = 4

    def kernel(at_ref, gq_ref, gs_ref, f_ref, is_ref, ig_ref, x_ref, *refs):
        ga_ref, send_ref, keep_ref, mark = refs[len(token):]
        mark[...] = jnp.zeros_like(mark)

        @pl.when(pl.program_id(0) == 0)
        def _():
            mean1, rstd1 = moments(is_ref, total)
            lift = ig_ref[...] * rstd1
            slant = rstd1 * gs_ref[1:2, :] * (1.0 / total)
            base = gs_ref[0:1, :] * (1.0 / total) - mean1 * slant
            ga = lift * (gq_ref[...] - base - f_ref[...] * slant)
            ga_ref[...] = live(order, ga.reshape(slabs, 8, chan)).reshape(rows, chan).astype(BF16)

        weight = mm_tn(x_ref[...], ga_ref[...]).reshape(merge, 2, units, own // units, chan)
        halves(lambda c: jnp.swapaxes(weight[:, c], 0, 1), at_ref[0], send_ref, keep_ref)

    half = pl.BlockSpec((units, merge, own // units, chan), lambda j: (0, j, 0, 0))
    return pl.pallas_call(
        kernel,
        grid=(width // (each * merge),),
        in_specs=[SMEM, whole(rows, chan), whole(2, chan), whole(rows, chan), whole(2, chan), whole(1, chan),
                  lanes_of(each * merge, rows)] + [whole(8, 128)] * len(token),
        out_specs=[whole(rows, chan), half, half, whole(8, 128)],
        out_shape=(
            jax.ShapeDtypeStruct((rows, chan), BF16),
            jax.ShapeDtypeStruct((units, nblk // 2, own // units, chan), F32),
            jax.ShapeDtypeStruct((units, nblk // 2, own // units, chan), F32),
            MARK,
        ),
        compiler_params=params(16),
        cost_estimate=cost(2 * rows * width * chan, 10 << 20),
        name="first_back",
    )(where, grad, grad_sums, first_pre, in_sums, in_gain, inputs, *token)


def input_grads(parts, order, slope, share, grad_first, conv_in, token):
    rows, width = slope.shape
    slabs = rows // 8
    chan = grad_first.shape[1]
    block = 512

    def kernel(s_ref, e_ref, g_ref, w_ref, *refs):
        gr = s_ref[...].astype(F32) * spread(order, e_ref).reshape(rows, block)
        gx = (gr + mm_nt(g_ref[...], w_ref[...])).reshape(slabs, 8, block)
        refs[-1][...] = jnp.zeros((8, 128), F32)
        for p, ref in zip(parts, refs[-4:-1]):
            piece = gx[p.cut]
            if p.by_column:
                ref[...] = piece.reshape(p.crops, p.side, 8, block)[:, :, 0 : p.side, :]
            else:
                ref[...] = piece

    out_specs = []
    out_shape = []
    for p in parts:
        if p.by_column:
            out_specs.append(pl.BlockSpec((p.crops, p.side, p.side, block), lambda j: (0, 0, 0, j)))
            out_shape.append(jax.ShapeDtypeStruct((p.crops, p.side, p.side, width), F32))
        else:
            out_specs.append(lanes_of(block, p.slabs, 8))
            out_shape.append(jax.ShapeDtypeStruct((p.slabs, 8, width), F32))
    return pl.pallas_call(
        kernel,
        grid=(width // block,),
        in_specs=[lanes_of(block, rows), lanes_of(block, share.shape[0]), whole(rows, chan),
                  pl.BlockSpec((block, chan), lambda j: (j, 0))] + [whole(8, 128)] * len(token),
        out_specs=out_specs + [whole(8, 128)],
        out_shape=(*out_shape, MARK),
        compiler_params=params(18),
        cost_estimate=cost(2 * rows * width * chan, 16 << 20),
        name="input_grads",
    )(slope, share, grad_first, conv_in, *token)


def masks_of(size, lowest=1):
    stages = []
    bit = lowest
    while bit < size:
        if 2 * bit < size:
            stages.append([bit, 2 * bit, 3 * bit])
            bit = 4 * bit
        else:
            stages.append([bit])
            bit = 2 * bit
    return stages


def swap(x, axis, mask):
    size = lax.axis_size(axis)
    return lax.ppermute(x, axis, [(i, i ^ mask) for i in range(size)])


def sum_stages(x, axis, stages):
    for masks in stages:
        got = [swap(x, axis, m) for m in masks]
        for g in got:
            x = x + g
    return x


def sum_core(x):
    return sum_stages(x, "blk", [[1]])


def sum_near(x):
    return sum_stages(x, "dp", masks_of(lax.axis_size("dp")))


def sum_far(x):
    return sum_stages(x, "blk", masks_of(lax.axis_size("blk"), 2))


def sum_all(x):
    return sum_far(sum_near(sum_core(x)))


def gather_all(x, between=None):
    dp = lax.axis_index("dp")
    blk = lax.axis_index("blk")
    nblk = lax.axis_size("blk")
    ndp = lax.axis_size("dp")
    joined = x[None]
    where = [0]
    for masks in masks_of(nblk, 2):
        joined = join([joined] + [swap(joined, "blk", m) for m in masks], []).reshape(-1, *x.shape)
        where = where + [w ^ m for m in masks for w in where]
    rows = [joined] + [swap(joined, "dp", k) for k in range(1, ndp)]
    extra = ()
    if between is not None:
        *extra, rows[0] = between(joined)
    rows += [swap(r, "blk", 1) for r in rows]
    number = [
        (dp ^ k) * nblk + (blk ^ (w ^ c)) for c in range(2) for k in range(ndp) for w in where
    ]
    return rows, jnp.stack(number), extra


def fold(kernel, count, where, ins, outs, token, hold, name):
    ins_n, outs_n, hold_n = len(ins), len(outs), len(hold)

    def whole_kernel(at_ref, *refs):
        kernel(at_ref, refs[:ins_n], refs[ins_n + hold_n + len(token) :][:outs_n])
        for k in range(hold_n):
            refs[len(refs) - 1 - hold_n + k][...] = refs[ins_n + k][...]
        refs[-1][...] = jnp.zeros((8, 128), F32)

    def unit(shape):
        if len(shape) == 3:
            return pl.BlockSpec((*shape[:2], shape[2] // count), lambda i: (0, 0, i))
        return pl.BlockSpec((1, *shape[1:]), lambda i: (i,) + (0,) * (len(shape) - 1))

    kept = [whole(*h.shape) for h in hold]
    result = pl.pallas_call(
        whole_kernel,
        grid=(count,),
        in_specs=[SMEM] + [unit(x.shape) for x in ins] + kept + [whole(8, 128)] * len(token),
        out_specs=[unit(x) for x in outs] + kept + [whole(8, 128)],
        out_shape=[jax.ShapeDtypeStruct(x, F32) for x in outs] + [jax.ShapeDtypeStruct(h.shape, F32) for h in hold] + [MARK],
        compiler_params=params(12),
        cost_estimate=cost(0, 8 << 20),
        name=name,
    )(where, *ins, *hold, *token)
    return result[:outs_n], result[outs_n:-1], result[-1]


def fold_first(keep, got, way, where, token, hold, extra=None):
    t, nz, _, r, n = keep.shape
    h = r // 2 if way == "both" else r
    ways = {"x": [0], "y": [1], "both": [0, 1]}[way]
    more = 0 if extra is None else 1

    def kernel(at_ref, ins, outs):
        x = at_ref[1] & 1
        y = at_ref[1] >> 1
        for k, w in enumerate(ways):
            rows = slice(k * h, k * h + h)
            for o in range(2):
                for out, q in (
                    (outs[2 * k], 2 * (1 - y) + o if w else 2 * o + 1 - x),
                    (outs[2 * k + 1], 2 * y + o if w else 2 * o + x),
                ):
                    out[0, 0:nz, o] = ins[0][0, :, q, rows, :] + ins[1][0, :, q, rows, :]
                    if more:
                        out[0, nz, o] = ins[2][q, rows, :]

    ins = [keep, got] + ([extra.reshape(4, r, t * n)] if more else [])
    return fold(kernel, t, where, ins, [(t, nz + more, 2, h, n)] * (2 * len(ways)), token, hold, "fold_first")


def fold_second(sums, way, where, token, hold):
    t, nz, _, h, n = sums[0].shape
    ways = {"x": [0], "y": [1], "both": [0, 1]}[way]

    def kernel(at_ref, ins, outs):
        for k, w in enumerate(ways):
            at = at_ref[1] & 1 if w else at_ref[1] >> 1
            add = lambda q: ins[2 * k][0, :, q] + ins[2 * k + 1][0, :, q]
            outs[2 * k][0] = add(1 - at)
            outs[2 * k + 1][0] = add(at)

    return fold(kernel, t, where, sums, [(t, nz, h, n)] * len(sums), token, hold, "fold_second")


def far_masks(nz):
    if nz == 4:
        return [1, 3]
    return [1 << k for k in range(nz.bit_length() - 1)]


def span(masks):
    offsets = [0]
    for m in masks:
        offsets = offsets + [o ^ m for o in offsets]
    return offsets


def fold_far_first(chains, masks, where, token, more):
    rest = span(masks[1:])
    ins = [x for chain in chains for x in chain]
    full = len(chains[0]) // 2 * chains[0][0].shape[2]
    n = ins[0].shape[-1]
    total = sum(chain[0].shape[0] for chain in chains)

    def kernel(at_ref, *refs):
        outs = refs[len(ins) + len(token) :]
        send, keep, mark = outs[:3]
        mark[...] = jnp.zeros_like(mark)
        first = at = 0
        for chain in chains:
            t, nz, h, _ = chain[0].shape
            for w in range(len(chain) // 2):
                a, b = refs[at : at + 2]
                at += 2
                rows = slice(w * h, w * h + h)
                for k, o in enumerate(rest):
                    send[first : first + t, k, rows, :] = a[:, at_ref[2] ^ o ^ masks[0]] + b[:, at_ref[2] ^ o ^ masks[0]]
                    keep[first : first + t, k, rows, :] = a[:, at_ref[2] ^ o] + b[:, at_ref[2] ^ o]
                if more:
                    outs[3][first : first + t, rows, :] = a[:, nz - 1] + b[:, nz - 1]
            first += t

    shape = (total, len(rest), full, n)
    whole_shape = [(total, full, n)] if more else []
    return pl.pallas_call(
        kernel,
        in_specs=[SMEM] + [whole(*x.shape) for x in ins] + [whole(8, 128)] * len(token),
        out_specs=[whole(*shape)] * 2 + [whole(8, 128)] + [whole(*x) for x in whole_shape],
        out_shape=[jax.ShapeDtypeStruct(shape, F32)] * 2 + [MARK] + [jax.ShapeDtypeStruct(x, F32) for x in whole_shape],
        compiler_params=params(14),
        cost_estimate=cost(0, 8 << 20),
        name="fold_far_first",
    )(where, *ins, *token)


def fold_far(keep, got, step, masks, where, token):
    rest = span(masks[step + 1 :])
    before = span(masks[step:])
    t, _, r, n = keep.shape

    def kernel(at_ref, a, b, *refs):
        send, stay, mark = refs[-3:]
        mark[...] = jnp.zeros_like(mark)
        for k, o in enumerate(rest):
            for out, offset in ((send, o ^ masks[step]), (stay, o)):
                out[:, k] = a[:, before.index(offset)] + b[:, before.index(offset)]

    shape = (t, len(rest), r, n)
    return pl.pallas_call(
        kernel,
        in_specs=[SMEM] + [whole(*keep.shape)] * 2 + [whole(8, 128)] * len(token),
        out_specs=[whole(*shape)] * 2 + [whole(8, 128)],
        out_shape=[jax.ShapeDtypeStruct(shape, F32)] * 2 + [MARK],
        compiler_params=params(12),
        cost_estimate=cost(0, 8 << 20),
        name="fold_far",
    )(where, keep, got, *token)


def place(pieces, where, side=0):
    t, r, n = pieces[0].shape
    count = len(pieces)
    rest = t - side

    def kernel(at_ref, *refs):
        for k in range(count):
            to = at_ref[1] ^ k
            refs[count][:, to] = refs[k][0:rest]
            for u in range(side):
                refs[-1][to, :, u * n : (u + 1) * n] = refs[k][rest + u]

    shapes = [(rest, count, r, n)] + ([(count, r, side * n)] if side else [])
    out = pl.pallas_call(
        kernel,
        in_specs=[SMEM] + [whole(t, r, n)] * count,
        out_specs=[whole(*x) for x in shapes],
        out_shape=[jax.ShapeDtypeStruct(x, F32) for x in shapes],
        compiler_params=params(12),
        name="place",
    )(where, *pieces)
    first = out[0].reshape(rest, count * r, n)
    return (first, out[1].reshape(count * r, side * n)) if side else first


def place_taps(pieces, where, first, taps, before=None):
    t, r, n = pieces[0].shape
    count = len(pieces)

    def kernel(at_ref, *refs):
        for k in range(count):
            refs[-2][0, at_ref[1] ^ k] = refs[k][0]
        refs[-1][...] = jnp.zeros((8, 128), F32)

    kept = [] if before is None else [before]
    return pl.pallas_call(
        kernel,
        grid=(t,),
        in_specs=[SMEM] + [pl.BlockSpec((1, r, n), lambda i: (i, 0, 0))] * count + [ANY] * len(kept),
        out_specs=[pl.BlockSpec((1, count, r, n), lambda i: (i + first, 0, 0, 0)), whole(8, 128)],
        out_shape=[jax.ShapeDtypeStruct((taps, count, r, n), F32), MARK],
        input_output_aliases={1 + count: 0} if kept else {},
        compiler_params=params(8),
        name="place_taps",
    )(where, *pieces, *kept)


def total_of(groups, token):
    total = sum(g[0].shape[0] for g in groups)
    r, n = groups[0][0].shape[-2:]
    ins = [x.reshape(x.shape[0], r, n) for g in groups for x in g]

    def kernel(*refs):
        at = row = 0
        for g in groups:
            t = g[0].shape[0]
            out = refs[at][...]
            for k in range(1, len(g)):
                out = out + refs[at + k][...]
            at += len(g)
            refs[-2][row : row + t] = out
            row += t
        refs[-1][...] = jnp.zeros((8, 128), F32)

    return pl.pallas_call(
        kernel,
        in_specs=[whole(*x.shape) for x in ins] + [whole(8, 128)] * len(token),
        out_specs=[whole(total, r, n), whole(8, 128)],
        out_shape=[jax.ShapeDtypeStruct((total, r, n), F32), MARK],
        compiler_params=params(8),
        cost_estimate=cost(0, 3 << 20),
        name="total_of",
    )(*ins, *token)


class Reduce:
    def __init__(self, send, keep, mark, way, where, extra=None):
        self.where = where
        self.extra = extra
        self.mark = mark
        self.way = way
        t, nz, rows, n = keep.shape
        ndp = lax.axis_size("dp")
        cut = (t, nz, ndp, rows // ndp, n)
        self.keep = keep.reshape(cut)
        self.got = swap(send, "blk", 1).reshape(cut)
        self.masks = far_masks(nz)
        self.first_way = {"x": [1], "y": [2], "both": [1, 2]}[way]

    def near(self, folded, masks):
        outs, kept, self.mark = folded
        self.sums = []
        for k, mask in enumerate(masks):
            self.sums += [outs[2 * k + 1], swap(outs[2 * k], "dp", mask)]
        return kept

    def first(self, token=(), hold=()):
        return self.near(fold_first(self.keep, self.got, self.way, self.where, token, hold, self.extra), self.first_way)

    def second(self, token=(), hold=()):
        return self.near(fold_second(self.sums, self.way, self.where, token, hold), [3 - m for m in self.first_way])


class Spread:
    def __init__(self, chains, token=()):
        self.where = chains[0].where
        self.masks = chains[0].masks
        more = chains[0].extra is not None
        folded = fold_far_first([c.sums for c in chains], self.masks, self.where, token, more)
        self.extra = folded[3] if more else None
        self.next(folded[:3], 0)

    def next(self, folded, step):
        send, keep, self.mark = folded
        self.sums = [keep, swap(send, "blk", 2 * self.masks[step])]

    def far(self, token=()):
        for step in range(1, len(self.masks)):
            self.next(fold_far(*self.sums, step, self.masks, self.where, token), step)


class Gather:
    def __init__(self, parts, token=()):
        self.where = parts[0].where
        out, self.mark = total_of([p.sums if isinstance(p, Spread) else [p] for p in parts], token)
        self.pieces = [out] + [swap(out, "dp", k) for k in range(1, lax.axis_size("dp"))]


def share_sum(local, where):
    nblk, rows, n = local.shape
    local = local.reshape(1, nblk // 2, 2, rows, n)
    pick = lambda c: lax.dynamic_index_in_dim(local, c, 2, keepdims=False)
    whole_sum = Reduce(pick(1 - where[0]), pick(where[0]), None, "x", where)
    whole_sum.first()
    whole_sum.second()
    out = Spread([whole_sum])
    out.far()
    return place(Gather([out]).pieces, where)[0]


def projector_spread(order, pre, gain, bias, embed_map, hidden_map, plain, normed_sums, crop_total):
    slots = pre.shape[0]
    crops = sum(p.crops for p in order)
    high = lax.Precision.HIGHEST
    embed_map = embed_map.astype(F32)
    raw = pre[:crops]
    sums = sum_all(jnp.stack([jnp.sum(raw, axis=0), jnp.sum(raw * raw, axis=0)]))
    mean = sums[0] / crop_total
    rstd = lax.rsqrt(sums[1] / crop_total - mean * mean + NORM_EPS)
    normed = (raw - mean) * rstd
    q = gain * normed + bias
    sig = jax.nn.sigmoid(q)
    hp = q * sig
    z = jnp.dot(hp, embed_map, precision=high)
    emb = z.shape[1]
    z = jnp.concatenate([z, pre[crops : crops + 1, :emb], jnp.zeros((slots - crops - 1, emb), F32)], axis=0)
    z, _, _ = gather_all(z)
    z = jnp.concatenate(z, axis=0)
    blocks = z.shape[0]
    pairs = z[:, crops, :64]
    z = z[:, :crops].reshape(blocks * crops, emb)
    zc = z - jnp.sum(z, axis=0) / crop_total
    cov = jnp.dot(zc.T, zc, precision=high) / crop_total
    white = jax.scipy.linalg.solve_triangular(jnp.linalg.cholesky(cov), jnp.eye(emb, dtype=F32), lower=True)
    w = jnp.dot(zc, white.T, precision=high)
    inv_len = lax.rsqrt(jnp.sum(w * w, axis=1, keepdims=True) + UNIT_EPS)
    u = w * inv_len
    slot = jnp.arange(crops, dtype=F32)
    ends = (pairs[:, :32, None] == slot).astype(F32) - (pairs[:, 32:, None] == slot).astype(F32)
    gap = jnp.einsum("bpc,bce->bpe", ends, u.reshape(blocks, crops, emb), precision=high)
    gu = 2.0 * jnp.einsum("bpc,bpe->bce", ends, gap, precision=high).reshape(blocks * crops, emb)
    gw = (gu - u * jnp.sum(u * gu, axis=1, keepdims=True)) * inv_len
    moment = jnp.dot(gw.T, w, precision=high)
    sym = jnp.tril(moment) + jnp.tril(moment, -1).T
    back = gw[:crops] - (jnp.sum(gw, axis=0) + jnp.dot(w[:crops], sym, precision=high)) / crop_total
    gz = jnp.dot(back, white, precision=high)
    gq = jnp.dot(gz, embed_map.T, precision=high) * (sig * (1.0 + q * (1.0 - sig)))
    sums = sum_all(jnp.stack([jnp.sum(gq, axis=0), jnp.sum(gq * normed, axis=0)]))
    gap = gain * rstd * (gq - sums[0] / crop_total - normed * (sums[1] / crop_total))
    ge = jnp.dot(gap, hidden_map.astype(F32).T, precision=high)
    area = jnp.concatenate([jnp.full((p.crops, 1), 1.0 / (p.side * p.side), F32) for p in order])
    share = jnp.pad(ge * area, ((0, slots - crops), (0, 0)))
    stats = jnp.stack([jnp.sum(share * plain, axis=0), jnp.sum(share * normed_sums, axis=0)])
    return hp, gap, gz, sums[1:2], sums[0:1], share, stats


def body(crops_seven, crops_six, crops_five, conv_in, gain_in, bias_in, conv_mid, gain_mid, bias_mid,
         conv_out, gain_out, bias_out, proj_hidden, gain_proj, bias_proj, proj_embed, pair_index):
    crops_in = (crops_seven, crops_six, crops_five)
    parts, order, slabs = layout([c.shape for c in crops_in])
    ndp = lax.axis_size("dp")
    nblk = lax.axis_size("blk")
    dp = lax.axis_index("dp")
    blk = lax.axis_index("blk")
    devices = ndp * nblk
    crops = sum(p.crops for p in parts)
    total = float(sum(p.crops * p.side * p.side for p in parts) * devices)
    crop_total = float(crops * devices)
    slots = 24
    width, chan = conv_in.shape
    hidden, emb = proj_embed.shape
    row = lambda v: v.reshape(1, -1)
    where = jnp.stack([blk % 2, dp, blk // 2]).astype(jnp.int32)
    first_crop = 0
    pair_slot = pair_index
    for p in parts:
        mine = (pair_index >= first_crop) & (pair_index < first_crop + p.crops)
        pair_slot = jnp.where(mine, pair_index - first_crop + p.slot, pair_slot)
        first_crop += p.crops
    pair_row = jnp.pad(
        jnp.concatenate([pair_slot[:, 0], pair_slot[:, 1]]).astype(F32), (0, hidden - 2 * pair_index.shape[0])
    )
    laid = [
        c if p.by_column else jnp.transpose(c, (1, 2, 0, 3)).reshape(p.slabs, 8, width) for c, p in zip(crops_in, parts)
    ]

    inputs, first_pre, sums = first_conv(parts, order, slabs, laid, conv_in)
    in_sums = sum_all(sums)
    hidden_one, second_pre, sums = middle_conv(
        order, first_pre, in_sums, total, row(gain_in), row(bias_in), conv_mid.reshape(9 * chan, chan)
    )
    mid_sums = sum_all(sums)
    hidden_two, third_pre, sums = last_conv(order, second_pre, mid_sums, total, row(gain_mid), row(bias_mid), conv_out)
    out_sums = sum_all(sums)
    gain_o, bias_o = row(gain_out), row(bias_out)
    pooled, pre = pool_embed(
        order, slots, third_pre, out_sums, total, gain_o, bias_o, inputs, proj_hidden, row(pair_row)
    )
    small = devices <= 32
    slopes = lambda *hold: slope_sums(
        order, slots, third_pre, out_sums, total, gain_o, bias_o, inputs, hold
    )
    if small:
        pre, number, (slope, plain, normed_sums) = gather_all(pre, slopes)
    else:
        slope, plain, normed_sums = slopes()
    middle = projector if small else projector_spread
    hp, gap, gz, gg_proj, gb_proj, share, sums = middle(
        order, pre, row(gain_proj), row(bias_proj), proj_embed, proj_hidden, plain, normed_sums, crop_total
    )
    out_back = sum_all(sums)
    grad_two, sums, local_out = last_back(
        order, slope, share, third_pre, out_sums, out_back, total, gain_o, conv_out,
        second_pre, mid_sums, row(gain_mid), row(bias_mid), hidden_two
    )
    pooled_all = lax.all_gather(pooled, ("dp", "blk"), axis=0) if small else pooled
    out_part = lax.psum_scatter(local_out, "blk", scatter_dimension=0, tiled=True)
    mid_back = sum_all(sums)
    grad_second, grad_one, sums = middle_back(
        order, grad_two, mid_back, total, second_pre, mid_sums, row(gain_mid), conv_mid.reshape(9, chan, chan),
        first_pre, in_sums, row(gain_in), row(bias_in), [mark_of(pooled_all)]
    )
    send, keep, core, mark = middle_weight(
        order, hidden_one, grad_second, where, nblk, (0, 5), [], [sum_core(sums)]
    )
    m0 = Reduce(send, keep, mark, "both", where)
    (near,) = m0.first(hold=[sum_near(core)])
    in_back = sum_stages(near, "blk", [[1 << k] for k in range(1, nblk.bit_length() - 1)])
    grad_first, send, keep, mark = first_back(
        order, grad_one, in_back, total, first_pre, in_sums, row(gain_in), inputs, where, nblk, []
    )
    i = Reduce(send, keep, mark, "both", where, out_part)
    m0.second([mark])
    m1 = Reduce(*middle_weight(order, hidden_one, grad_second, where, nblk, (5, 4), [m0.mark]), "both", where)
    i.first([m1.mark])
    far0 = Spread([m0], [i.mark])
    high = lax.Precision.HIGH
    if small:
        hidden_grad, embed_grad, mark = projector_weights(
            pooled_all, number, blk, gap, hp, gz, nblk, [far0.mark]
        )
    else:
        local = lax.dot_general(pooled[:crops], gap, (((0,), (0,)), ((), ())), precision=high)
        hidden_grad = share_sum(local.reshape(nblk, width // nblk, hidden), where)
        local = lax.dot_general(hp, gz, (((0,), (0,)), ((), ())), precision=high)
        embed_grad = share_sum(local.reshape(nblk, hidden // nblk, emb), where)
    m1.first([mark])
    far0.far([m1.mark])
    *grads, mark = input_grads(parts, order, slope, share, grad_first, conv_in, [far0.mark])
    grads = [
        g if p.by_column else jnp.transpose(g.reshape(p.side, p.side, 8, width), (2, 0, 1, 3))
        for g, p in zip(grads, parts)
    ]
    i.second([mark])
    m1.second([i.mark])
    early = Gather([far0], [m1.mark])
    last = Spread([i], [early.mark])
    far1 = Spread([m1], [last.mark])
    taps = m0.keep.shape[0] + m1.keep.shape[0]
    mid_grad, mark = place_taps(early.pieces, where, 0, taps)
    last.far([far1.mark, mark])
    far1.far([last.mark])
    middle = Gather([last, last.extra], [far1.mark])
    late = Gather([far1], [middle.mark])
    conv_in_grad, out_grad = place(middle.pieces, where, 4)
    conv_in_grad = conv_in_grad.reshape(width // nblk, chan)
    mid_grad, _ = place_taps(late.pieces, where, m0.keep.shape[0], taps, mid_grad)
    return (
        *grads,
        conv_in_grad,
        mid_grad.reshape(3, 3, chan // nblk, chan),
        out_grad,
        hidden_grad,
        embed_grad,
        in_back[1],
        in_back[0],
        mid_back[1],
        mid_back[0],
        out_back[1],
        out_back[0],
        gg_proj[0],
        gb_proj[0],
    )


def solution(mesh):
    from_both = ("dp", "blk")
    crop_spec = jax.sharding.PartitionSpec(from_both, None, None, None)
    spec = jax.sharding.PartitionSpec
    in_specs = (crop_spec,) * 3 + (spec(),) * 13 + (spec(from_both, None),)
    out_specs = (crop_spec,) * 3 + (
        spec("blk", None),
        spec(None, None, "blk", None),
        spec("blk", None),
        spec("blk", None),
        spec("blk", None),
    ) + (spec(),) * 8
    return jax.shard_map(body, mesh=mesh, in_specs=in_specs, out_specs=out_specs, check_vma=False)
```

```python
import jax
import jax.numpy as jnp
from jax import lax
from jax.experimental import pallas as pl
from jax.experimental.pallas import tpu as pltpu

F32 = jnp.float32
BF16 = jnp.bfloat16
NORM_EPS = 1e-05
UNIT_EPS = 1e-06
MIB = 1 << 20
ANY = pl.BlockSpec(memory_space=pl.ANY)
HBM = pl.BlockSpec(memory_space=pltpu.HBM)
SMEM = pl.BlockSpec(memory_space=pltpu.SMEM)
MARK = jax.ShapeDtypeStruct((8, 128), F32)


def params(mib):
    return pltpu.CompilerParams(vmem_limit_bytes=mib * MIB)


def cost(flops, moved, special=0):
    return pl.CostEstimate(flops=int(flops), bytes_accessed=int(moved), transcendentals=int(special))


class Part:
    def __init__(self, crops, side, first, slot):
        self.crops, self.side, self.first, self.slot = crops, side, first, slot
        self.by_column = crops != 8
        self.slabs = crops * side if self.by_column else side * side
        self.cut = slice(first, first + self.slabs)

    def sources(self, down, right):
        found = []
        for k in range(self.slabs):
            i, j = divmod(k, self.side)
            if self.by_column:
                i, j = j + down, 0
                there = 0 <= i < self.side
                found.append(k + down if there else None)
            else:
                i, j = i + down, j + right
                there = 0 <= i < self.side and 0 <= j < self.side
                found.append(i * self.side + j if there else None)
        return found


def layout(shapes):
    order = sorted(range(len(shapes)), key=lambda k: (shapes[k][0] != 8, -shapes[k][1]))
    parts = [None] * len(shapes)
    first = slot = 0
    for k in order:
        parts[k] = Part(shapes[k][0], shapes[k][1], first, slot)
        first += parts[k].slabs
        slot += shapes[k][0]
    return parts, [parts[k] for k in order], first


def sigmoid(q):
    return 0.5 * jnp.tanh(0.5 * q) + 0.5


def column_live(shape, side):
    return lax.broadcasted_iota(jnp.int32, shape, len(shape) - 2) < side


def live(parts, value):
    pieces = []
    for p in parts:
        piece = value[p.cut]
        if p.by_column:
            piece = jnp.where(column_live(piece.shape, p.side), piece, 0.0)
        pieces.append(piece)
    return jnp.concatenate(pieces, axis=0)


def crop_totals(parts, value, ref):
    for p in parts:
        piece = value[p.cut]
        if p.by_column:
            piece = piece.reshape(p.crops, p.side, 8, piece.shape[-1])
            total = jnp.sum(jnp.sum(piece, axis=1), axis=1)
        else:
            total = jnp.sum(piece, axis=0)
        ref[p.slot : p.slot + p.crops, :] = total


def spread(parts, ref):
    lanes = ref.shape[-1]
    pieces = []
    for p in parts:
        if p.by_column:
            for c in range(p.crops):
                row = ref[p.slot + c : p.slot + c + 1, :]
                pieces.append(jnp.broadcast_to(row[None], (p.side, 8, lanes)))
        else:
            pieces.append(jnp.broadcast_to(ref[p.slot : p.slot + 8, :][None], (p.slabs, 8, lanes)))
    return jnp.concatenate(pieces, axis=0)


def moments(st_ref, total):
    mean = st_ref[0:1, :] * (1.0 / total)
    var = st_ref[1:2, :] * (1.0 / total) - mean * mean
    return mean, lax.rsqrt(var + NORM_EPS)


def put_sums(ref, first, second):
    ref[0:1, :] = jnp.sum(first, axis=0, keepdims=True)
    ref[1:2, :] = jnp.sum(second, axis=0, keepdims=True)


def split3(x):
    h = x.astype(BF16)
    r = x - h.astype(F32)
    m = r.astype(BF16)
    return h, m, (r - m.astype(F32)).astype(BF16)


def split2(x):
    h = x.astype(BF16)
    return h, (x - h.astype(F32)).astype(BF16)


def mm(a, b):
    return jnp.dot(a, b, preferred_element_type=F32)


def mm_nt(a, b):
    return lax.dot_general(a, b, (((1,), (1,)), ((), ())), preferred_element_type=F32)


def mm_tn(a, b):
    return lax.dot_general(a, b, (((0,), (0,)), ((), ())), preferred_element_type=F32)


def whole(*shape):
    return pl.BlockSpec(shape, lambda *_: (0,) * len(shape))


def mark_of(x):
    return x[(0,) * (x.ndim - 2)][0:8, 0:128]


def lanes_of(block, *lead):
    return pl.BlockSpec((*lead, block), lambda j: (0,) * len(lead) + (j,))


def first_conv(parts, order, slabs, crops, conv_in):
    width, chan = conv_in.shape
    block = 512
    steps = width // block

    def kernel(*refs):
        x_refs, w_ref, xp_ref, a_ref, st_ref, scr = refs[:3], *refs[3:]
        j = pl.program_id(0)
        for p, ref in zip(parts, x_refs):
            x = ref[...].astype(F32)
            if p.by_column:
                x = x.reshape(p.slabs, p.side, block)
                x = jnp.concatenate([x, jnp.zeros((p.slabs, 8 - p.side, block), F32)], axis=1)
            scr[p.cut] = x
        xp_ref[...] = scr[...].reshape(slabs * 8, block).astype(BF16)
        out = mm(xp_ref[...], w_ref[...])

        @pl.when(j == 0)
        def _():
            a_ref[...] = out

        @pl.when(j > 0)
        def _():
            a_ref[...] += out

        @pl.when(j == steps - 1)
        def _():
            total = a_ref[...]
            put_sums(st_ref, total, total * total)

    rows = slabs * 8
    x_specs = [
        pl.BlockSpec((p.crops, p.side, p.side, block), lambda j: (0, 0, 0, j)) if p.by_column else lanes_of(block, p.slabs, 8)
        for p in parts
    ]
    return pl.pallas_call(
        kernel,
        grid=(steps,),
        in_specs=[*x_specs, pl.BlockSpec((block, chan), lambda j: (j, 0))],
        out_specs=[lanes_of(block, rows), whole(rows, chan), whole(2, chan)],
        out_shape=(
            jax.ShapeDtypeStruct((rows, width), BF16),
            jax.ShapeDtypeStruct((rows, chan), F32),
            jax.ShapeDtypeStruct((2, chan), F32),
        ),
        scratch_shapes=[pltpu.VMEM((slabs, 8, block), F32)],
        compiler_params=params(20),
        cost_estimate=cost(2 * rows * width * chan, 10 << 20),
        name="first_conv",
    )(*crops, conv_in)


def turn(order, chan, source, turned):
    for p in order:
        if p.by_column:
            value = source[p.cut].reshape(p.slabs * 8, chan)
            turned[0] = pltpu.roll(value, 1, 0).reshape(p.slabs, 8, chan)
            turned[1] = pltpu.roll(value, p.slabs * 8 - 1, 0).reshape(p.slabs, 8, chan)

def shifted(order, chan, source, turned, tap, forward):
    r, t = divmod(tap, 3)
    down, right = (r - 1, t - 1) if forward else (1 - r, 1 - t)
    pieces = []
    for p in order:
        found = p.sources(down, right)
        k = 0
        while k < p.slabs:
            end = k + 1
            if found[k] is None:
                while end < p.slabs and found[end] is None:
                    end += 1
                pieces.append(jnp.zeros((end - k, 8, chan), F32))
            else:
                while end < p.slabs and found[end] == found[k] + end - k:
                    end += 1
                at = found[k]
                if p.by_column and right:
                    pieces.append(turned[0 if right < 0 else 1, at : at + end - k])
                else:
                    pieces.append(source[p.first + at : p.first + at + end - k])
            k = end
    value = jnp.concatenate(pieces, axis=0)
    return value.reshape(value.shape[0] * 8, chan).astype(BF16)


def patch_columns(order, chan, source, turned, cat_ref, forward):
    turn(order, chan, source, turned)
    for tap in range(9):
        cat_ref[:, tap * chan : (tap + 1) * chan] = shifted(order, chan, source, turned, tap, forward)


def turned_shape(order, chan):
    return (2, max([p.slabs for p in order if p.by_column] + [1]), 8, chan)


def middle_conv(order, first_pre, sums, total, gain, bias, kernel_flat):
    rows, chan = first_pre.shape
    slabs = rows // 8

    def kernel(a_ref, st_ref, g_ref, b_ref, w_ref, y_ref, o_ref, so_ref, turned, cat_scr):
        mean, rstd = moments(st_ref, total)
        scale = g_ref[...] * rstd
        q = (a_ref[...] * scale + (b_ref[...] - mean * scale)).reshape(slabs, 8, chan)
        y_ref[...] = live(order, q * sigmoid(q))
        patch_columns(order, chan, y_ref, turned, cat_scr, True)
        out = live(order, mm(cat_scr[...], w_ref[...]).reshape(slabs, 8, chan)).reshape(rows, chan)
        o_ref[...] = out
        put_sums(so_ref, out, out * out)

    return pl.pallas_call(
        kernel,
        in_specs=[whole(rows, chan), whole(2, chan), whole(1, chan), whole(1, chan), whole(9 * chan, chan)],
        out_specs=[whole(slabs, 8, chan), whole(rows, chan), whole(2, chan)],
        out_shape=(
            jax.ShapeDtypeStruct((slabs, 8, chan), F32),
            jax.ShapeDtypeStruct((rows, chan), F32),
            jax.ShapeDtypeStruct((2, chan), F32),
        ),
        scratch_shapes=[
            pltpu.VMEM(turned_shape(order, chan), F32),
            pltpu.VMEM((rows, 9 * chan), BF16),
        ],
        compiler_params=params(40),
        cost_estimate=cost(18 * rows * chan * chan, 20 << 20),
        name="middle_conv",
    )(first_pre, sums, gain, bias, kernel_flat)


def last_conv(order, second_pre, sums, total, gain, bias, conv_out):
    rows, chan = second_pre.shape
    slabs = rows // 8
    width = conv_out.shape[1]
    block = 512

    def kernel(a_ref, st_ref, g_ref, b_ref, w_ref, y_ref, o_ref, so_ref):
        @pl.when(pl.program_id(0) == 0)
        def _():
            mean, rstd = moments(st_ref, total)
            scale = g_ref[...] * rstd
            q = (a_ref[...] * scale + (b_ref[...] - mean * scale)).reshape(slabs, 8, chan)
            y_ref[...] = live(order, q * sigmoid(q)).reshape(rows, chan).astype(BF16)

        out = mm(y_ref[...], w_ref[...])
        o_ref[...] = out
        put_sums(so_ref, out, out * out)

    return pl.pallas_call(
        kernel,
        grid=(width // block,),
        in_specs=[whole(rows, chan), whole(2, chan), whole(1, chan), whole(1, chan), lanes_of(block, chan)],
        out_specs=[whole(rows, chan), lanes_of(block, rows), lanes_of(block, 2)],
        out_shape=(
            jax.ShapeDtypeStruct((rows, chan), BF16),
            jax.ShapeDtypeStruct((rows, width), F32),
            jax.ShapeDtypeStruct((2, width), F32),
        ),
        compiler_params=params(16),
        cost_estimate=cost(2 * rows * width * chan, 12 << 20),
        name="last_conv",
    )(second_pre, sums, gain, bias, conv_out)


def pool_embed(order, slots, third_pre, sums, total, gain, bias, inputs, hidden_map, pair_row):
    rows, width = third_pre.shape
    slabs = rows // 8
    hidden = hidden_map.shape[1]
    crops = sum(p.crops for p in order)
    block = 512
    steps = width // block

    def kernel(a_ref, st_ref, g_ref, b_ref, x_ref, w_ref, p_ref, e_ref, ap_ref, scr, acc):
        j = pl.program_id(0)
        mean, rstd = moments(st_ref, total)
        scale = g_ref[...] * rstd
        shift = b_ref[...] - mean * scale
        r = x_ref[...].astype(F32) + (a_ref[...] * scale + shift)
        v = live(order, (r * sigmoid(r)).reshape(slabs, 8, block))
        scr[...] = jnp.zeros_like(scr)
        crop_totals(order, v, scr)
        for p in order:
            at = slice(p.slot, p.slot + p.crops)
            scr[at, :] = scr[at, :] * (1.0 / (p.side * p.side))
        e = scr[...]
        e_ref[...] = e[0:slots]
        h, m, l = split3(e)
        out = mm(jnp.concatenate([h, m, l], axis=0), w_ref[...])

        @pl.when(j == 0)
        def _():
            acc[...] = out

        @pl.when(j > 0)
        def _():
            acc[...] += out

        @pl.when(j == steps - 1)
        def _():
            ap_ref[...] = acc[0:slots] + acc[32 : 32 + slots] + acc[64 : 64 + slots]
            ap_ref[crops : crops + 1, :] = p_ref[...]

    return pl.pallas_call(
        kernel,
        grid=(steps,),
        in_specs=[
            lanes_of(block, rows), lanes_of(block, 2), lanes_of(block, 1), lanes_of(block, 1), lanes_of(block, rows),
            pl.BlockSpec((block, hidden), lambda j: (j, 0)), whole(1, hidden),
        ],
        out_specs=[lanes_of(block, slots), whole(slots, hidden)],
        out_shape=(jax.ShapeDtypeStruct((slots, width), F32), jax.ShapeDtypeStruct((slots, hidden), F32)),
        scratch_shapes=[pltpu.VMEM((32, block), F32), pltpu.VMEM((96, hidden), F32)],
        compiler_params=params(20),
        cost_estimate=cost(2 * 96 * width * hidden, 16 << 20, 2 * rows * width),
        name="pool_embed",
    )(third_pre, sums, gain, bias, inputs, hidden_map, pair_row)


def slope_sums(order, slots, third_pre, sums, total, gain, bias, inputs, hold=()):
    rows, width = third_pre.shape
    slabs = rows // 8
    block = 256

    def kernel(a_ref, st_ref, g_ref, b_ref, x_ref, *refs):
        s_ref, p_ref, t_ref = refs[len(hold) :][:3]
        for k in range(len(hold)):
            refs[len(hold) + 3 + k][...] = refs[k][...]
        mean, rstd = moments(st_ref, total)
        p_ref[...] = jnp.zeros_like(p_ref)
        t_ref[...] = jnp.zeros_like(t_ref)
        normed = (a_ref[...] - mean) * rstd
        r = x_ref[...].astype(F32) + (normed * g_ref[...] + b_ref[...])
        sig = sigmoid(r)
        v = live(order, (sig * (1.0 + r * (1.0 - sig))).reshape(slabs, 8, block))
        s_ref[...] = v.reshape(rows, block).astype(BF16)
        crop_totals(order, v, p_ref)
        crop_totals(order, v * normed.reshape(slabs, 8, block), t_ref)

    lane = lambda lead: lanes_of(block, lead)
    kept = [whole(*h.shape) for h in hold]
    return pl.pallas_call(
        kernel,
        grid=(width // block,),
        in_specs=[lane(rows), lane(2), lane(1), lane(1), lane(rows)] + kept,
        out_specs=[lane(rows), lane(slots), lane(slots)] + kept,
        out_shape=(
            jax.ShapeDtypeStruct((rows, width), BF16),
            jax.ShapeDtypeStruct((slots, width), F32),
            jax.ShapeDtypeStruct((slots, width), F32),
            *(jax.ShapeDtypeStruct(h.shape, F32) for h in hold),
        ),
        compiler_params=params(14),
        cost_estimate=cost(24 * rows * width, 8 * rows * width, 2 * rows * width),
        name="slope_sums",
    )(third_pre, sums, gain, bias, inputs, *hold)


def join(pieces, token):
    count = len(pieces)
    shape = pieces[0].shape

    def kernel(*refs):
        for k in range(count):
            refs[-1][k] = refs[k][...]

    return pl.pallas_call(
        kernel,
        in_specs=[whole(*shape)] * count + [whole(8, 128)] * len(token),
        out_specs=whole(count, *shape),
        out_shape=jax.ShapeDtypeStruct((count, *shape), F32),
        compiler_params=params(8),
        name="join",
    )(*pieces, *token)


def projector(order, pres, gain, bias, embed_map, hidden_map, plain, normed_sums, crop_total):
    held = [p.shape[0] for p in pres]
    blocks = sum(held)
    _, slots, hidden = pres[0].shape
    emb = embed_map.shape[1]
    width = hidden_map.shape[0]
    crops = sum(p.crops for p in order)
    rows_all = blocks * slots
    lanes = 256
    cols = hidden // lanes
    inv_total = 1.0 / crop_total
    group = 8
    half = 32

    def kernel(*refs):
        p_refs = refs[: len(held)]
        (g_ref, b_ref, we_ref, wh_ref, s1_ref, s2_ref, hp_ref, gap_ref, gz_ref, gg_ref, gb_ref, ge_ref, st_ref,
         n_scr, d_scr, z_scr, a_scr, i_scr, u_scr) = refs[len(held):]
        live_l = (lax.broadcasted_iota(jnp.int32, (blocks, slots, lanes), 1) < crops).reshape(rows_all, lanes)
        live_e = (lax.broadcasted_iota(jnp.int32, (blocks, slots, emb), 1) < crops).reshape(rows_all, emb)
        rstds = []
        for k in range(cols):
            at = slice(k * lanes, (k + 1) * lanes)
            raw = jnp.concatenate([ref[:, :, at].reshape(n * slots, lanes) for ref, n in zip(p_refs, held)], axis=0)
            raw = jnp.where(live_l, raw, 0.0)
            mean = jnp.sum(raw, axis=0, keepdims=True) * inv_total
            var = jnp.sum(raw * raw, axis=0, keepdims=True) * inv_total - mean * mean
            rstd = lax.rsqrt(var + NORM_EPS)
            rstds.append(rstd)
            normed = (raw - mean) * rstd
            q = normed * g_ref[:, at] + b_ref[:, at]
            sig = sigmoid(q)
            n_scr[:, at] = normed
            d_scr[:, at] = sig * (1.0 + q * (1.0 - sig))
            hp = jnp.where(live_l, q * sig, 0.0)
            hp_ref[:, at] = hp
            h, m = split2(hp)
            z = mm(h, we_ref[at, :]) + mm(m, we_ref[at, :])
            if k == 0:
                z_scr[...] = z
            else:
                z_scr[...] += z
        z = z_scr[...]
        mu = jnp.sum(z, axis=0, keepdims=True) * inv_total
        zc = jnp.where(live_e, z - mu, 0.0)
        zh, zm, zl = split3(zc)
        cat = jnp.concatenate([zh, zm, zl], axis=1)
        prod = mm_tn(cat, cat)
        cov = jnp.zeros((emb, emb), F32)
        for u in (2, 1, 0):
            for v in (2, 1, 0):
                cov = cov + prod[u * emb : (u + 1) * emb, v * emb : (v + 1) * emb]
        row_id = lax.broadcasted_iota(jnp.int32, (emb, emb), 0)
        col_id = lax.broadcasted_iota(jnp.int32, (emb, emb), 1)
        a_scr[...] = cov * inv_total
        i_scr[...] = jnp.where(row_id == col_id, 1.0, 0.0)

        def eliminate(step, carry):
            j = 4 * step
            a = a_scr[...]
            image = i_scr[...]
            at = [jnp.full((emb, emb), j + q, jnp.int32) for q in range(4)]
            lane = lambda row, q: jnp.take_along_axis(jnp.broadcast_to(row, (8, emb)), at[q][0:8], axis=1)[0:1]
            rows = [a_scr[pl.ds(j + p, 1), :] for p in range(4)]
            images = [i_scr[pl.ds(j + p, 1), :] for p in range(4)]
            entry = [[lane(rows[p], q) for q in range(4)] for p in range(4)]
            columns = [jnp.take_along_axis(a, at[q], axis=1) for q in range(4)]
            inverse = []
            for q in range(4):
                inverse.append(1.0 / entry[q][q])
                for p in range(q + 1, 4):
                    ratio = entry[p][q] * inverse[q]
                    rows[p] = rows[p] - ratio * rows[q]
                    images[p] = images[p] - ratio * images[q]
                    for c in range(q + 1, 4):
                        entry[p][c] = entry[p][c] - ratio * entry[q][c]
            for q in range(4):
                column = columns[q]
                for p in range(q):
                    column = column - columns[p] * entry[p][q]
                columns[q] = jnp.where(row_id > j + q, column * inverse[q], 0.0)
                a = a - columns[q] * rows[q]
                image = image - columns[q] * images[q]
            a_scr[...] = a
            i_scr[...] = image
            return carry

        lax.fori_loop(0, emb // 4, eliminate, 0)
        diag = jnp.sum(jnp.where(row_id == col_id, a_scr[...], 0.0), axis=1, keepdims=True)
        white = i_scr[...] * lax.rsqrt(diag)
        ph, pm, pq = split3(white)
        w = mm_nt(
            jnp.concatenate([zh, zh, zm, zh, zl, zm], axis=1),
            jnp.concatenate([ph, pm, ph, pq, ph, pm], axis=1),
        )
        inv_len = lax.rsqrt(jnp.sum(w * w, axis=1, keepdims=True) + UNIT_EPS)
        u = w * inv_len
        uh, um, ul = split3(u)
        ucat = jnp.concatenate([uh, um, ul], axis=1)
        slot_id = lax.broadcasted_iota(jnp.int32, (slots, emb), 0).astype(F32)
        lane_id = lax.broadcasted_iota(jnp.int32, (slots, emb), 1)
        size = group * slots
        own = lax.broadcasted_iota(jnp.int32, (group, slots, size), 0).reshape(size, size)
        other_lane = lax.broadcasted_iota(jnp.int32, (size, size), 1)
        other = jnp.zeros((size, size), jnp.int32)
        for k in range(1, group):
            other = other + jnp.where(other_lane >= k * slots, 1, 0)
        same = own == other
        pair_rows = [ref[b, crops : crops + 1, 0:emb] for ref, n in zip(p_refs, held) for b in range(n)]
        for k in range(blocks // group):
            ends = []
            for b in range(group):
                hit = jnp.where(slot_id == pair_rows[k * group + b], 1.0, 0.0)
                hit = hit - pltpu.roll(hit, emb - half, 1)
                ends.append(jnp.where(lane_id < half, hit, 0.0))
            ends = jnp.concatenate(ends, axis=0).astype(BF16)
            graph = jnp.where(same, mm_nt(ends, ends), 0.0).astype(BF16)
            at = slice(k * size, (k + 1) * size)
            gu = mm(graph, ucat[at])
            u_scr[at, :] = 2.0 * (gu[:, 0:emb] + (gu[:, emb : 2 * emb] + gu[:, 2 * emb : 3 * emb]))
        gu = u_scr[...]
        gw = (gu - u * jnp.sum(u * gu, axis=1, keepdims=True)) * inv_len
        g_col = jnp.sum(gw, axis=0, keepdims=True)
        wh, wm, _ = split3(w)
        gh, gm = split2(gw)
        prod = mm_tn(jnp.concatenate([gh, gm], axis=1), jnp.concatenate([wh, wm], axis=1))
        moment = (
            prod[emb:, emb:] + prod[0:emb, emb:] + prod[emb:, 0:emb] + prod[0:emb, 0:emb]
        )
        low = jnp.where(row_id >= col_id, moment, 0.0)
        strict = jnp.where(row_id > col_id, moment, 0.0)
        sym = (low + strict.T) * inv_total
        sh, sm = split2(sym)
        back = gw - g_col * inv_total - mm(
            jnp.concatenate([wh, wh, wm], axis=1), jnp.concatenate([sh, sm, sh], axis=0)
        )
        bh, bm = split2(back)
        gz = mm(jnp.concatenate([bh, bh, bm], axis=1), jnp.concatenate([ph, pm, ph], axis=0))
        gz = jnp.where(live_e, gz, 0.0)
        gz_ref[...] = gz
        zh2, zm2 = split2(gz)
        zcat = jnp.concatenate([zh2, zm2], axis=0)
        for k in range(cols):
            at = slice(k * lanes, (k + 1) * lanes)
            both = mm_nt(zcat, we_ref[at, :])
            gq = (both[0:rows_all] + both[rows_all:]) * d_scr[:, at]
            gb = jnp.sum(gq, axis=0, keepdims=True)
            gg = jnp.sum(gq * n_scr[:, at], axis=0, keepdims=True)
            gb_ref[:, at] = gb
            gg_ref[:, at] = gg
            gap = (g_ref[:, at] * rstds[k]) * (gq - gb * inv_total - n_scr[:, at] * (gg * inv_total))
            gap_ref[:, at] = jnp.where(live_l, gap, 0.0)
        mine = jnp.concatenate([gap_ref[0:slots, :], jnp.zeros((32 - slots, hidden), F32)], axis=0)
        h, m, l = split3(mine)
        out = mm_nt(jnp.concatenate([h, m, l], axis=0), wh_ref[...])
        ge_ref[...] = out[0:slots] + (out[32 : 32 + slots] + out[64 : 64 + slots])
        for p in order:
            at = slice(p.slot, p.slot + p.crops)
            ge_ref[at, :] = ge_ref[at, :] * (1.0 / (p.side * p.side))
        ge_ref[crops:, :] = jnp.zeros((slots - crops, width), F32)
        ge = ge_ref[...]
        put_sums(st_ref, ge * s1_ref[...], ge * s2_ref[...])

    return pl.pallas_call(
        kernel,
        out_shape=(
            jax.ShapeDtypeStruct((rows_all, hidden), F32),
            jax.ShapeDtypeStruct((rows_all, hidden), F32),
            jax.ShapeDtypeStruct((rows_all, emb), F32),
            jax.ShapeDtypeStruct((1, hidden), F32),
            jax.ShapeDtypeStruct((1, hidden), F32),
            jax.ShapeDtypeStruct((slots, width), F32),
            jax.ShapeDtypeStruct((2, width), F32),
        ),
        scratch_shapes=[
            pltpu.VMEM((rows_all, hidden), F32),
            pltpu.VMEM((rows_all, hidden), F32),
            pltpu.VMEM((rows_all, emb), F32),
            pltpu.VMEM((emb, emb), F32),
            pltpu.VMEM((emb, emb), F32),
            pltpu.VMEM((rows_all, emb), F32),
        ],
        compiler_params=params(30),
        cost_estimate=cost(10 << 30, 20 << 20),
        name="projector",
    )(*pres, gain, bias, embed_map, hidden_map, plain, normed_sums)


def projector_weights(pooled_all, order_of, blk, gap, hp, gz, nblk, token):
    blocks, slots, width = pooled_all.shape
    rows, hidden = gap.shape
    emb = gz.shape[1]
    own, own_hidden = width // nblk, hidden // nblk
    lanes = 256

    def kernel(at_ref, p_ref, ga_ref, hp_ref, gz_ref, *refs):
        o_ref, e_ref, mark, scr, high, low = refs[len(token) :]

        @pl.when(pl.program_id(0) == 0)
        def _():
            mark[...] = jnp.zeros_like(mark)
            for b in range(blocks):
                scr[b * slots : (b + 1) * slots, :] = p_ref[at_ref[1 + b]]
            h, m = split2(scr[...])
            high[...] = h
            low[...] = m
            hh, hm = split2(hp_ref[...])
            gh, gm = split2(gz_ref[...])
            e_ref[...] = mm_tn(hh, gh) + (mm_tn(hh, gm) + mm_tn(hm, gh))

        gh, gm = split2(ga_ref[...])
        o_ref[...] = mm_tn(high[...], gh) + (mm_tn(high[...], gm) + mm_tn(low[...], gh))

    return pl.pallas_call(
        kernel,
        grid_spec=pltpu.PrefetchScalarGridSpec(
            num_scalar_prefetch=1,
            grid=(hidden // lanes,),
            in_specs=[
                pl.BlockSpec((blocks, slots, own), lambda j, at: (0, 0, at[0])),
                pl.BlockSpec((rows, lanes), lambda j, at: (0, j)),
                pl.BlockSpec((rows, own_hidden), lambda j, at: (0, at[0])),
                pl.BlockSpec((rows, emb), lambda j, at: (0, 0)),
            ]
            + [pl.BlockSpec((8, 128), lambda j, at: (0, 0))] * len(token),
            out_specs=[
                pl.BlockSpec((own, lanes), lambda j, at: (0, j)),
                pl.BlockSpec((own_hidden, emb), lambda j, at: (0, 0)),
                pl.BlockSpec((8, 128), lambda j, at: (0, 0)),
            ],
            scratch_shapes=[pltpu.VMEM((rows, own), F32), pltpu.VMEM((rows, own), BF16), pltpu.VMEM((rows, own), BF16)],
        ),
        out_shape=(
            jax.ShapeDtypeStruct((own, hidden), F32),
            jax.ShapeDtypeStruct((own_hidden, emb), F32),
            MARK,
        ),
        compiler_params=params(58),
        cost_estimate=cost(2 << 30, 16 << 20),
        name="projector_weights",
    )(jnp.concatenate([blk[None], order_of]).astype(jnp.int32), pooled_all, gap, hp, gz, *token)


def halves(value, core, send, keep):
    for mine in range(2):

        @pl.when(core == mine)
        def _(mine=mine):
            send[...] = value(1 - mine)
            keep[...] = value(mine)


def last_back(order, slope, share, third_pre, sums, grad_sums, total, gain, conv_out,
              second_pre, mid_sums, mid_gain, mid_bias, hidden_two):
    rows, width = third_pre.shape
    slabs = rows // 8
    chan = second_pre.shape[1]
    block = 512
    steps = width // block

    def kernel(s_ref, e_ref, a_ref, st_ref, gs_ref, g_ref, w_ref, m_ref, ms_ref, mg_ref, mb_ref, y_ref,
               gq_ref, so_ref, weight_ref, ga_scr):
        j = pl.program_id(0)
        mean, rstd = moments(st_ref, total)
        lift = g_ref[...] * rstd
        slant = rstd * gs_ref[1:2, :] * (1.0 / total)
        base = gs_ref[0:1, :] * (1.0 / total) - mean * slant
        gr = s_ref[...].astype(F32) * spread(order, e_ref).reshape(rows, block)
        ga = lift * (gr - base - a_ref[...] * slant)
        ga_scr[...] = live(order, ga.reshape(slabs, 8, block)).reshape(rows, block).astype(BF16)
        out = mm_nt(ga_scr[...], w_ref[...])

        @pl.when(j == 0)
        def _():
            gq_ref[...] = out

        @pl.when(j > 0)
        def _():
            gq_ref[...] += out

        weight_ref[...] = mm_tn(y_ref[...], ga_scr[...])

        @pl.when(j == steps - 1)
        def _():
            mean2, rstd2 = moments(ms_ref, total)
            normed = (m_ref[...] - mean2) * rstd2
            q = normed * mg_ref[...] + mb_ref[...]
            sig = sigmoid(q)
            gq = gq_ref[...] * (sig * (1.0 + q * (1.0 - sig)))
            gq_ref[...] = gq
            put_sums(so_ref, gq, gq * normed)

    return pl.pallas_call(
        kernel,
        grid=(steps,),
        in_specs=[lanes_of(block, rows), lanes_of(block, share.shape[0]), lanes_of(block, rows), lanes_of(block, 2),
                  lanes_of(block, 2), lanes_of(block, 1), lanes_of(block, chan),
                  whole(rows, chan), whole(2, chan), whole(1, chan), whole(1, chan), whole(rows, chan)],
        out_specs=[whole(rows, chan), whole(2, chan), lanes_of(block, chan)],
        out_shape=(
            jax.ShapeDtypeStruct((rows, chan), F32),
            jax.ShapeDtypeStruct((2, chan), F32),
            jax.ShapeDtypeStruct((chan, width), F32),
        ),
        scratch_shapes=[pltpu.VMEM((rows, block), BF16)],
        compiler_params=params(40),
        cost_estimate=cost(4 * rows * width * chan, 24 << 20),
        name="last_back",
    )(slope, share, third_pre, sums, grad_sums, gain, conv_out, second_pre, mid_sums, mid_gain, mid_bias, hidden_two)


def middle_back(order, grad, grad_sums, total, second_pre, mid_sums, mid_gain, kernel_taps,
                first_pre, in_sums, in_gain, in_bias, token):
    rows, chan = grad.shape
    slabs = rows // 8

    def kernel(gq_ref, gs_ref, a_ref, ms_ref, mg_ref, w_ref, f_ref, is_ref, ig_ref, ib_ref, *refs):
        ga_ref, o_ref, so_ref, g_scr, turned, cat_scr, w_scr, sems = refs[len(token):]
        copies = [
            pltpu.make_async_copy(w_ref.at[k], w_scr.at[:, pl.ds(k * chan, chan)], sems.at[k]) for k in range(9)
        ]
        for copy in copies:
            copy.start()
        mean2, rstd2 = moments(ms_ref, total)
        lift = mg_ref[...] * rstd2
        slant = rstd2 * gs_ref[1:2, :] * (1.0 / total)
        base = gs_ref[0:1, :] * (1.0 / total) - mean2 * slant
        ga = live(order, (lift * (gq_ref[...] - base - a_ref[...] * slant)).reshape(slabs, 8, chan))
        g_scr[...] = ga
        ga_ref[...] = ga.reshape(rows, chan).astype(BF16)
        patch_columns(order, chan, g_scr, turned, cat_scr, False)
        for copy in copies:
            copy.wait()
        out = mm_nt(cat_scr[...], w_scr[...])
        mean1, rstd1 = moments(is_ref, total)
        normed = (f_ref[...] - mean1) * rstd1
        q = normed * ig_ref[...] + ib_ref[...]
        sig = sigmoid(q)
        gq = live(order, (out * (sig * (1.0 + q * (1.0 - sig)))).reshape(slabs, 8, chan)).reshape(rows, chan)
        o_ref[...] = gq
        put_sums(so_ref, gq, gq * normed)

    return pl.pallas_call(
        kernel,
        in_specs=[whole(rows, chan), whole(2, chan), whole(rows, chan), whole(2, chan), whole(1, chan), ANY,
                  whole(rows, chan), whole(2, chan), whole(1, chan), whole(1, chan)] + [whole(8, 128)] * len(token),
        out_specs=[whole(rows, chan), whole(rows, chan), whole(2, chan)],
        out_shape=(
            jax.ShapeDtypeStruct((rows, chan), BF16),
            jax.ShapeDtypeStruct((rows, chan), F32),
            jax.ShapeDtypeStruct((2, chan), F32),
        ),
        scratch_shapes=[
            pltpu.VMEM((slabs, 8, chan), F32),
            pltpu.VMEM(turned_shape(order, chan), F32),
            pltpu.VMEM((rows, 9 * chan), BF16),
            pltpu.VMEM((chan, 9 * chan), BF16),
            pltpu.SemaphoreType.DMA((9,)),
        ],
        compiler_params=params(28),
        cost_estimate=cost(18 * rows * chan * chan, 20 << 20),
        name="middle_back",
    )(grad, grad_sums, second_pre, mid_sums, mid_gain, kernel_taps, first_pre, in_sums, in_gain, in_bias, *token)


def middle_weight(order, hidden_one, grad, where, nblk, taps, token, hold=()):
    rows, chan = grad.shape
    slabs = rows // 8
    start, count = taps
    own = chan // nblk

    def kernel(at_ref, y_ref, g_ref, *refs):
        send_ref, keep_ref = refs[len(hold) + len(token) :][:2]
        mark, turned, lhs = refs[-3:]
        mark[...] = jnp.zeros_like(mark)
        k = pl.program_id(0)

        @pl.when(k == 0)
        def _():
            turn(order, chan, y_ref, turned)

        for tap in range(count):

            @pl.when(k == tap)
            def _(tap=tap):
                lhs[...] = shifted(order, chan, y_ref, turned, start + tap, True)

        weight = mm_tn(lhs[...], g_ref[...]).reshape(1, nblk // 2, 2, own, chan)
        halves(lambda c: weight[:, :, c], at_ref[0], send_ref, keep_ref)
        if hold:
            refs[-4][...] = refs[0][...]

    half = pl.BlockSpec((1, nblk // 2, own, chan), lambda k: (k, 0, 0, 0))
    kept = [whole(*h.shape) for h in hold]
    return pl.pallas_call(
        kernel,
        grid=(count,),
        in_specs=[SMEM, whole(slabs, 8, chan), whole(rows, chan)] + kept + [whole(8, 128)] * len(token),
        out_specs=[half, half] + kept + [whole(8, 128)],
        out_shape=(jax.ShapeDtypeStruct((count, nblk // 2, own, chan), F32),) * 2
        + tuple(jax.ShapeDtypeStruct(h.shape, F32) for h in hold)
        + (MARK,),
        scratch_shapes=[pltpu.VMEM(turned_shape(order, chan), F32), pltpu.VMEM((rows, chan), BF16)],
        compiler_params=params(14),
        cost_estimate=cost(2 * rows * chan * chan * count, 12 << 20),
        name="middle_weight",
    )(where, hidden_one, grad, *hold, *token)


def first_back(order, grad, grad_sums, total, first_pre, in_sums, in_gain, inputs, where, nblk, token):
    rows, chan = grad.shape
    slabs = rows // 8
    width = inputs.shape[1]
    own = width // nblk
    each = 2 * own
    merge = max(1, 512 // each)
    units = 4

    def kernel(at_ref, gq_ref, gs_ref, f_ref, is_ref, ig_ref, x_ref, *refs):
        ga_ref, send_ref, keep_ref, mark = refs[len(token):]
        mark[...] = jnp.zeros_like(mark)

        @pl.when(pl.program_id(0) == 0)
        def _():
            mean1, rstd1 = moments(is_ref, total)
            lift = ig_ref[...] * rstd1
            slant = rstd1 * gs_ref[1:2, :] * (1.0 / total)
            base = gs_ref[0:1, :] * (1.0 / total) - mean1 * slant
            ga = lift * (gq_ref[...] - base - f_ref[...] * slant)
            ga_ref[...] = live(order, ga.reshape(slabs, 8, chan)).reshape(rows, chan).astype(BF16)

        weight = mm_tn(x_ref[...], ga_ref[...]).reshape(merge, 2, units, own // units, chan)
        halves(lambda c: jnp.swapaxes(weight[:, c], 0, 1), at_ref[0], send_ref, keep_ref)

    half = pl.BlockSpec((units, merge, own // units, chan), lambda j: (0, j, 0, 0))
    return pl.pallas_call(
        kernel,
        grid=(width // (each * merge),),
        in_specs=[SMEM, whole(rows, chan), whole(2, chan), whole(rows, chan), whole(2, chan), whole(1, chan),
                  lanes_of(each * merge, rows)] + [whole(8, 128)] * len(token),
        out_specs=[whole(rows, chan), half, half, whole(8, 128)],
        out_shape=(
            jax.ShapeDtypeStruct((rows, chan), BF16),
            jax.ShapeDtypeStruct((units, nblk // 2, own // units, chan), F32),
            jax.ShapeDtypeStruct((units, nblk // 2, own // units, chan), F32),
            MARK,
        ),
        compiler_params=params(16),
        cost_estimate=cost(2 * rows * width * chan, 10 << 20),
        name="first_back",
    )(where, grad, grad_sums, first_pre, in_sums, in_gain, inputs, *token)


def input_grads(parts, order, slope, share, grad_first, conv_in, token):
    rows, width = slope.shape
    slabs = rows // 8
    chan = grad_first.shape[1]
    block = 512

    def kernel(s_ref, e_ref, g_ref, w_ref, *refs):
        gr = s_ref[...].astype(F32) * spread(order, e_ref).reshape(rows, block)
        gx = (gr + mm_nt(g_ref[...], w_ref[...])).reshape(slabs, 8, block)
        refs[-1][...] = jnp.zeros((8, 128), F32)
        for p, ref in zip(parts, refs[-4:-1]):
            piece = gx[p.cut]
            if p.by_column:
                ref[...] = piece.reshape(p.crops, p.side, 8, block)[:, :, 0 : p.side, :]
            else:
                ref[...] = piece

    out_specs = []
    out_shape = []
    for p in parts:
        if p.by_column:
            out_specs.append(pl.BlockSpec((p.crops, p.side, p.side, block), lambda j: (0, 0, 0, j)))
            out_shape.append(jax.ShapeDtypeStruct((p.crops, p.side, p.side, width), F32))
        else:
            out_specs.append(lanes_of(block, p.slabs, 8))
            out_shape.append(jax.ShapeDtypeStruct((p.slabs, 8, width), F32))
    return pl.pallas_call(
        kernel,
        grid=(width // block,),
        in_specs=[lanes_of(block, rows), lanes_of(block, share.shape[0]), whole(rows, chan),
                  pl.BlockSpec((block, chan), lambda j: (j, 0))] + [whole(8, 128)] * len(token),
        out_specs=out_specs + [whole(8, 128)],
        out_shape=(*out_shape, MARK),
        compiler_params=params(18),
        cost_estimate=cost(2 * rows * width * chan, 16 << 20),
        name="input_grads",
    )(slope, share, grad_first, conv_in, *token)


def masks_of(size, lowest=1):
    stages = []
    bit = lowest
    while bit < size:
        if 2 * bit < size:
            stages.append([bit, 2 * bit, 3 * bit])
            bit = 4 * bit
        else:
            stages.append([bit])
            bit = 2 * bit
    return stages


def swap(x, axis, mask):
    size = lax.axis_size(axis)
    return lax.ppermute(x, axis, [(i, i ^ mask) for i in range(size)])


def sum_stages(x, axis, stages):
    for masks in stages:
        got = [swap(x, axis, m) for m in masks]
        for g in got:
            x = x + g
    return x


def sum_core(x):
    return sum_stages(x, "blk", [[1]])


def sum_near(x):
    return sum_stages(x, "dp", masks_of(lax.axis_size("dp")))


def sum_far(x):
    return sum_stages(x, "blk", masks_of(lax.axis_size("blk"), 2))


def sum_all(x):
    return sum_far(sum_near(sum_core(x)))


def gather_all(x, between=None):
    dp = lax.axis_index("dp")
    blk = lax.axis_index("blk")
    nblk = lax.axis_size("blk")
    ndp = lax.axis_size("dp")
    joined = x[None]
    where = [0]
    for masks in masks_of(nblk, 2):
        joined = join([joined] + [swap(joined, "blk", m) for m in masks], []).reshape(-1, *x.shape)
        where = where + [w ^ m for m in masks for w in where]
    rows = [joined] + [swap(joined, "dp", k) for k in range(1, ndp)]
    extra = ()
    if between is not None:
        *extra, rows[0] = between(joined)
    rows += [swap(r, "blk", 1) for r in rows]
    number = [
        (dp ^ k) * nblk + (blk ^ (w ^ c)) for c in range(2) for k in range(ndp) for w in where
    ]
    return rows, jnp.stack(number), extra


def fold(kernel, count, where, ins, outs, token, hold, name):
    ins_n, outs_n, hold_n = len(ins), len(outs), len(hold)

    def whole_kernel(at_ref, *refs):
        kernel(at_ref, refs[:ins_n], refs[ins_n + hold_n + len(token) :][:outs_n])
        for k in range(hold_n):
            refs[len(refs) - 1 - hold_n + k][...] = refs[ins_n + k][...]
        refs[-1][...] = jnp.zeros((8, 128), F32)

    def unit(shape):
        if len(shape) == 3:
            return pl.BlockSpec((*shape[:2], shape[2] // count), lambda i: (0, 0, i))
        return pl.BlockSpec((1, *shape[1:]), lambda i: (i,) + (0,) * (len(shape) - 1))

    kept = [whole(*h.shape) for h in hold]
    result = pl.pallas_call(
        whole_kernel,
        grid=(count,),
        in_specs=[SMEM] + [unit(x.shape) for x in ins] + kept + [whole(8, 128)] * len(token),
        out_specs=[unit(x) for x in outs] + kept + [whole(8, 128)],
        out_shape=[jax.ShapeDtypeStruct(x, F32) for x in outs] + [jax.ShapeDtypeStruct(h.shape, F32) for h in hold] + [MARK],
        compiler_params=params(12),
        cost_estimate=cost(0, 8 << 20),
        name=name,
    )(where, *ins, *hold, *token)
    return result[:outs_n], result[outs_n:-1], result[-1]


def fold_first(keep, got, way, where, token, hold, extra=None):
    t, nz, _, r, n = keep.shape
    h = r // 2 if way == "both" else r
    ways = {"x": [0], "y": [1], "both": [0, 1]}[way]
    more = 0 if extra is None else 1

    def kernel(at_ref, ins, outs):
        x = at_ref[1] & 1
        y = at_ref[1] >> 1
        for k, w in enumerate(ways):
            rows = slice(k * h, k * h + h)
            for o in range(2):
                for out, q in (
                    (outs[2 * k], 2 * (1 - y) + o if w else 2 * o + 1 - x),
                    (outs[2 * k + 1], 2 * y + o if w else 2 * o + x),
                ):
                    out[0, 0:nz, o] = ins[0][0, :, q, rows, :] + ins[1][0, :, q, rows, :]
                    if more:
                        out[0, nz, o] = ins[2][q, rows, :]

    ins = [keep, got] + ([extra.reshape(4, r, t * n)] if more else [])
    return fold(kernel, t, where, ins, [(t, nz + more, 2, h, n)] * (2 * len(ways)), token, hold, "fold_first")


def fold_second(sums, way, where, token, hold):
    t, nz, _, h, n = sums[0].shape
    ways = {"x": [0], "y": [1], "both": [0, 1]}[way]

    def kernel(at_ref, ins, outs):
        for k, w in enumerate(ways):
            at = at_ref[1] & 1 if w else at_ref[1] >> 1
            add = lambda q: ins[2 * k][0, :, q] + ins[2 * k + 1][0, :, q]
            outs[2 * k][0] = add(1 - at)
            outs[2 * k + 1][0] = add(at)

    return fold(kernel, t, where, sums, [(t, nz, h, n)] * len(sums), token, hold, "fold_second")


def far_masks(nz):
    if nz == 4:
        return [1, 3]
    return [1 << k for k in range(nz.bit_length() - 1)]


def span(masks):
    offsets = [0]
    for m in masks:
        offsets = offsets + [o ^ m for o in offsets]
    return offsets


def fold_far_first(chains, masks, where, token, more):
    rest = span(masks[1:])
    ins = [x for chain in chains for x in chain]
    full = len(chains[0]) // 2 * chains[0][0].shape[2]
    n = ins[0].shape[-1]
    total = sum(chain[0].shape[0] for chain in chains)

    def kernel(at_ref, *refs):
        outs = refs[len(ins) + len(token) :]
        send, keep, mark = outs[:3]
        mark[...] = jnp.zeros_like(mark)
        first = at = 0
        for chain in chains:
            t, nz, h, _ = chain[0].shape
            for w in range(len(chain) // 2):
                a, b = refs[at : at + 2]
                at += 2
                rows = slice(w * h, w * h + h)
                for k, o in enumerate(rest):
                    send[first : first + t, k, rows, :] = a[:, at_ref[2] ^ o ^ masks[0]] + b[:, at_ref[2] ^ o ^ masks[0]]
                    keep[first : first + t, k, rows, :] = a[:, at_ref[2] ^ o] + b[:, at_ref[2] ^ o]
                if more:
                    outs[3][first : first + t, rows, :] = a[:, nz - 1] + b[:, nz - 1]
            first += t

    shape = (total, len(rest), full, n)
    whole_shape = [(total, full, n)] if more else []
    return pl.pallas_call(
        kernel,
        in_specs=[SMEM] + [whole(*x.shape) for x in ins] + [whole(8, 128)] * len(token),
        out_specs=[whole(*shape)] * 2 + [whole(8, 128)] + [whole(*x) for x in whole_shape],
        out_shape=[jax.ShapeDtypeStruct(shape, F32)] * 2 + [MARK] + [jax.ShapeDtypeStruct(x, F32) for x in whole_shape],
        compiler_params=params(14),
        cost_estimate=cost(0, 8 << 20),
        name="fold_far_first",
    )(where, *ins, *token)


def fold_far(keep, got, step, masks, where, token):
    rest = span(masks[step + 1 :])
    before = span(masks[step:])
    t, _, r, n = keep.shape

    def kernel(at_ref, a, b, *refs):
        send, stay, mark = refs[-3:]
        mark[...] = jnp.zeros_like(mark)
        for k, o in enumerate(rest):
            for out, offset in ((send, o ^ masks[step]), (stay, o)):
                out[:, k] = a[:, before.index(offset)] + b[:, before.index(offset)]

    shape = (t, len(rest), r, n)
    return pl.pallas_call(
        kernel,
        in_specs=[SMEM] + [whole(*keep.shape)] * 2 + [whole(8, 128)] * len(token),
        out_specs=[whole(*shape)] * 2 + [whole(8, 128)],
        out_shape=[jax.ShapeDtypeStruct(shape, F32)] * 2 + [MARK],
        compiler_params=params(12),
        cost_estimate=cost(0, 8 << 20),
        name="fold_far",
    )(where, keep, got, *token)


def place(pieces, where, side=0):
    t, r, n = pieces[0].shape
    count = len(pieces)
    rest = t - side

    def kernel(at_ref, *refs):
        for k in range(count):
            to = at_ref[1] ^ k
            refs[count][:, to] = refs[k][0:rest]
            for u in range(side):
                refs[-1][to, :, u * n : (u + 1) * n] = refs[k][rest + u]

    shapes = [(rest, count, r, n)] + ([(count, r, side * n)] if side else [])
    out = pl.pallas_call(
        kernel,
        in_specs=[SMEM] + [whole(t, r, n)] * count,
        out_specs=[whole(*x) for x in shapes],
        out_shape=[jax.ShapeDtypeStruct(x, F32) for x in shapes],
        compiler_params=params(12),
        name="place",
    )(where, *pieces)
    first = out[0].reshape(rest, count * r, n)
    return (first, out[1].reshape(count * r, side * n)) if side else first


def place_taps(pieces, where, first, taps, before=None):
    t, r, n = pieces[0].shape
    count = len(pieces)

    def kernel(at_ref, *refs):
        for k in range(count):
            refs[-2][0, at_ref[1] ^ k] = refs[k][0]
        refs[-1][...] = jnp.zeros((8, 128), F32)

    kept = [] if before is None else [before]
    return pl.pallas_call(
        kernel,
        grid=(t,),
        in_specs=[SMEM] + [pl.BlockSpec((1, r, n), lambda i: (i, 0, 0))] * count + [ANY] * len(kept),
        out_specs=[pl.BlockSpec((1, count, r, n), lambda i: (i + first, 0, 0, 0)), whole(8, 128)],
        out_shape=[jax.ShapeDtypeStruct((taps, count, r, n), F32), MARK],
        input_output_aliases={1 + count: 0} if kept else {},
        compiler_params=params(8),
        name="place_taps",
    )(where, *pieces, *kept)


def total_of(groups, token):
    total = sum(g[0].shape[0] for g in groups)
    r, n = groups[0][0].shape[-2:]
    ins = [x.reshape(x.shape[0], r, n) for g in groups for x in g]

    def kernel(*refs):
        at = row = 0
        for g in groups:
            t = g[0].shape[0]
            out = refs[at][...]
            for k in range(1, len(g)):
                out = out + refs[at + k][...]
            at += len(g)
            refs[-2][row : row + t] = out
            row += t
        refs[-1][...] = jnp.zeros((8, 128), F32)

    return pl.pallas_call(
        kernel,
        in_specs=[whole(*x.shape) for x in ins] + [whole(8, 128)] * len(token),
        out_specs=[whole(total, r, n), whole(8, 128)],
        out_shape=[jax.ShapeDtypeStruct((total, r, n), F32), MARK],
        compiler_params=params(8),
        cost_estimate=cost(0, 3 << 20),
        name="total_of",
    )(*ins, *token)


class Reduce:
    def __init__(self, send, keep, mark, way, where, extra=None):
        self.where = where
        self.extra = extra
        self.mark = mark
        self.way = way
        t, nz, rows, n = keep.shape
        ndp = lax.axis_size("dp")
        cut = (t, nz, ndp, rows // ndp, n)
        self.keep = keep.reshape(cut)
        self.got = swap(send, "blk", 1).reshape(cut)
        self.masks = far_masks(nz)
        self.first_way = {"x": [1], "y": [2], "both": [1, 2]}[way]

    def near(self, folded, masks):
        outs, kept, self.mark = folded
        self.sums = []
        for k, mask in enumerate(masks):
            self.sums += [outs[2 * k + 1], swap(outs[2 * k], "dp", mask)]
        return kept

    def first(self, token=(), hold=()):
        return self.near(fold_first(self.keep, self.got, self.way, self.where, token, hold, self.extra), self.first_way)

    def second(self, token=(), hold=()):
        return self.near(fold_second(self.sums, self.way, self.where, token, hold), [3 - m for m in self.first_way])


class Spread:
    def __init__(self, chains, token=()):
        self.where = chains[0].where
        self.masks = chains[0].masks
        more = chains[0].extra is not None
        folded = fold_far_first([c.sums for c in chains], self.masks, self.where, token, more)
        self.extra = folded[3] if more else None
        self.next(folded[:3], 0)

    def next(self, folded, step):
        send, keep, self.mark = folded
        self.sums = [keep, swap(send, "blk", 2 * self.masks[step])]

    def far(self, token=()):
        for step in range(1, len(self.masks)):
            self.next(fold_far(*self.sums, step, self.masks, self.where, token), step)


class Gather:
    def __init__(self, parts, token=()):
        self.where = parts[0].where
        out, self.mark = total_of([p.sums if isinstance(p, Spread) else [p] for p in parts], token)
        self.pieces = [out] + [swap(out, "dp", k) for k in range(1, lax.axis_size("dp"))]


def share_sum(local, where):
    nblk, rows, n = local.shape
    local = local.reshape(1, nblk // 2, 2, rows, n)
    pick = lambda c: lax.dynamic_index_in_dim(local, c, 2, keepdims=False)
    whole_sum = Reduce(pick(1 - where[0]), pick(where[0]), None, "x", where)
    whole_sum.first()
    whole_sum.second()
    out = Spread([whole_sum])
    out.far()
    return place(Gather([out]).pieces, where)[0]


def projector_spread(order, pre, gain, bias, embed_map, hidden_map, plain, normed_sums, crop_total):
    slots = pre.shape[0]
    crops = sum(p.crops for p in order)
    high = lax.Precision.HIGHEST
    embed_map = embed_map.astype(F32)
    raw = pre[:crops]
    sums = sum_all(jnp.stack([jnp.sum(raw, axis=0), jnp.sum(raw * raw, axis=0)]))
    mean = sums[0] / crop_total
    rstd = lax.rsqrt(sums[1] / crop_total - mean * mean + NORM_EPS)
    normed = (raw - mean) * rstd
    q = gain * normed + bias
    sig = jax.nn.sigmoid(q)
    hp = q * sig
    z = jnp.dot(hp, embed_map, precision=high)
    emb = z.shape[1]
    z = jnp.concatenate([z, pre[crops : crops + 1, :emb], jnp.zeros((slots - crops - 1, emb), F32)], axis=0)
    z, _, _ = gather_all(z)
    z = jnp.concatenate(z, axis=0)
    blocks = z.shape[0]
    pairs = z[:, crops, :64]
    z = z[:, :crops].reshape(blocks * crops, emb)
    zc = z - jnp.sum(z, axis=0) / crop_total
    cov = jnp.dot(zc.T, zc, precision=high) / crop_total
    white = jax.scipy.linalg.solve_triangular(jnp.linalg.cholesky(cov), jnp.eye(emb, dtype=F32), lower=True)
    w = jnp.dot(zc, white.T, precision=high)
    inv_len = lax.rsqrt(jnp.sum(w * w, axis=1, keepdims=True) + UNIT_EPS)
    u = w * inv_len
    slot = jnp.arange(crops, dtype=F32)
    ends = (pairs[:, :32, None] == slot).astype(F32) - (pairs[:, 32:, None] == slot).astype(F32)
    gap = jnp.einsum("bpc,bce->bpe", ends, u.reshape(blocks, crops, emb), precision=high)
    gu = 2.0 * jnp.einsum("bpc,bpe->bce", ends, gap, precision=high).reshape(blocks * crops, emb)
    gw = (gu - u * jnp.sum(u * gu, axis=1, keepdims=True)) * inv_len
    moment = jnp.dot(gw.T, w, precision=high)
    sym = jnp.tril(moment) + jnp.tril(moment, -1).T
    back = gw[:crops] - (jnp.sum(gw, axis=0) + jnp.dot(w[:crops], sym, precision=high)) / crop_total
    gz = jnp.dot(back, white, precision=high)
    gq = jnp.dot(gz, embed_map.T, precision=high) * (sig * (1.0 + q * (1.0 - sig)))
    sums = sum_all(jnp.stack([jnp.sum(gq, axis=0), jnp.sum(gq * normed, axis=0)]))
    gap = gain * rstd * (gq - sums[0] / crop_total - normed * (sums[1] / crop_total))
    ge = jnp.dot(gap, hidden_map.astype(F32).T, precision=high)
    area = jnp.concatenate([jnp.full((p.crops, 1), 1.0 / (p.side * p.side), F32) for p in order])
    share = jnp.pad(ge * area, ((0, slots - crops), (0, 0)))
    stats = jnp.stack([jnp.sum(share * plain, axis=0), jnp.sum(share * normed_sums, axis=0)])
    return hp, gap, gz, sums[1:2], sums[0:1], share, stats


def body(crops_seven, crops_six, crops_five, conv_in, gain_in, bias_in, conv_mid, gain_mid, bias_mid,
         conv_out, gain_out, bias_out, proj_hidden, gain_proj, bias_proj, proj_embed, pair_index):
    crops_in = (crops_seven, crops_six, crops_five)
    parts, order, slabs = layout([c.shape for c in crops_in])
    ndp = lax.axis_size("dp")
    nblk = lax.axis_size("blk")
    dp = lax.axis_index("dp")
    blk = lax.axis_index("blk")
    devices = ndp * nblk
    crops = sum(p.crops for p in parts)
    total = float(sum(p.crops * p.side * p.side for p in parts) * devices)
    crop_total = float(crops * devices)
    slots = 24
    width, chan = conv_in.shape
    hidden, emb = proj_embed.shape
    row = lambda v: v.reshape(1, -1)
    where = jnp.stack([blk % 2, dp, blk // 2]).astype(jnp.int32)
    first_crop = 0
    pair_slot = pair_index
    for p in parts:
        mine = (pair_index >= first_crop) & (pair_index < first_crop + p.crops)
        pair_slot = jnp.where(mine, pair_index - first_crop + p.slot, pair_slot)
        first_crop += p.crops
    pair_row = jnp.pad(
        jnp.concatenate([pair_slot[:, 0], pair_slot[:, 1]]).astype(F32), (0, hidden - 2 * pair_index.shape[0])
    )
    laid = [
        c if p.by_column else jnp.transpose(c, (1, 2, 0, 3)).reshape(p.slabs, 8, width) for c, p in zip(crops_in, parts)
    ]

    inputs, first_pre, sums = first_conv(parts, order, slabs, laid, conv_in)
    in_sums = sum_all(sums)
    hidden_one, second_pre, sums = middle_conv(
        order, first_pre, in_sums, total, row(gain_in), row(bias_in), conv_mid.reshape(9 * chan, chan)
    )
    mid_sums = sum_all(sums)
    hidden_two, third_pre, sums = last_conv(order, second_pre, mid_sums, total, row(gain_mid), row(bias_mid), conv_out)
    out_sums = sum_all(sums)
    gain_o, bias_o = row(gain_out), row(bias_out)
    pooled, pre = pool_embed(
        order, slots, third_pre, out_sums, total, gain_o, bias_o, inputs, proj_hidden, row(pair_row)
    )
    small = devices <= 32
    slopes = lambda *hold: slope_sums(
        order, slots, third_pre, out_sums, total, gain_o, bias_o, inputs, hold
    )
    if small:
        pre, number, (slope, plain, normed_sums) = gather_all(pre, slopes)
    else:
        slope, plain, normed_sums = slopes()
    middle = projector if small else projector_spread
    hp, gap, gz, gg_proj, gb_proj, share, sums = middle(
        order, pre, row(gain_proj), row(bias_proj), proj_embed, proj_hidden, plain, normed_sums, crop_total
    )
    out_back = sum_all(sums)
    grad_two, sums, local_out = last_back(
        order, slope, share, third_pre, out_sums, out_back, total, gain_o, conv_out,
        second_pre, mid_sums, row(gain_mid), row(bias_mid), hidden_two
    )
    pooled_all = lax.all_gather(pooled, ("dp", "blk"), axis=0) if small else pooled
    out_part = lax.psum_scatter(local_out, "blk", scatter_dimension=0, tiled=True)
    mid_back = sum_all(sums)
    grad_second, grad_one, sums = middle_back(
        order, grad_two, mid_back, total, second_pre, mid_sums, row(gain_mid), conv_mid.reshape(9, chan, chan),
        first_pre, in_sums, row(gain_in), row(bias_in), [mark_of(pooled_all)]
    )
    send, keep, core, mark = middle_weight(
        order, hidden_one, grad_second, where, nblk, (0, 5), [], [sum_core(sums)]
    )
    m0 = Reduce(send, keep, mark, "both", where)
    (near,) = m0.first(hold=[sum_near(core)])
    in_back = sum_stages(near, "blk", [[1 << k] for k in range(1, nblk.bit_length() - 1)])
    grad_first, send, keep, mark = first_back(
        order, grad_one, in_back, total, first_pre, in_sums, row(gain_in), inputs, where, nblk, []
    )
    i = Reduce(send, keep, mark, "both", where, out_part)
    m0.second([mark])
    m1 = Reduce(*middle_weight(order, hidden_one, grad_second, where, nblk, (5, 4), [m0.mark]), "both", where)
    i.first([m1.mark])
    far0 = Spread([m0], [i.mark])
    high = lax.Precision.HIGH
    if small:
        hidden_grad, embed_grad, mark = projector_weights(
            pooled_all, number, blk, gap, hp, gz, nblk, [far0.mark]
        )
    else:
        local = lax.dot_general(pooled[:crops], gap, (((0,), (0,)), ((), ())), precision=high)
        hidden_grad = share_sum(local.reshape(nblk, width // nblk, hidden), where)
        local = lax.dot_general(hp, gz, (((0,), (0,)), ((), ())), precision=high)
        embed_grad = share_sum(local.reshape(nblk, hidden // nblk, emb), where)
    m1.first([mark])
    far0.far([m1.mark])
    *grads, mark = input_grads(parts, order, slope, share, grad_first, conv_in, [far0.mark])
    grads = [
        g if p.by_column else jnp.transpose(g.reshape(p.side, p.side, 8, width), (2, 0, 1, 3))
        for g, p in zip(grads, parts)
    ]
    i.second([mark])
    m1.second([i.mark])
    early = Gather([far0], [m1.mark])
    last = Spread([i], [early.mark])
    far1 = Spread([m1], [last.mark])
    taps = m0.keep.shape[0] + m1.keep.shape[0]
    mid_grad, mark = place_taps(early.pieces, where, 0, taps)
    last.far([far1.mark])
    far1.far([last.mark])
    middle = Gather([last, last.extra], [far1.mark, mark])
    late = Gather([far1], [middle.mark])
    conv_in_grad, out_grad = place(middle.pieces, where, 4)
    conv_in_grad = conv_in_grad.reshape(width // nblk, chan)
    mid_grad, _ = place_taps(late.pieces, where, m0.keep.shape[0], taps, mid_grad)
    return (
        *grads,
        conv_in_grad,
        mid_grad.reshape(3, 3, chan // nblk, chan),
        out_grad,
        hidden_grad,
        embed_grad,
        in_back[1],
        in_back[0],
        mid_back[1],
        mid_back[0],
        out_back[1],
        out_back[0],
        gg_proj[0],
        gb_proj[0],
    )


def solution(mesh):
    from_both = ("dp", "blk")
    crop_spec = jax.sharding.PartitionSpec(from_both, None, None, None)
    spec = jax.sharding.PartitionSpec
    in_specs = (crop_spec,) * 3 + (spec(),) * 13 + (spec(from_both, None),)
    out_specs = (crop_spec,) * 3 + (
        spec("blk", None),
        spec(None, None, "blk", None),
        spec("blk", None),
        spec("blk", None),
        spec("blk", None),
    ) + (spec(),) * 8
    return jax.shard_map(body, mesh=mesh, in_specs=in_specs, out_specs=out_specs, check_vma=False)
```
